32 devices in a mesh: groups: 2 (over y), tm: 16 (over z, x, core), rows: 1.
Axes of the slice: x: 2, y: 2, z: 4, core: 2. Of those that a mesh axis runs over, the one named last changes fastest.
Arguments:
- queries: bfloat16 [32, 4, 64, 1024], P(('groups', 'tm'), 'rows'), parts along dimension 0, may hold values from -60 to 60
- keys: bfloat16 [32, 4, 64, 256], P(('groups', 'tm'), 'rows'), parts along dimension 0, may hold values from -4 to 4
- values: bfloat16 [32, 4, 64, 256], P(('groups', 'tm'), 'rows'), parts along dimension 0, may hold values from -6 to 6
- grad_out: bfloat16 [32, 4, 64, 1024], P(('groups', 'tm'), 'rows'), parts along dimension 0, may hold values from -12 to 12
- frame_mask: int32 [32, 16], P('groups'), parts along dimension 0, may hold values 0 or 1
- clip_frames: int32 [12], P('groups'), parts along dimension 0, may hold values from 1 to 4, 16 in all
- offsets: int32 [24, 2], replicated, may hold values from -3 to 3, as said below
Outputs:
- grad_queries: float32 [32, 4, 64, 1024], P(('groups', 'tm'), 'rows'), parts along dimension 0
- grad_keys: float32 [32, 4, 64, 256], P(('groups', 'tm'), 'rows'), parts along dimension 0
- grad_values: float32 [32, 4, 64, 256], P(('groups', 'tm'), 'rows'), parts along dimension 0
The draws below stay inside these ranges and needn't reach their ends.
There are 2 independent parts, one for each index of `groups`. The reference program is written for one: setup_inputs(seed, part) draws one part's arguments, and reference() takes and returns one part's arrays. A program takes and returns all parts, laid end to end along the dimension named above; an argument that names none is the same for every part. Nothing has to cross between parts.
Inputs may be any that keep to these rules, and one draw needn't show every extreme that they name: `offsets`: row 0 is (0, 0) and row 1 is (0, 1); the rows are distinct cells of the 7 x 7 neighbourhood. `clip_frames`: the lengths sum to 16; the longest clip has exactly 4 frames.
All inputs are finite; a program needn't handle non-finite values.
Results may differ from the reference program's by a relative error of at most 0.005.
Values may be sent and summed in bfloat16 or wider, within the bound.
A program may use at most 128 MiB of HBM per device.

```python
import math
import jax
import jax.numpy as jnp
import numpy as np
from jax import lax

HQ = 8
HK = 2
HD = 128
COLS = 64
NBR = 24
IMG_ROWS = 4
FRAMES = 16
CLIP_MOST = 4
CLIPS = 6


def key_field(key):
    full_shape = (FRAMES, IMG_ROWS, COLS, HK * HD)
    return jnp.clip(jax.random.normal(jax.random.fold_in(key, 11), full_shape, jnp.float32), -4.0, 4.0)


def draw_keys(key, part):
    return key_field(key).astype(jnp.bfloat16)


def draw_queries(key, part):
    full_shape = (FRAMES, IMG_ROWS, COLS, HQ * HD)
    field = jnp.clip(jax.random.normal(jax.random.fold_in(key, 12), full_shape, jnp.float32), -4.0, 4.0)
    return field.astype(jnp.bfloat16)


def draw_offsets(key, part):
    order = jax.random.permutation(jax.random.fold_in(key, 21), 47).astype(jnp.int32)
    chosen = order[:NBR - 2]
    cells = chosen + 2 * (chosen >= 24).astype(jnp.int32)
    others = jnp.stack([cells // 7 - 3, cells % 7 - 3], axis=1)
    fixed_rows = jnp.array([[0, 0], [0, 1]], jnp.int32)
    return jnp.concatenate([fixed_rows, others.astype(jnp.int32)], axis=0)


def plant(entries, own_key, low, high):
    longest = entries.shape.index(max(entries.shape))
    spots = []
    for shift in (0, 1):
        where = [jax.random.randint(jax.random.fold_in(own_key, axis), (), 0, length) for axis, length in enumerate(entries.shape)]
        where[longest] = (where[longest] + shift) % entries.shape[longest]
        spots.append(tuple(where))
    return entries.at[spots[0]].set(low).at[spots[1]].set(high)


def shard_levels(stream_key, dims, split, least, high):
    def one(axis_at, shards_of):
        steps = jax.random.uniform(jax.random.fold_in(jax.random.fold_in(stream_key, 6), axis_at), (shards_of,), jnp.float32, least / len(split), high / len(split))
        return jnp.repeat(jnp.exp(steps), dims[axis_at] // shards_of).reshape((-1,) + (1,) * (len(dims) - axis_at - 1))

    factor_of = one(*split[0])
    for cut in split[1:]:
        factor_of = factor_of * one(*cut)
    return factor_of


def profile(amount, total, most, skew):
    portions = [(1 << 20) // math.isqrt(grade ** skew) + 1 for grade in range(2, amount + 1)]
    rest, given = total - most - (amount - 1), [1] * (amount - 1)
    while rest > 0:
        free = [i for i in range(amount - 1) if given[i] < most]
        mass, remaining = sum([portions[i] for i in free]), rest
        for i in free:
            extra = min(most - given[i], max(1, remaining * portions[i] // mass), rest)
            given[i] = given[i] + extra
            rest = rest - extra
    return np.array([most] + given)


def ragged(own_key, amount, total, bound, slope):
    if amount == 2:
        one = jax.random.randint(own_key, (), max(1, total - bound), min(bound, total - 1) + 1)
        return jnp.stack([one, total - one])
    sizes = jnp.asarray(profile(amount, total, bound, slope), jnp.int32)
    couples = (amount - 1) // 2
    source_of, taker = sizes[1:1 + 2 * couples:2], sizes[2:2 + 2 * couples:2]
    room = jnp.minimum(source_of - 1, bound - taker)
    moved = jax.random.randint(jax.random.fold_in(own_key, 1), (couples,), 0, 1 << 20) % (room + 1)
    sizes = sizes.at[1:1 + 2 * couples:2].set(source_of - moved).at[2:2 + 2 * couples:2].set(taker + moved)
    return sizes[jax.random.permutation(jax.random.fold_in(own_key, 2), amount)]


def normal_values(own_key, shape, width, reach, cuts=(), held_as=jnp.bfloat16):
    level = shard_levels(own_key, shape, cuts, -0.22, 0.18) if cuts else 1.0
    result = jax.random.normal(own_key, shape, jnp.float32) * width * level
    return jnp.minimum(jnp.maximum(result, -reach), reach).astype(held_as)


def setup_inputs(seed: int = 0, part: int = 0) -> dict:
    seeds = jax.random.split(jax.random.key(seed), 8)
    part_keys = jax.random.split(jax.random.fold_in(seeds[7], part), 8)
    return {
        "queries": draw_queries(jax.random.fold_in(jax.random.fold_in(seeds[7], part), 71), part),
        "keys": draw_keys(jax.random.fold_in(jax.random.fold_in(seeds[7], part), 71), part),
        "values": normal_values(part_keys[2], (FRAMES, IMG_ROWS, COLS, HK * HD), 1.0, 6.0, ((0, 16),)),
        "grad_out": normal_values(part_keys[3], (FRAMES, IMG_ROWS, COLS, HQ * HD), 2.0, 12.0, ((0, 16),)),
        "frame_mask": plant((jax.random.randint(part_keys[4], (FRAMES, FRAMES), 0, 4) < 3).astype(jnp.int32), jax.random.fold_in(part_keys[4], 1), 0, 1),
        "clip_frames": ragged(part_keys[5], CLIPS, FRAMES, CLIP_MOST, 2).astype(jnp.int32),
        "offsets": draw_offsets(jax.random.fold_in(seeds[7], 71), part),
    }


negative_big = -1.0e30


def cycle_positions(clip_frames, frame_ids):
    clip_ends = jnp.cumsum(clip_frames).astype(jnp.int32)
    clip_starts = (clip_ends - clip_frames).astype(jnp.int32)
    is_longest = (clip_frames == CLIP_MOST).astype(jnp.int32)
    first_longest = (is_longest == 1) & (jnp.cumsum(is_longest) == 1)
    rotation = jnp.sum(jnp.where(first_longest, clip_starts, 0)).astype(jnp.int32)
    position = ((frame_ids + 2 + rotation) % FRAMES).astype(jnp.int32)
    return position, clip_ends


def allowed_table(frame_mask, clip_frames):
    frame_ids = jnp.arange(FRAMES).astype(jnp.int32)
    position, clip_ends = cycle_positions(clip_frames, frame_ids)
    clip_of = jnp.sum((position[:, None] >= clip_ends[None, :]).astype(jnp.int32), axis=1)
    lag_ids = jnp.arange(CLIP_MOST).astype(jnp.int32)
    seen = ((frame_ids[:, None] - lag_ids[None, :]) % FRAMES).astype(jnp.int32)
    same_clip = clip_of[seen] == clip_of[:, None]
    causal = position[seen] <= position[:, None]
    kept = (lag_ids[None, :] <= 1) | (frame_mask[frame_ids[:, None], seen] == 1)
    return same_clip & causal & kept, seen


def reference(queries, keys, values, grad_out, frame_mask, clip_frames, offsets):
    group_size = HQ // HK
    scale = HD ** -0.5
    allowed, seen = allowed_table(frame_mask, clip_frames)
    pads = ((0, 0), (3, 3), (3, 3), (0, 0))
    key_pad = jnp.pad(keys, pads)
    value_pad = jnp.pad(values, pads)
    inside = jnp.pad(jnp.ones((IMG_ROWS, COLS), jnp.float32), 3) > 0.5
    zero_index = jnp.zeros((), jnp.int32)

    def one_frame(carry, frame):
        key_acc, value_acc = carry
        query_now = queries[frame].astype(jnp.float32).reshape(IMG_ROWS, COLS, HK, group_size, HD)
        grad_now = grad_out[frame].astype(jnp.float32).reshape(IMG_ROWS, COLS, HK, group_size, HD)
        frame_list = seen[frame]
        frame_live = allowed[frame]
        key_win = key_pad[frame_list]
        value_win = value_pad[frame_list]
        score_list = []
        grad_list = []
        live_list = []
        for index in range(NBR):
            row_shift = (3 + offsets[index, 0]).astype(jnp.int32)
            col_shift = (3 + offsets[index, 1]).astype(jnp.int32)
            starts = (zero_index, row_shift, col_shift, zero_index)
            size_four = (CLIP_MOST, IMG_ROWS, COLS, HK * HD)
            shifted_key = lax.dynamic_slice(key_win, starts, size_four).astype(jnp.float32).reshape(CLIP_MOST, IMG_ROWS, COLS, HK, HD)
            shifted_value = lax.dynamic_slice(value_win, starts, size_four).astype(jnp.float32).reshape(CLIP_MOST, IMG_ROWS, COLS, HK, HD)
            spatial = lax.dynamic_slice(inside, (row_shift, col_shift), (IMG_ROWS, COLS))
            live_list.append(spatial[None] & frame_live[:, None, None])
            score_list.append(jnp.einsum('rcgad,lrcgd->lrcga', query_now, shifted_key) * scale)
            grad_list.append(jnp.einsum('rcgad,lrcgd->lrcga', grad_now, shifted_value))
        scores = jnp.stack(score_list)
        grad_dots = jnp.stack(grad_list)
        lives = jnp.stack(live_list)[..., None, None]
        masked = jnp.where(lives, scores, negative_big)
        top_score = jnp.max(masked, axis=(0, 1))
        total = jnp.sum(jnp.where(lives, jnp.exp(scores - top_score), 0.0), axis=(0, 1))
        log_total = top_score + jnp.log(total)
        probs = jnp.where(lives, jnp.exp(scores - log_total), 0.0)
        delta = jnp.sum(probs * grad_dots, axis=(0, 1))
        probs_low = lax.optimization_barrier(probs.astype(jnp.bfloat16))
        dscore = lax.optimization_barrier((probs * (grad_dots - delta)).astype(jnp.bfloat16))
        query_grad = jnp.zeros((IMG_ROWS, COLS, HK, group_size, HD), jnp.float32)
        for index in range(NBR):
            row_shift = (3 + offsets[index, 0]).astype(jnp.int32)
            col_shift = (3 + offsets[index, 1]).astype(jnp.int32)
            starts = (zero_index, row_shift, col_shift, zero_index)
            size_four = (CLIP_MOST, IMG_ROWS, COLS, HK * HD)
            shifted_key = lax.dynamic_slice(key_win, starts, size_four).astype(jnp.float32).reshape(CLIP_MOST, IMG_ROWS, COLS, HK, HD)
            score_part = dscore[index].astype(jnp.float32)
            prob_part = probs_low[index].astype(jnp.float32)
            query_grad = query_grad + jnp.einsum('lrcga,lrcgd->rcgad', score_part, shifted_key)
            key_part = jnp.einsum('lrcga,rcgad->lrcgd', score_part, query_now) * scale
            value_part = jnp.einsum('lrcga,rcgad->lrcgd', prob_part, grad_now)
            for distance in range(CLIP_MOST):
                target = frame_list[distance].astype(jnp.int32)
                place = (target, row_shift, col_shift, zero_index)
                block_size = (1, IMG_ROWS, COLS, HK * HD)
                old_key = lax.dynamic_slice(key_acc, place, block_size)
                key_acc = lax.dynamic_update_slice(key_acc, old_key + key_part[distance].reshape(block_size), place)
                old_value = lax.dynamic_slice(value_acc, place, block_size)
                value_acc = lax.dynamic_update_slice(value_acc, old_value + value_part[distance].reshape(block_size), place)
        query_out = (query_grad * scale).reshape(IMG_ROWS, COLS, HQ * HD)
        return (key_acc, value_acc), query_out

    start_acc = jnp.zeros((FRAMES, IMG_ROWS + 6, COLS + 6, HK * HD), jnp.float32)
    (key_acc, value_acc), query_grads = lax.scan(one_frame, (start_acc, start_acc), jnp.arange(FRAMES).astype(jnp.int32))
    return query_grads, key_acc[:, 3:-3, 3:-3], value_acc[:, 3:-3, 3:-3]
```

```python
import jax
import jax.numpy as jnp
from jax import lax
from jax.experimental import pallas as pl
from jax.experimental.pallas import tpu as pltpu
from jax.sharding import PartitionSpec as P

HQ = 8
HK = 2
HD = 128


tile_cols = 8
key_span = 14
negative_big = -1e30


def padded_2(cells, sides, width):
    for axis, dim in sides:
        count = lax.axis_size(axis)
        ends = count - 1
        head = lax.slice_in_dim(cells, 0, width, axis=dim)
        tail = lax.slice_in_dim(cells, cells.shape[dim] - width, cells.shape[dim], axis=dim)
        cells = jnp.concatenate(
            [
                lax.ppermute(tail, axis, [(i, (i + 1) % count) for i in range(ends)]),
                cells,
                lax.ppermute(head, axis, [((i + 1) % count, i) for i in range(ends)]),
            ],
            axis=dim,
        )
    return cells


def passed_along(value, axis, steps):
    count = lax.axis_size(axis)
    pairs = [(source, (source + steps) % count) for source in range(count)]
    return lax.ppermute(value, axis, pairs)


def to_tiles(block, group_size):
    band_rows = block.shape[0]
    count_tiles = block.shape[1] // tile_cols
    shaped = block.reshape(band_rows, count_tiles, tile_cols, HK, group_size, HD)
    shaped = shaped.transpose(1, 3, 4, 0, 2, 5)
    return shaped.reshape(count_tiles, HK, group_size, band_rows * tile_cols, HD)


def from_tiles(tiles, band_rows):
    count_tiles = tiles.shape[0]
    group_size = tiles.shape[2]
    shaped = tiles.reshape(count_tiles, HK, group_size, band_rows, tile_cols, HD)
    shaped = shaped.transpose(3, 0, 4, 1, 2, 5)
    return shaped.reshape(1, band_rows, count_tiles * tile_cols, HK * group_size * HD)


def to_windows(extended):
    ext_rows = extended.shape[1]
    total_width = extended.shape[2]
    padded = jnp.pad(extended, ((0, 0), (0, 0), (3, 3), (0, 0)))
    pieces = [
        padded[:, :, column_tile * tile_cols : column_tile * tile_cols + key_span]
        for column_tile in range(total_width // tile_cols)
    ]
    stacked = jnp.stack(pieces, 0)
    stacked = stacked.reshape(len(pieces), 2, ext_rows, key_span, HK, HD)
    stacked = stacked.transpose(1, 0, 4, 2, 3, 5)
    return stacked.reshape(2, len(pieces), HK, ext_rows * key_span, HD)


def from_windows(window_grads, ext_rows, total_width):
    count_tiles = window_grads.shape[1]
    shaped = window_grads.reshape(2, count_tiles, HK, ext_rows, key_span, HD)
    shaped = shaped.transpose(0, 1, 3, 4, 2, 5).reshape(2, count_tiles, ext_rows, key_span, HK * HD)
    summed = jnp.zeros((2, ext_rows, total_width + 6, HK * HD), jnp.float32)
    for column_tile in range(count_tiles):
        first_col = column_tile * tile_cols
        summed = summed.at[:, :, first_col : first_col + key_span].add(shaped[:, column_tile])
    return summed[:, :, 3 : 3 + total_width]


def spatial_live(offsets, band_rows, total_width):
    ext_rows = band_rows + 6
    count_tiles = total_width // tile_cols
    query_row = jnp.repeat(jnp.arange(band_rows), tile_cols)
    query_col = jnp.tile(jnp.arange(tile_cols), band_rows)
    key_row = jnp.repeat(jnp.arange(ext_rows), key_span)
    key_col = jnp.tile(jnp.arange(key_span), ext_rows)
    delta_row = key_row[None, :] - 3 - query_row[:, None]
    delta_col = key_col[None, :] - 3 - query_col[:, None]
    offset_hit = jnp.any(
        (delta_row[None] == offsets[:, 0, None, None])
        & (delta_col[None] == offsets[:, 1, None, None]),
        axis=0,
    )
    band_index = lax.axis_index("rows")
    image_rows = band_rows * lax.axis_size("rows")
    image_row = band_index * band_rows + key_row - 3
    row_inside = (image_row >= 0) & (image_row < image_rows)
    tile_first = jnp.arange(count_tiles) * tile_cols
    image_col = tile_first[:, None] + key_col[None, :] - 3
    col_inside = (image_col >= 0) & (image_col < total_width)
    return offset_hit[None] & row_inside[None, None] & col_inside[:, None, :]


def running_sum(entries):
    places = jnp.arange(entries.shape[0])
    return jnp.sum(jnp.where(places[None, :] <= places[:, None], entries[None, :], 0), axis=1)


def frame_allowed(frame_mask, clip_frames, distance):
    frames = lax.axis_size("tm")
    lags = min(4, frames)
    own_frame = lax.axis_index("tm")
    seen_frame = (own_frame - distance) % frames
    clip_ends = running_sum(clip_frames)
    clip_starts = clip_ends - clip_frames
    is_longest = (clip_frames == lags).astype(jnp.int32)
    first_longest = (is_longest == 1) & (running_sum(is_longest) == 1)
    rotation = jnp.sum(jnp.where(first_longest, clip_starts, 0))
    own_place = (own_frame + 2 + rotation) % frames
    seen_place = (seen_frame + 2 + rotation) % frames
    own_clip = jnp.sum((own_place >= clip_ends).astype(jnp.int32))
    seen_clip = jnp.sum((seen_place >= clip_ends).astype(jnp.int32))
    grid_rows = jnp.arange(frames)[:, None]
    grid_cols = jnp.arange(frames)[None, :]
    picked = jnp.sum(jnp.where((grid_rows == own_frame) & (grid_cols == seen_frame), frame_mask, 0))
    kept = (picked == 1) | (distance <= 1)
    return (own_clip == seen_clip) & (seen_place <= own_place) & kept


def fold_rims(extended_grads, band_rows):
    interior = extended_grads[:, 3 : 3 + band_rows]
    rim_rows = jnp.concatenate([extended_grads[:, :3], extended_grads[:, band_rows + 3 :]], 1)
    haloed = padded_2(rim_rows.astype(jnp.bfloat16), (("rows", 1),), 3).astype(rim_rows.dtype)
    interior = interior.at[:, :3].add(haloed[:, :3])
    return interior.at[:, band_rows - 3 :].add(haloed[:, 9:])


def body(queries, keys, values, grad_out, frame_mask, clip_frames, offsets):
    band_rows = queries.shape[1]
    total_width = queries.shape[2]
    ext_rows = band_rows + 6
    group_size = HQ // HK
    scale = HD ** (-0.5)
    lags = min(4, lax.axis_size("tm"))
    query_tiles = to_tiles(queries[0], group_size)
    grad_tiles = to_tiles(grad_out[0], group_size)
    spatial = spatial_live(offsets, band_rows, total_width)[:, None, None]
    allowed = [frame_allowed(frame_mask, clip_frames, distance) for distance in range(lags)]
    stacked = jnp.stack([keys[0], values[0]], 0)
    resident = padded_2(stacked, (("rows", 1),), 3)

    def pair_terms(extended):
        windows = to_windows(extended)
        logits = (
            jnp.einsum(
                "cgaqd,cgkd->cgaqk", query_tiles, windows[0], preferred_element_type=jnp.float32
            )
            * scale
        )
        grad_dot = jnp.einsum(
            "cgaqd,cgkd->cgaqk", grad_tiles, windows[1], preferred_element_type=jnp.float32
        )
        return (windows, logits, grad_dot)

    stat_shape = (total_width // tile_cols, HK, group_size, band_rows * tile_cols)
    running = (
        jnp.full(stat_shape, negative_big, jnp.float32),
        jnp.zeros(stat_shape, jnp.float32),
        jnp.zeros(stat_shape, jnp.float32),
    )
    visiting = resident
    visited = []
    for distance in range(lags):
        visited.append(visiting)
        extended = visiting
        live_mask = spatial & allowed[distance]
        run_max, run_sum, run_dot = running
        stat_windows, stat_logits, stat_grad_dot = pair_terms(extended)
        masked = jnp.where(live_mask, stat_logits, negative_big)
        new_max = jnp.maximum(run_max, jnp.max(masked, axis=-1))
        factor = jnp.exp(run_max - new_max)
        weights = jnp.where(live_mask, jnp.exp(stat_logits - new_max[..., None]), 0.0)
        running = (
            new_max,
            run_sum * factor + jnp.sum(weights, axis=-1),
            run_dot * factor + jnp.sum(weights * stat_grad_dot, axis=-1),
        )
        if distance + 1 < lags:
            visiting = passed_along(visiting, "tm", 1)
    log_total = running[0] + jnp.log(running[1])
    mean_grad = running[2] / running[1]
    query_total = jnp.zeros(stat_shape + (HD,), jnp.float32)
    carried = jnp.zeros(resident.shape, jnp.float32)
    visiting = resident
    for distance in range(lags):
        extended = visiting
        live_mask = spatial & allowed[distance]
        grad_windows, grad_logits, grad_grad_dot = pair_terms(extended)
        probs = jnp.where(live_mask, jnp.exp(grad_logits - log_total[..., None]), 0.0)
        probs_low = probs.astype(jnp.bfloat16)
        dscore = (probs * (grad_grad_dot - mean_grad[..., None])).astype(jnp.bfloat16)
        query_part = jnp.einsum(
            "cgaqk,cgkd->cgaqd", dscore, grad_windows[0], preferred_element_type=jnp.float32
        )
        key_part = (
            jnp.einsum("cgaqk,cgaqd->cgkd", dscore, query_tiles, preferred_element_type=jnp.float32)
            * scale
        )
        value_part = jnp.einsum(
            "cgaqk,cgaqd->cgkd", probs_low, grad_tiles, preferred_element_type=jnp.float32
        )
        query_part, window_grads = (query_part, jnp.stack([key_part, value_part], 0))
        query_total = query_total + query_part
        ext_grads = from_windows(window_grads, ext_rows, total_width)
        carried = carried + ext_grads
        if distance + 1 < lags:
            visiting = passed_along(visiting, "tm", 1)
            carried = passed_along(carried, "tm", 1)
    carried = passed_along(carried, "tm", 1 - lags)
    finished = fold_rims(carried, band_rows)
    grad_queries = from_tiles(query_total * scale, band_rows)
    return (grad_queries, finished[0][None], finished[1][None])


MESH = pl.DeviceIdType.MESH
LOG2E = 1.4426950408889634
SCALE = HD**-0.5
GROUP = HQ // HK


def lag_allowed(mask_ref, clip_ref, own_frame, frames, lag):
    clips = clip_ref.shape[0]
    seen_frame = lax.rem(own_frame - lag + frames, frames)
    total = jnp.int32(0)
    rotation = jnp.int32(0)
    found = jnp.int32(0)
    for clip in range(clips):
        length = clip_ref[clip]
        first = jnp.where(length == 4, 1, 0) * (1 - found)
        rotation = rotation + first * total
        found = found + first
        total = total + length
    own_place = own_frame + 2 + rotation
    own_place = jnp.where(own_place >= frames, own_place - frames, own_place)
    own_place = jnp.where(own_place >= frames, own_place - frames, own_place)
    seen_place = seen_frame + 2 + rotation
    seen_place = jnp.where(seen_place >= frames, seen_place - frames, seen_place)
    seen_place = jnp.where(seen_place >= frames, seen_place - frames, seen_place)
    own_clip = jnp.int32(0)
    seen_clip = jnp.int32(0)
    end = jnp.int32(0)
    for clip in range(clips):
        end = end + clip_ref[clip]
        own_clip = own_clip + jnp.where(own_place >= end, 1, 0)
        seen_clip = seen_clip + jnp.where(seen_place >= end, 1, 0)
    kept = jnp.maximum(jnp.where(mask_ref[own_frame, seen_frame] == 1, 1, 0), jnp.where(lag <= 1, 1, 0))
    same = jnp.where(own_clip == seen_clip, 1, 0)
    causal = jnp.where(seen_place <= own_place, 1, 0)
    return kept * same * causal


TILE = 8
REACH = 4


def fused(
    width, frames,
    mask_hbm, clip_hbm, offset_hbm, query_hbm, key_hbm, value_hbm, cot_hbm,
    dq_out, dk_out, dv_out,
    mask_ref, clip_ref, offset_ref, query_ref, cot_ref, raw, keyed, mixed, bias, held, own_grads, grads, arrived,
    scores_low, dq_acc, final, load_sem, send_sem, recv_sem,
):
    tokens = query_ref.shape[0]
    rows = tokens // width
    tiles = width // TILE
    tile = TILE * rows
    rim = REACH * rows
    span = tile + 2 * rim
    lane_count = GROUP * tile

    def lanes(index):
        return pl.ds(pl.multiple_of(index * HD, HD), HD)

    pairs = [
        (offset_hbm, offset_ref),
        (clip_hbm, clip_ref),
        (mask_hbm, mask_ref),
        (query_hbm, query_ref),
        (cot_hbm, cot_ref),
    ]
    for g in range(HK):
        pairs.append((key_hbm.at[:, lanes(g)], raw.at[0, g, :, pl.ds(0, HD)]))
        pairs.append((value_hbm.at[:, lanes(g)], raw.at[0, g, :, pl.ds(HD, HD)]))
    loads = [pltpu.make_async_copy(pair[0], pair[1], load_sem.at[i]) for i, pair in enumerate(pairs)]
    own = lax.axis_index("tm")
    core = lax.rem(own, 2)

    def device(step):
        return {"tm": lax.rem(own + step + frames, frames)}

    partner = device(1 - 2 * core)
    ahead, behind = device(2), device(frames - 2)
    third = device(jnp.where(core == 0, frames - 3, frames - 1))
    second_to = device(jnp.where(core == 0, 1, 3))
    second_back = device(jnp.where(core == 0, frames - 3, frames - 1))

    barrier = pltpu.get_barrier_semaphore()
    for peer in (partner, behind, third):
        pl.semaphore_signal(barrier, inc=1, device_id=peer, device_id_type=MESH)
    for load in loads:
        load.start()

    def remote(index, source, target, peer):
        return pltpu.make_async_remote_copy(
            src_ref=source, dst_ref=target, send_sem=send_sem.at[index], recv_sem=recv_sem.at[index],
            device_id=peer, device_id_type=MESH,
        )

    def outward(slot, role, g, peer):
        return (
            remote(slot, key_hbm.at[:, lanes(g)], raw.at[role, g, :, pl.ds(0, HD)], peer),
            remote(slot + 1, value_hbm.at[:, lanes(g)], raw.at[role, g, :, pl.ds(HD, HD)], peer),
        )

    send_two = [outward(2 * g, 2, g, ahead) for g in range(HK)]
    send_one = [outward(4 + 2 * g, 1, g, second_to) for g in range(HK)]
    relay = [remote(8 + g, raw.at[2, g], raw.at[3, g], partner) for g in range(HK)]
    inner = pl.ds(rim, tokens)
    back_relay = [remote(10 + g, grads.at[2, g, inner], arrived.at[2, g], partner) for g in range(HK)]
    back_two = [remote(12 + g, grads.at[1, g, inner], arrived.at[1, g], behind) for g in range(HK)]
    back_one = [remote(14 + g, grads.at[0, g, inner], arrived.at[0, g], second_back) for g in range(HK)]

    pl.semaphore_wait(barrier, 3)
    for g in range(HK):
        for copy in send_two[g] + send_one[g]:
            copy.start()

    new_id = lax.broadcasted_iota(jnp.int32, (tokens, tokens), 0)
    old_id = lax.broadcasted_iota(jnp.int32, (tokens, tokens), 1)
    turn = jnp.where((new_id % rows) * width + new_id // rows == old_id, 1.0, 0.0).astype(jnp.bfloat16)

    def permuted(block):
        return jnp.dot(turn, block, preferred_element_type=jnp.float32).astype(jnp.bfloat16)

    for load in loads[:3]:
        load.wait()
    key_id = lax.broadcasted_iota(jnp.int32, (span, lane_count), 0)
    query_id = lax.broadcasted_iota(jnp.int32, (span, lane_count), 1) % tile
    delta_row = key_id % rows - query_id % rows
    delta_col = key_id // rows - REACH - query_id // rows
    code = jnp.where((delta_col >= -3) & (delta_col <= 3), delta_row * 8 + delta_col, 1000)

    def mark(index, hit):
        wanted = offset_ref[0, index] * 8 + offset_ref[1, index]
        return jnp.where(code == wanted, 0.0, hit)

    spatial = lax.fori_loop(
        0, offset_ref.shape[1], mark, jnp.full((span, lane_count), negative_big, jnp.float32), unroll=True
    )
    lags = (jnp.int32(0), jnp.where(core == 0, 3, 1), jnp.int32(2), jnp.where(core == 0, 1, 3))
    for role in range(4):
        allow = lag_allowed(mask_ref, clip_ref, own, frames, lags[role])
        shut = jnp.where(allow == 1, 0.0, negative_big).astype(jnp.float32)
        bias[1, role] = spatial + shut
        bias[0, role] = jnp.where(key_id < rim, negative_big, spatial) + shut
        bias[2, role] = jnp.where(key_id >= span - rim, negative_big, spatial) + shut

    blank = jnp.zeros((rim, 2 * HD), jnp.bfloat16)
    for role in range(4):
        for g in range(HK):
            keyed[g, role, pl.ds(0, rim)] = blank
            keyed[g, role, pl.ds(rim + tokens, rim)] = blank

    for load in loads[3:5]:
        load.wait()
    hole = jnp.zeros((tiles, lane_count, HD), jnp.bfloat16)
    for g in range(HK):
        mixed[g, :, pl.ds(0, lane_count), pl.ds(HD, HD)] = hole
        mixed[g, :, pl.ds(lane_count, lane_count), pl.ds(0, HD)] = hole
        for a in range(GROUP):
            h = g * GROUP + a
            mixed[g, :, pl.ds(a * tile, tile), pl.ds(0, HD)] = permuted(query_ref[:, lanes(h)]).reshape(
                tiles, tile, HD
            )
            mixed[g, :, pl.ds(lane_count + a * tile, tile), pl.ds(HD, HD)] = permuted(
                cot_ref[:, lanes(h)]
            ).reshape(tiles, tile, HD)

    def place(role, g):
        keyed[g, role, pl.ds(rim, tokens)] = permuted(raw[role, g])

    for load in loads[5:]:
        load.wait()
    for g in range(HK):
        place(0, g)

    def unit(g, j):
        first = pl.multiple_of(j * tile, tile)
        window = keyed[g, :, pl.ds(first, span), :].reshape(4 * span, 2 * HD)
        mix = mixed[g, j]
        both = lax.dot_general(window, mix, (((1,), (1,)), ((), ())), preferred_element_type=jnp.float32)
        variant = jnp.where(j == 0, 0, jnp.where(j == tiles - 1, 2, 1))
        logit = both[:, :lane_count] * (SCALE * LOG2E) + bias[variant].reshape(4 * span, lane_count)
        dot = both[:, lane_count:]
        top = jnp.max(logit, axis=0, keepdims=True)
        weight = jnp.exp2(logit - top)
        total = jnp.sum(weight, axis=0, keepdims=True)
        mean = jnp.sum(weight * dot, axis=0, keepdims=True) / total
        prob = weight * (1.0 / total)
        score = (prob * (dot - mean)).astype(jnp.bfloat16)
        scores_low[g, j] = score
        low = jnp.concatenate([score, prob.astype(jnp.bfloat16)], axis=1)
        part = jnp.dot(low, mix, preferred_element_type=jnp.float32).reshape(4, span, 2 * HD)
        begin = part[:, :tile] + held[...]
        held[...] = part[:, tile:]
        own_grads[g, pl.ds(first, tile)] = begin[0]
        grads[:, g, pl.ds(first, tile)] = begin[1:].astype(jnp.bfloat16)

    def queries_unit(g, j):
        first = pl.multiple_of(j * tile, tile)
        window = keyed[g, :, pl.ds(first, span), pl.ds(0, HD)].reshape(4 * span, HD)
        out = jnp.dot(scores_low[g, j].T, window, preferred_element_type=jnp.float32)
        for a in range(GROUP):
            dq_acc[g * GROUP + a, pl.ds(first, tile)] = out[a * tile : (a + 1) * tile]

    for g in range(HK):
        for copy in send_two[g]:
            copy.wait_recv()
        relay[g].start()
        place(2, g)
        for copy in send_one[g]:
            copy.wait_recv()
        place(1, g)
        relay[g].wait_recv()
        place(3, g)
        held[...] = jnp.zeros_like(held)

        def step(j, _, g=g):
            unit(g, j)
            return 0

        lax.fori_loop(0, tiles, step, 0, unroll=UNROLL)
        end = pl.ds(tokens, span - tile)
        own_grads[g, end] = held[0]
        grads[:, g, end] = held[1:].astype(jnp.bfloat16)
        back_relay[g].start()
        back_one[g].start()
        back_relay[g].wait_recv()
        grads[1, g, inner] = (
            grads[1, g, inner].astype(jnp.float32) + arrived[2, g].astype(jnp.float32)
        ).astype(jnp.bfloat16)
        back_two[g].start()

    for g in range(HK):

        def turn_step(j, _, g=g):
            queries_unit(g, j)
            return 0

        lax.fori_loop(0, tiles, turn_step, 0, unroll=UNROLL)

    for h in range(HQ):
        for r in range(rows):
            dq_out[pl.ds(r * width, width), lanes(h)] = dq_acc[h, pl.ds(r, width, stride=rows), :] * SCALE

    for g in range(HK):
        back_one[g].wait_recv()
        back_two[g].wait_recv()
        came = arrived[0, g].astype(jnp.float32) + arrived[1, g].astype(jnp.float32) + own_grads[g, inner]
        final[0, g] = came[:, :HD] * SCALE
        final[1, g] = came[:, HD:]
        for r in range(rows):
            dk_out[pl.ds(r * width, width), lanes(g)] = final[0, g, pl.ds(r, width, stride=rows), :]
            dv_out[pl.ds(r * width, width), lanes(g)] = final[1, g, pl.ds(r, width, stride=rows), :]
    for g in range(HK):
        for copy in send_two[g] + send_one[g] + (relay[g], back_relay[g], back_two[g], back_one[g]):
            copy.wait_send()


UNROLL = 8
VL = 62 * 1024 * 1024


def fused_body(queries, keys, values, grad_out, frame_mask, clip_frames, offsets):
    _, rows, width, wide = queries.shape
    tokens = rows * width
    narrow = keys.shape[3]
    frames = lax.axis_size("tm")
    tiles = width // TILE
    tile = TILE * rows
    padded = tokens + 2 * REACH * rows
    span = tile + 2 * REACH * rows

    def flat(array):
        return array.reshape(tokens, array.shape[3])

    hbm = pl.BlockSpec(memory_space=pltpu.HBM)
    vmem = pl.BlockSpec(memory_space=pltpu.VMEM)

    def kernel(*refs):
        fused(width, frames, *refs)

    dq, dk, dv = pl.pallas_call(
        kernel,
        out_shape=(
            pltpu.VMEM((tokens, wide), jnp.float32),
            pltpu.VMEM((tokens, narrow), jnp.float32),
            pltpu.VMEM((tokens, narrow), jnp.float32),
        ),
        in_specs=[hbm] * 7,
        out_specs=(vmem, vmem, vmem),
        scratch_shapes=[
            pltpu.SMEM(frame_mask.shape, jnp.int32),
            pltpu.SMEM(clip_frames.shape, jnp.int32),
            pltpu.SMEM(offsets.shape[::-1], jnp.int32),
            pltpu.VMEM((tokens, wide), jnp.bfloat16),
            pltpu.VMEM((tokens, wide), jnp.bfloat16),
            pltpu.VMEM((4, HK, tokens, 2 * HD), jnp.bfloat16),
            pltpu.VMEM((HK, 4, padded, 2 * HD), jnp.bfloat16),
            pltpu.VMEM((HK, tiles, 2 * GROUP * tile, 2 * HD), jnp.bfloat16),
            pltpu.VMEM((3, 4, span, GROUP * tile), jnp.float32),
            pltpu.VMEM((4, span - tile, 2 * HD), jnp.float32),
            pltpu.VMEM((HK, padded, 2 * HD), jnp.float32),
            pltpu.VMEM((3, HK, padded, 2 * HD), jnp.bfloat16),
            pltpu.VMEM((3, HK, tokens, 2 * HD), jnp.bfloat16),
            pltpu.VMEM((HK, tiles, 4 * span, GROUP * tile), jnp.bfloat16),
            pltpu.VMEM((HQ, tokens, HD), jnp.float32),
            pltpu.VMEM((2, HK, tokens, HD), jnp.float32),
            pltpu.SemaphoreType.DMA((9,)),
            pltpu.SemaphoreType.DMA((16,)),
            pltpu.SemaphoreType.DMA((16,)),
        ],
        compiler_params=pltpu.CompilerParams(
            collective_id=0, has_side_effects=True, vmem_limit_bytes=VL
        ),
    )(frame_mask, clip_frames, offsets.T, flat(queries), flat(keys), flat(values), flat(grad_out))
    shape = (1, rows, width)
    return dq.reshape(shape + (wide,)), dk.reshape(shape + (narrow,)), dv.reshape(shape + (narrow,))


def solution(mesh):
    whole_rows = mesh.shape["rows"] == 1 and mesh.shape["tm"] % 2 == 0 and mesh.shape["tm"] > 6
    return jax.shard_map(
        fused_body if whole_rows else body,
        mesh=mesh,
        in_specs=(
            P(("groups", "tm"), "rows", None, None),
            P(("groups", "tm"), "rows", None, None),
            P(("groups", "tm"), "rows", None, None),
            P(("groups", "tm"), "rows", None, None),
            P("groups", None),
            P("groups"),
            P(),
        ),
        out_specs=(
            P(("groups", "tm"), "rows", None, None),
            P(("groups", "tm"), "rows", None, None),
            P(("groups", "tm"), "rows", None, None),
        ),
        check_vma=False,
    )
```

```python
import jax
import jax.numpy as jnp
from jax import lax
from jax.experimental import pallas as pl
from jax.experimental.pallas import tpu as pltpu
from jax.sharding import PartitionSpec as P

HQ = 8
HK = 2
HD = 128


tile_cols = 8
key_span = 14
negative_big = -1e30


def padded_2(cells, sides, width):
    for axis, dim in sides:
        count = lax.axis_size(axis)
        ends = count - 1
        head = lax.slice_in_dim(cells, 0, width, axis=dim)
        tail = lax.slice_in_dim(cells, cells.shape[dim] - width, cells.shape[dim], axis=dim)
        cells = jnp.concatenate(
            [
                lax.ppermute(tail, axis, [(i, (i + 1) % count) for i in range(ends)]),
                cells,
                lax.ppermute(head, axis, [((i + 1) % count, i) for i in range(ends)]),
            ],
            axis=dim,
        )
    return cells


def passed_along(value, axis, steps):
    count = lax.axis_size(axis)
    pairs = [(source, (source + steps) % count) for source in range(count)]
    return lax.ppermute(value, axis, pairs)


def to_tiles(block, group_size):
    band_rows = block.shape[0]
    count_tiles = block.shape[1] // tile_cols
    shaped = block.reshape(band_rows, count_tiles, tile_cols, HK, group_size, HD)
    shaped = shaped.transpose(1, 3, 4, 0, 2, 5)
    return shaped.reshape(count_tiles, HK, group_size, band_rows * tile_cols, HD)


def from_tiles(tiles, band_rows):
    count_tiles = tiles.shape[0]
    group_size = tiles.shape[2]
    shaped = tiles.reshape(count_tiles, HK, group_size, band_rows, tile_cols, HD)
    shaped = shaped.transpose(3, 0, 4, 1, 2, 5)
    return shaped.reshape(1, band_rows, count_tiles * tile_cols, HK * group_size * HD)


def to_windows(extended):
    ext_rows = extended.shape[1]
    total_width = extended.shape[2]
    padded = jnp.pad(extended, ((0, 0), (0, 0), (3, 3), (0, 0)))
    pieces = [
        padded[:, :, column_tile * tile_cols : column_tile * tile_cols + key_span]
        for column_tile in range(total_width // tile_cols)
    ]
    stacked = jnp.stack(pieces, 0)
    stacked = stacked.reshape(len(pieces), 2, ext_rows, key_span, HK, HD)
    stacked = stacked.transpose(1, 0, 4, 2, 3, 5)
    return stacked.reshape(2, len(pieces), HK, ext_rows * key_span, HD)


def from_windows(window_grads, ext_rows, total_width):
    count_tiles = window_grads.shape[1]
    shaped = window_grads.reshape(2, count_tiles, HK, ext_rows, key_span, HD)
    shaped = shaped.transpose(0, 1, 3, 4, 2, 5).reshape(2, count_tiles, ext_rows, key_span, HK * HD)
    summed = jnp.zeros((2, ext_rows, total_width + 6, HK * HD), jnp.float32)
    for column_tile in range(count_tiles):
        first_col = column_tile * tile_cols
        summed = summed.at[:, :, first_col : first_col + key_span].add(shaped[:, column_tile])
    return summed[:, :, 3 : 3 + total_width]


def spatial_live(offsets, band_rows, total_width):
    ext_rows = band_rows + 6
    count_tiles = total_width // tile_cols
    query_row = jnp.repeat(jnp.arange(band_rows), tile_cols)
    query_col = jnp.tile(jnp.arange(tile_cols), band_rows)
    key_row = jnp.repeat(jnp.arange(ext_rows), key_span)
    key_col = jnp.tile(jnp.arange(key_span), ext_rows)
    delta_row = key_row[None, :] - 3 - query_row[:, None]
    delta_col = key_col[None, :] - 3 - query_col[:, None]
    offset_hit = jnp.any(
        (delta_row[None] == offsets[:, 0, None, None])
        & (delta_col[None] == offsets[:, 1, None, None]),
        axis=0,
    )
    band_index = lax.axis_index("rows")
    image_rows = band_rows * lax.axis_size("rows")
    image_row = band_index * band_rows + key_row - 3
    row_inside = (image_row >= 0) & (image_row < image_rows)
    tile_first = jnp.arange(count_tiles) * tile_cols
    image_col = tile_first[:, None] + key_col[None, :] - 3
    col_inside = (image_col >= 0) & (image_col < total_width)
    return offset_hit[None] & row_inside[None, None] & col_inside[:, None, :]


def running_sum(entries):
    places = jnp.arange(entries.shape[0])
    return jnp.sum(jnp.where(places[None, :] <= places[:, None], entries[None, :], 0), axis=1)


def frame_allowed(frame_mask, clip_frames, distance):
    frames = lax.axis_size("tm")
    lags = min(4, frames)
    own_frame = lax.axis_index("tm")
    seen_frame = (own_frame - distance) % frames
    clip_ends = running_sum(clip_frames)
    clip_starts = clip_ends - clip_frames
    is_longest = (clip_frames == lags).astype(jnp.int32)
    first_longest = (is_longest == 1) & (running_sum(is_longest) == 1)
    rotation = jnp.sum(jnp.where(first_longest, clip_starts, 0))
    own_place = (own_frame + 2 + rotation) % frames
    seen_place = (seen_frame + 2 + rotation) % frames
    own_clip = jnp.sum((own_place >= clip_ends).astype(jnp.int32))
    seen_clip = jnp.sum((seen_place >= clip_ends).astype(jnp.int32))
    grid_rows = jnp.arange(frames)[:, None]
    grid_cols = jnp.arange(frames)[None, :]
    picked = jnp.sum(jnp.where((grid_rows == own_frame) & (grid_cols == seen_frame), frame_mask, 0))
    kept = (picked == 1) | (distance <= 1)
    return (own_clip == seen_clip) & (seen_place <= own_place) & kept


def fold_rims(extended_grads, band_rows):
    interior = extended_grads[:, 3 : 3 + band_rows]
    rim_rows = jnp.concatenate([extended_grads[:, :3], extended_grads[:, band_rows + 3 :]], 1)
    haloed = padded_2(rim_rows.astype(jnp.bfloat16), (("rows", 1),), 3).astype(rim_rows.dtype)
    interior = interior.at[:, :3].add(haloed[:, :3])
    return interior.at[:, band_rows - 3 :].add(haloed[:, 9:])


def body(queries, keys, values, grad_out, frame_mask, clip_frames, offsets):
    band_rows = queries.shape[1]
    total_width = queries.shape[2]
    ext_rows = band_rows + 6
    group_size = HQ // HK
    scale = HD ** (-0.5)
    lags = min(4, lax.axis_size("tm"))
    query_tiles = to_tiles(queries[0], group_size)
    grad_tiles = to_tiles(grad_out[0], group_size)
    spatial = spatial_live(offsets, band_rows, total_width)[:, None, None]
    allowed = [frame_allowed(frame_mask, clip_frames, distance) for distance in range(lags)]
    stacked = jnp.stack([keys[0], values[0]], 0)
    resident = padded_2(stacked, (("rows", 1),), 3)

    def pair_terms(extended):
        windows = to_windows(extended)
        logits = (
            jnp.einsum(
                "cgaqd,cgkd->cgaqk", query_tiles, windows[0], preferred_element_type=jnp.float32
            )
            * scale
        )
        grad_dot = jnp.einsum(
            "cgaqd,cgkd->cgaqk", grad_tiles, windows[1], preferred_element_type=jnp.float32
        )
        return (windows, logits, grad_dot)

    stat_shape = (total_width // tile_cols, HK, group_size, band_rows * tile_cols)
    running = (
        jnp.full(stat_shape, negative_big, jnp.float32),
        jnp.zeros(stat_shape, jnp.float32),
        jnp.zeros(stat_shape, jnp.float32),
    )
    visiting = resident
    visited = []
    for distance in range(lags):
        visited.append(visiting)
        extended = visiting
        live_mask = spatial & allowed[distance]
        run_max, run_sum, run_dot = running
        stat_windows, stat_logits, stat_grad_dot = pair_terms(extended)
        masked = jnp.where(live_mask, stat_logits, negative_big)
        new_max = jnp.maximum(run_max, jnp.max(masked, axis=-1))
        factor = jnp.exp(run_max - new_max)
        weights = jnp.where(live_mask, jnp.exp(stat_logits - new_max[..., None]), 0.0)
        running = (
            new_max,
            run_sum * factor + jnp.sum(weights, axis=-1),
            run_dot * factor + jnp.sum(weights * stat_grad_dot, axis=-1),
        )
        if distance + 1 < lags:
            visiting = passed_along(visiting, "tm", 1)
    log_total = running[0] + jnp.log(running[1])
    mean_grad = running[2] / running[1]
    query_total = jnp.zeros(stat_shape + (HD,), jnp.float32)
    carried = jnp.zeros(resident.shape, jnp.float32)
    visiting = resident
    for distance in range(lags):
        extended = visiting
        live_mask = spatial & allowed[distance]
        grad_windows, grad_logits, grad_grad_dot = pair_terms(extended)
        probs = jnp.where(live_mask, jnp.exp(grad_logits - log_total[..., None]), 0.0)
        probs_low = probs.astype(jnp.bfloat16)
        dscore = (probs * (grad_grad_dot - mean_grad[..., None])).astype(jnp.bfloat16)
        query_part = jnp.einsum(
            "cgaqk,cgkd->cgaqd", dscore, grad_windows[0], preferred_element_type=jnp.float32
        )
        key_part = (
            jnp.einsum("cgaqk,cgaqd->cgkd", dscore, query_tiles, preferred_element_type=jnp.float32)
            * scale
        )
        value_part = jnp.einsum(
            "cgaqk,cgaqd->cgkd", probs_low, grad_tiles, preferred_element_type=jnp.float32
        )
        query_part, window_grads = (query_part, jnp.stack([key_part, value_part], 0))
        query_total = query_total + query_part
        ext_grads = from_windows(window_grads, ext_rows, total_width)
        carried = carried + ext_grads
        if distance + 1 < lags:
            visiting = passed_along(visiting, "tm", 1)
            carried = passed_along(carried, "tm", 1)
    carried = passed_along(carried, "tm", 1 - lags)
    finished = fold_rims(carried, band_rows)
    grad_queries = from_tiles(query_total * scale, band_rows)
    return (grad_queries, finished[0][None], finished[1][None])


MESH = pl.DeviceIdType.MESH
LOG2E = 1.4426950408889634
SCALE = HD**-0.5
GROUP = HQ // HK


def lag_allowed(mask_ref, clip_ref, own_frame, frames, lag):
    clips = clip_ref.shape[0]
    seen_frame = lax.rem(own_frame - lag + frames, frames)
    total = jnp.int32(0)
    rotation = jnp.int32(0)
    found = jnp.int32(0)
    for clip in range(clips):
        length = clip_ref[clip]
        first = jnp.where(length == 4, 1, 0) * (1 - found)
        rotation = rotation + first * total
        found = found + first
        total = total + length
    own_place = own_frame + 2 + rotation
    own_place = jnp.where(own_place >= frames, own_place - frames, own_place)
    own_place = jnp.where(own_place >= frames, own_place - frames, own_place)
    seen_place = seen_frame + 2 + rotation
    seen_place = jnp.where(seen_place >= frames, seen_place - frames, seen_place)
    seen_place = jnp.where(seen_place >= frames, seen_place - frames, seen_place)
    own_clip = jnp.int32(0)
    seen_clip = jnp.int32(0)
    end = jnp.int32(0)
    for clip in range(clips):
        end = end + clip_ref[clip]
        own_clip = own_clip + jnp.where(own_place >= end, 1, 0)
        seen_clip = seen_clip + jnp.where(seen_place >= end, 1, 0)
    kept = jnp.maximum(jnp.where(mask_ref[own_frame, seen_frame] == 1, 1, 0), jnp.where(lag <= 1, 1, 0))
    same = jnp.where(own_clip == seen_clip, 1, 0)
    causal = jnp.where(seen_place <= own_place, 1, 0)
    return kept * same * causal


TILE = 8
REACH = 4


def fused(
    width, frames,
    mask_hbm, clip_hbm, offset_hbm, query_hbm, key_hbm, value_hbm, cot_hbm,
    dq_out, dkv_out,
    mask_ref, clip_ref, offset_ref, query_ref, cot_ref, raw, keyed, mixed, bias, held, own_grads, grads, arrived,
    scores_low, dq_acc, final, load_sem, send_sem, recv_sem,
):
    tokens = query_ref.shape[0]
    rows = tokens // width
    tiles = width // TILE
    tile = TILE * rows
    rim = REACH * rows
    span = tile + 2 * rim
    lane_count = GROUP * tile

    def lanes(index):
        return pl.ds(pl.multiple_of(index * HD, HD), HD)

    pairs = [
        (offset_hbm, offset_ref),
        (clip_hbm, clip_ref),
        (mask_hbm, mask_ref),
        (query_hbm, query_ref),
        (cot_hbm, cot_ref),
    ]
    for g in range(HK):
        pairs.append((key_hbm.at[:, lanes(g)], raw.at[0, g, :, pl.ds(0, HD)]))
        pairs.append((value_hbm.at[:, lanes(g)], raw.at[0, g, :, pl.ds(HD, HD)]))
    loads = [pltpu.make_async_copy(pair[0], pair[1], load_sem.at[i]) for i, pair in enumerate(pairs)]
    own = lax.axis_index("tm")
    core = lax.rem(own, 2)

    def device(step):
        return {"tm": lax.rem(own + step + frames, frames)}

    partner = device(1 - 2 * core)
    ahead, behind = device(2), device(frames - 2)
    third = device(jnp.where(core == 0, frames - 3, frames - 1))
    second_to = device(jnp.where(core == 0, 1, 3))
    second_back = device(jnp.where(core == 0, frames - 3, frames - 1))

    barrier = pltpu.get_barrier_semaphore()
    for peer in (partner, behind, third):
        pl.semaphore_signal(barrier, inc=1, device_id=peer, device_id_type=MESH)
    for load in loads:
        load.start()

    def remote(index, source, target, peer):
        return pltpu.make_async_remote_copy(
            src_ref=source, dst_ref=target, send_sem=send_sem.at[index], recv_sem=recv_sem.at[index],
            device_id=peer, device_id_type=MESH,
        )

    def outward(slot, role, g, peer):
        return (
            remote(slot, key_hbm.at[:, lanes(g)], raw.at[role, g, :, pl.ds(0, HD)], peer),
            remote(slot + 1, value_hbm.at[:, lanes(g)], raw.at[role, g, :, pl.ds(HD, HD)], peer),
        )

    send_two = [outward(2 * g, 2, g, ahead) for g in range(HK)]
    send_one = [outward(4 + 2 * g, 1, g, second_to) for g in range(HK)]
    relay = [remote(8 + g, raw.at[2, g], raw.at[3, g], partner) for g in range(HK)]
    inner = pl.ds(rim, tokens)
    back_relay = [remote(10 + g, grads.at[2, g, inner], arrived.at[2, g], partner) for g in range(HK)]
    back_two = [remote(12 + g, grads.at[1, g, inner], arrived.at[1, g], behind) for g in range(HK)]
    back_one = [remote(14 + g, grads.at[0, g, inner], arrived.at[0, g], second_back) for g in range(HK)]

    pl.semaphore_wait(barrier, 3)
    for copy in send_two[0] + send_one[0]:
        copy.start()

    new_id = lax.broadcasted_iota(jnp.int32, (tokens, tokens), 0)
    old_id = lax.broadcasted_iota(jnp.int32, (tokens, tokens), 1)
    turn = jnp.where((new_id % rows) * width + new_id // rows == old_id, 1.0, 0.0).astype(jnp.bfloat16)

    def permuted(block):
        return jnp.dot(turn, block, preferred_element_type=jnp.float32).astype(jnp.bfloat16)

    for load in loads[:3]:
        load.wait()
    key_id = lax.broadcasted_iota(jnp.int32, (span, lane_count), 0)
    query_id = lax.broadcasted_iota(jnp.int32, (span, lane_count), 1) % tile
    delta_row = key_id % rows - query_id % rows
    delta_col = key_id // rows - REACH - query_id // rows
    code = jnp.where((delta_col >= -3) & (delta_col <= 3), delta_row * 8 + delta_col, 1000)

    def mark(index, hit):
        wanted = offset_ref[0, index] * 8 + offset_ref[1, index]
        return jnp.where(code == wanted, 0.0, hit)

    spatial = lax.fori_loop(
        0, offset_ref.shape[1], mark, jnp.full((span, lane_count), negative_big, jnp.float32), unroll=True
    )
    lags = (jnp.int32(0), jnp.where(core == 0, 3, 1), jnp.int32(2), jnp.where(core == 0, 1, 3))
    for role in range(4):
        allow = lag_allowed(mask_ref, clip_ref, own, frames, lags[role])
        shut = jnp.where(allow == 1, 0.0, negative_big).astype(jnp.float32)
        bias[1, role] = spatial + shut
        bias[0, role] = jnp.where(key_id < rim, negative_big, spatial) + shut
        bias[2, role] = jnp.where(key_id >= span - rim, negative_big, spatial) + shut

    blank = jnp.zeros((rim, 2 * HD), jnp.bfloat16)
    for role in range(4):
        for g in range(HK):
            keyed[g, role, pl.ds(0, rim)] = blank
            keyed[g, role, pl.ds(rim + tokens, rim)] = blank

    for load in loads[3:5]:
        load.wait()
    hole = jnp.zeros((tiles, lane_count, HD), jnp.bfloat16)
    for g in range(HK):
        mixed[g, :, pl.ds(0, lane_count), pl.ds(HD, HD)] = hole
        mixed[g, :, pl.ds(lane_count, lane_count), pl.ds(0, HD)] = hole
        for a in range(GROUP):
            h = g * GROUP + a
            mixed[g, :, pl.ds(a * tile, tile), pl.ds(0, HD)] = permuted(query_ref[:, lanes(h)]).reshape(
                tiles, tile, HD
            )
            mixed[g, :, pl.ds(lane_count + a * tile, tile), pl.ds(HD, HD)] = permuted(
                cot_ref[:, lanes(h)]
            ).reshape(tiles, tile, HD)

    def follow(first, then):
        for copy in first:
            copy.wait_send()
        for copy in then:
            copy.start()

    def place(role, g):
        keyed[g, role, pl.ds(rim, tokens)] = permuted(raw[role, g])

    for load in loads[5:]:
        load.wait()
    for g in range(HK):
        place(0, g)

    def unit(g, j):
        first = pl.multiple_of(j * tile, tile)
        window = keyed[g, :, pl.ds(first, span), :].reshape(4 * span, 2 * HD)
        mix = mixed[g, j]
        both = lax.dot_general(window, mix, (((1,), (1,)), ((), ())), preferred_element_type=jnp.float32)
        variant = jnp.where(j == 0, 0, jnp.where(j == tiles - 1, 2, 1))
        logit = both[:, :lane_count] * (SCALE * LOG2E) + bias[variant].reshape(4 * span, lane_count)
        dot = both[:, lane_count:]
        top = jnp.max(logit, axis=0, keepdims=True)
        weight = jnp.exp2(logit - top)
        total = jnp.sum(weight, axis=0, keepdims=True)
        mean = jnp.sum(weight * dot, axis=0, keepdims=True) / total
        prob = weight * (1.0 / total)
        score = (prob * (dot - mean)).astype(jnp.bfloat16)
        scores_low[g, j] = score
        low = jnp.concatenate([score, prob.astype(jnp.bfloat16)], axis=1)
        part = jnp.dot(low, mix, preferred_element_type=jnp.float32).reshape(4, span, 2 * HD)
        begin = part[:, :tile] + held[...]
        held[...] = part[:, tile:]
        own_grads[g, pl.ds(first, tile)] = begin[0]
        grads[:, g, pl.ds(first, tile)] = begin[1:].astype(jnp.bfloat16)

    def queries_unit(g, j):
        first = pl.multiple_of(j * tile, tile)
        window = keyed[g, :, pl.ds(first, span), pl.ds(0, HD)].reshape(4 * span, HD)
        out = jnp.dot(scores_low[g, j].T, window, preferred_element_type=jnp.float32)
        for a in range(GROUP):
            dq_acc[g * GROUP + a, pl.ds(first, tile)] = out[a * tile : (a + 1) * tile]

    def receive(g):
        for copy in send_two[g]:
            copy.wait_recv()
        relay[g].start()
        place(2, g)
        for copy in send_one[g]:
            copy.wait_recv()
        place(1, g)
        relay[g].wait_recv()
        place(3, g)


    def work(g):
        held[...] = jnp.zeros_like(held)

        def step(j, _):
            unit(g, j)
            return 0

        lax.fori_loop(0, tiles, step, 0, unroll=UNROLL)
        end = pl.ds(tokens, span - tile)
        own_grads[g, end] = held[0]
        grads[:, g, end] = held[1:].astype(jnp.bfloat16)
        back_relay[g].start()
        back_one[g].start()

    def pass_two(g):
        back_relay[g].wait_recv()
        grads[1, g, inner] = (
            grads[1, g, inner].astype(jnp.float32) + arrived[2, g].astype(jnp.float32)
        ).astype(jnp.bfloat16)
        back_two[g].start()

    follow(send_two[0] + send_one[0], send_two[1] + send_one[1])
    receive(0)
    work(0)
    pass_two(0)
    receive(1)
    work(1)
    pass_two(1)

    for g in range(HK):

        def turn_step(j, _, g=g):
            queries_unit(g, j)
            return 0

        lax.fori_loop(0, tiles, turn_step, 0, unroll=UNROLL)

    for h in range(HQ):
        for r in range(rows):
            dq_out[pl.ds(r * width, width), lanes(h)] = dq_acc[h, pl.ds(r, width, stride=rows), :] * SCALE

    for g in range(HK):
        back_one[g].wait_recv()
        back_two[g].wait_recv()
        came = arrived[0, g].astype(jnp.float32) + arrived[1, g].astype(jnp.float32) + own_grads[g, inner]
        final[0, g] = came[:, :HD] * SCALE
        final[1, g] = came[:, HD:]
        for r in range(rows):
            dkv_out[0, pl.ds(r * width, width), lanes(g)] = final[0, g, pl.ds(r, width, stride=rows), :]
            dkv_out[1, pl.ds(r * width, width), lanes(g)] = final[1, g, pl.ds(r, width, stride=rows), :]
    for copy in send_two[1] + send_one[1]:
        copy.wait_send()
    for g in range(HK):
        for copy in (relay[g], back_relay[g], back_two[g], back_one[g]):
            copy.wait_send()


UNROLL = 8
VL = 62 * 1024 * 1024


def fused_body(queries, keys, values, grad_out, frame_mask, clip_frames, offsets):
    _, rows, width, wide = queries.shape
    tokens = rows * width
    narrow = keys.shape[3]
    frames = lax.axis_size("tm")
    tiles = width // TILE
    tile = TILE * rows
    padded = tokens + 2 * REACH * rows
    span = tile + 2 * REACH * rows

    def flat(array):
        return array.reshape(tokens, array.shape[3])

    hbm = pl.BlockSpec(memory_space=pltpu.HBM)
    vmem = pl.BlockSpec(memory_space=pltpu.VMEM)

    def kernel(*refs):
        fused(width, frames, *refs)

    dq, dkv = pl.pallas_call(
        kernel,
        out_shape=(
            pltpu.VMEM((tokens, wide), jnp.float32),
            pltpu.VMEM((2, tokens, narrow), jnp.float32),
        ),
        in_specs=[hbm] * 7,
        out_specs=(vmem, vmem),
        scratch_shapes=[
            pltpu.SMEM(frame_mask.shape, jnp.int32),
            pltpu.SMEM(clip_frames.shape, jnp.int32),
            pltpu.SMEM(offsets.shape[::-1], jnp.int32),
            pltpu.VMEM((tokens, wide), jnp.bfloat16),
            pltpu.VMEM((tokens, wide), jnp.bfloat16),
            pltpu.VMEM((4, HK, tokens, 2 * HD), jnp.bfloat16),
            pltpu.VMEM((HK, 4, padded, 2 * HD), jnp.bfloat16),
            pltpu.VMEM((HK, tiles, 2 * GROUP * tile, 2 * HD), jnp.bfloat16),
            pltpu.VMEM((3, 4, span, GROUP * tile), jnp.float32),
            pltpu.VMEM((4, span - tile, 2 * HD), jnp.float32),
            pltpu.VMEM((HK, padded, 2 * HD), jnp.float32),
            pltpu.VMEM((3, HK, padded, 2 * HD), jnp.bfloat16),
            pltpu.VMEM((3, HK, tokens, 2 * HD), jnp.bfloat16),
            pltpu.VMEM((HK, tiles, 4 * span, GROUP * tile), jnp.bfloat16),
            pltpu.VMEM((HQ, tokens, HD), jnp.float32),
            pltpu.VMEM((2, HK, tokens, HD), jnp.float32),
            pltpu.SemaphoreType.DMA((9,)),
            pltpu.SemaphoreType.DMA((16,)),
            pltpu.SemaphoreType.DMA((16,)),
        ],
        compiler_params=pltpu.CompilerParams(
            collective_id=0, has_side_effects=True, vmem_limit_bytes=VL
        ),
    )(frame_mask, clip_frames, offsets.T, flat(queries), flat(keys), flat(values), flat(grad_out))
    shape = (1, rows, width)
    return dq.reshape(shape + (wide,)), dkv[0].reshape(shape + (narrow,)), dkv[1].reshape(shape + (narrow,))


def solution(mesh):
    whole_rows = mesh.shape["rows"] == 1 and mesh.shape["tm"] % 2 == 0 and mesh.shape["tm"] > 6
    return jax.shard_map(
        fused_body if whole_rows else body,
        mesh=mesh,
        in_specs=(
            P(("groups", "tm"), "rows", None, None),
            P(("groups", "tm"), "rows", None, None),
            P(("groups", "tm"), "rows", None, None),
            P(("groups", "tm"), "rows", None, None),
            P("groups", None),
            P("groups"),
            P(),
        ),
        out_specs=(
            P(("groups", "tm"), "rows", None, None),
            P(("groups", "tm"), "rows", None, None),
            P(("groups", "tm"), "rows", None, None),
        ),
        check_vma=False,
    )
```

```python
import jax
import jax.numpy as jnp
from jax import lax
from jax.experimental import pallas as pl
from jax.experimental.pallas import tpu as pltpu
from jax.sharding import PartitionSpec as P

HQ = 8
HK = 2
HD = 128


tile_cols = 8
key_span = 14
negative_big = -1e30


def padded_2(cells, sides, width):
    for axis, dim in sides:
        count = lax.axis_size(axis)
        ends = count - 1
        head = lax.slice_in_dim(cells, 0, width, axis=dim)
        tail = lax.slice_in_dim(cells, cells.shape[dim] - width, cells.shape[dim], axis=dim)
        cells = jnp.concatenate(
            [
                lax.ppermute(tail, axis, [(i, (i + 1) % count) for i in range(ends)]),
                cells,
                lax.ppermute(head, axis, [((i + 1) % count, i) for i in range(ends)]),
            ],
            axis=dim,
        )
    return cells


def passed_along(value, axis, steps):
    count = lax.axis_size(axis)
    pairs = [(source, (source + steps) % count) for source in range(count)]
    return lax.ppermute(value, axis, pairs)


def to_tiles(block, group_size):
    band_rows = block.shape[0]
    count_tiles = block.shape[1] // tile_cols
    shaped = block.reshape(band_rows, count_tiles, tile_cols, HK, group_size, HD)
    shaped = shaped.transpose(1, 3, 4, 0, 2, 5)
    return shaped.reshape(count_tiles, HK, group_size, band_rows * tile_cols, HD)


def from_tiles(tiles, band_rows):
    count_tiles = tiles.shape[0]
    group_size = tiles.shape[2]
    shaped = tiles.reshape(count_tiles, HK, group_size, band_rows, tile_cols, HD)
    shaped = shaped.transpose(3, 0, 4, 1, 2, 5)
    return shaped.reshape(1, band_rows, count_tiles * tile_cols, HK * group_size * HD)


def to_windows(extended):
    ext_rows = extended.shape[1]
    total_width = extended.shape[2]
    padded = jnp.pad(extended, ((0, 0), (0, 0), (3, 3), (0, 0)))
    pieces = [
        padded[:, :, column_tile * tile_cols : column_tile * tile_cols + key_span]
        for column_tile in range(total_width // tile_cols)
    ]
    stacked = jnp.stack(pieces, 0)
    stacked = stacked.reshape(len(pieces), 2, ext_rows, key_span, HK, HD)
    stacked = stacked.transpose(1, 0, 4, 2, 3, 5)
    return stacked.reshape(2, len(pieces), HK, ext_rows * key_span, HD)


def from_windows(window_grads, ext_rows, total_width):
    count_tiles = window_grads.shape[1]
    shaped = window_grads.reshape(2, count_tiles, HK, ext_rows, key_span, HD)
    shaped = shaped.transpose(0, 1, 3, 4, 2, 5).reshape(2, count_tiles, ext_rows, key_span, HK * HD)
    summed = jnp.zeros((2, ext_rows, total_width + 6, HK * HD), jnp.float32)
    for column_tile in range(count_tiles):
        first_col = column_tile * tile_cols
        summed = summed.at[:, :, first_col : first_col + key_span].add(shaped[:, column_tile])
    return summed[:, :, 3 : 3 + total_width]


def spatial_live(offsets, band_rows, total_width):
    ext_rows = band_rows + 6
    count_tiles = total_width // tile_cols
    query_row = jnp.repeat(jnp.arange(band_rows), tile_cols)
    query_col = jnp.tile(jnp.arange(tile_cols), band_rows)
    key_row = jnp.repeat(jnp.arange(ext_rows), key_span)
    key_col = jnp.tile(jnp.arange(key_span), ext_rows)
    delta_row = key_row[None, :] - 3 - query_row[:, None]
    delta_col = key_col[None, :] - 3 - query_col[:, None]
    offset_hit = jnp.any(
        (delta_row[None] == offsets[:, 0, None, None])
        & (delta_col[None] == offsets[:, 1, None, None]),
        axis=0,
    )
    band_index = lax.axis_index("rows")
    image_rows = band_rows * lax.axis_size("rows")
    image_row = band_index * band_rows + key_row - 3
    row_inside = (image_row >= 0) & (image_row < image_rows)
    tile_first = jnp.arange(count_tiles) * tile_cols
    image_col = tile_first[:, None] + key_col[None, :] - 3
    col_inside = (image_col >= 0) & (image_col < total_width)
    return offset_hit[None] & row_inside[None, None] & col_inside[:, None, :]


def running_sum(entries):
    places = jnp.arange(entries.shape[0])
    return jnp.sum(jnp.where(places[None, :] <= places[:, None], entries[None, :], 0), axis=1)


def frame_allowed(frame_mask, clip_frames, distance):
    frames = lax.axis_size("tm")
    lags = min(4, frames)
    own_frame = lax.axis_index("tm")
    seen_frame = (own_frame - distance) % frames
    clip_ends = running_sum(clip_frames)
    clip_starts = clip_ends - clip_frames
    is_longest = (clip_frames == lags).astype(jnp.int32)
    first_longest = (is_longest == 1) & (running_sum(is_longest) == 1)
    rotation = jnp.sum(jnp.where(first_longest, clip_starts, 0))
    own_place = (own_frame + 2 + rotation) % frames
    seen_place = (seen_frame + 2 + rotation) % frames
    own_clip = jnp.sum((own_place >= clip_ends).astype(jnp.int32))
    seen_clip = jnp.sum((seen_place >= clip_ends).astype(jnp.int32))
    grid_rows = jnp.arange(frames)[:, None]
    grid_cols = jnp.arange(frames)[None, :]
    picked = jnp.sum(jnp.where((grid_rows == own_frame) & (grid_cols == seen_frame), frame_mask, 0))
    kept = (picked == 1) | (distance <= 1)
    return (own_clip == seen_clip) & (seen_place <= own_place) & kept


def fold_rims(extended_grads, band_rows):
    interior = extended_grads[:, 3 : 3 + band_rows]
    rim_rows = jnp.concatenate([extended_grads[:, :3], extended_grads[:, band_rows + 3 :]], 1)
    haloed = padded_2(rim_rows.astype(jnp.bfloat16), (("rows", 1),), 3).astype(rim_rows.dtype)
    interior = interior.at[:, :3].add(haloed[:, :3])
    return interior.at[:, band_rows - 3 :].add(haloed[:, 9:])


def body(queries, keys, values, grad_out, frame_mask, clip_frames, offsets):
    band_rows = queries.shape[1]
    total_width = queries.shape[2]
    ext_rows = band_rows + 6
    group_size = HQ // HK
    scale = HD ** (-0.5)
    lags = min(4, lax.axis_size("tm"))
    query_tiles = to_tiles(queries[0], group_size)
    grad_tiles = to_tiles(grad_out[0], group_size)
    spatial = spatial_live(offsets, band_rows, total_width)[:, None, None]
    allowed = [frame_allowed(frame_mask, clip_frames, distance) for distance in range(lags)]
    stacked = jnp.stack([keys[0], values[0]], 0)
    resident = padded_2(stacked, (("rows", 1),), 3)

    def pair_terms(extended):
        windows = to_windows(extended)
        logits = (
            jnp.einsum(
                "cgaqd,cgkd->cgaqk", query_tiles, windows[0], preferred_element_type=jnp.float32
            )
            * scale
        )
        grad_dot = jnp.einsum(
            "cgaqd,cgkd->cgaqk", grad_tiles, windows[1], preferred_element_type=jnp.float32
        )
        return (windows, logits, grad_dot)

    stat_shape = (total_width // tile_cols, HK, group_size, band_rows * tile_cols)
    running = (
        jnp.full(stat_shape, negative_big, jnp.float32),
        jnp.zeros(stat_shape, jnp.float32),
        jnp.zeros(stat_shape, jnp.float32),
    )
    visiting = resident
    visited = []
    for distance in range(lags):
        visited.append(visiting)
        extended = visiting
        live_mask = spatial & allowed[distance]
        run_max, run_sum, run_dot = running
        stat_windows, stat_logits, stat_grad_dot = pair_terms(extended)
        masked = jnp.where(live_mask, stat_logits, negative_big)
        new_max = jnp.maximum(run_max, jnp.max(masked, axis=-1))
        factor = jnp.exp(run_max - new_max)
        weights = jnp.where(live_mask, jnp.exp(stat_logits - new_max[..., None]), 0.0)
        running = (
            new_max,
            run_sum * factor + jnp.sum(weights, axis=-1),
            run_dot * factor + jnp.sum(weights * stat_grad_dot, axis=-1),
        )
        if distance + 1 < lags:
            visiting = passed_along(visiting, "tm", 1)
    log_total = running[0] + jnp.log(running[1])
    mean_grad = running[2] / running[1]
    query_total = jnp.zeros(stat_shape + (HD,), jnp.float32)
    carried = jnp.zeros(resident.shape, jnp.float32)
    visiting = resident
    for distance in range(lags):
        extended = visiting
        live_mask = spatial & allowed[distance]
        grad_windows, grad_logits, grad_grad_dot = pair_terms(extended)
        probs = jnp.where(live_mask, jnp.exp(grad_logits - log_total[..., None]), 0.0)
        probs_low = probs.astype(jnp.bfloat16)
        dscore = (probs * (grad_grad_dot - mean_grad[..., None])).astype(jnp.bfloat16)
        query_part = jnp.einsum(
            "cgaqk,cgkd->cgaqd", dscore, grad_windows[0], preferred_element_type=jnp.float32
        )
        key_part = (
            jnp.einsum("cgaqk,cgaqd->cgkd", dscore, query_tiles, preferred_element_type=jnp.float32)
            * scale
        )
        value_part = jnp.einsum(
            "cgaqk,cgaqd->cgkd", probs_low, grad_tiles, preferred_element_type=jnp.float32
        )
        query_part, window_grads = (query_part, jnp.stack([key_part, value_part], 0))
        query_total = query_total + query_part
        ext_grads = from_windows(window_grads, ext_rows, total_width)
        carried = carried + ext_grads
        if distance + 1 < lags:
            visiting = passed_along(visiting, "tm", 1)
            carried = passed_along(carried, "tm", 1)
    carried = passed_along(carried, "tm", 1 - lags)
    finished = fold_rims(carried, band_rows)
    grad_queries = from_tiles(query_total * scale, band_rows)
    return (grad_queries, finished[0][None], finished[1][None])


MESH = pl.DeviceIdType.MESH
LOG2E = 1.4426950408889634
SCALE = HD**-0.5
GROUP = HQ // HK


def lag_allowed(mask_ref, clip_ref, own_frame, frames, lag):
    clips = clip_ref.shape[0]
    seen_frame = lax.rem(own_frame - lag + frames, frames)
    total = jnp.int32(0)
    rotation = jnp.int32(0)
    found = jnp.int32(0)
    for clip in range(clips):
        length = clip_ref[clip]
        first = jnp.where(length == 4, 1, 0) * (1 - found)
        rotation = rotation + first * total
        found = found + first
        total = total + length
    own_place = own_frame + 2 + rotation
    own_place = jnp.where(own_place >= frames, own_place - frames, own_place)
    own_place = jnp.where(own_place >= frames, own_place - frames, own_place)
    seen_place = seen_frame + 2 + rotation
    seen_place = jnp.where(seen_place >= frames, seen_place - frames, seen_place)
    seen_place = jnp.where(seen_place >= frames, seen_place - frames, seen_place)
    own_clip = jnp.int32(0)
    seen_clip = jnp.int32(0)
    end = jnp.int32(0)
    for clip in range(clips):
        end = end + clip_ref[clip]
        own_clip = own_clip + jnp.where(own_place >= end, 1, 0)
        seen_clip = seen_clip + jnp.where(seen_place >= end, 1, 0)
    kept = jnp.maximum(jnp.where(mask_ref[own_frame, seen_frame] == 1, 1, 0), jnp.where(lag <= 1, 1, 0))
    same = jnp.where(own_clip == seen_clip, 1, 0)
    causal = jnp.where(seen_place <= own_place, 1, 0)
    return kept * same * causal


TILE = 8
REACH = 4


def fused(
    width, frames,
    mask_hbm, clip_hbm, offset_hbm, query_hbm, key_hbm, value_hbm, cot_hbm,
    dq_out, dkv_out,
    mask_ref, clip_ref, offset_ref, query_ref, cot_ref, raw, keyed, mixed, bias, held, own_grads, grads, arrived,
    scores_low, dq_acc, final, load_sem, send_sem, recv_sem,
):
    tokens = query_ref.shape[0]
    rows = tokens // width
    tiles = width // TILE
    tile = TILE * rows
    rim = REACH * rows
    span = tile + 2 * rim
    lane_count = GROUP * tile

    def lanes(index):
        return pl.ds(pl.multiple_of(index * HD, HD), HD)

    pairs = [
        (offset_hbm, offset_ref),
        (clip_hbm, clip_ref),
        (mask_hbm, mask_ref),
        (query_hbm, query_ref),
        (cot_hbm, cot_ref),
    ]
    for g in range(HK):
        pairs.append((key_hbm.at[:, lanes(g)], raw.at[0, g, :, pl.ds(0, HD)]))
        pairs.append((value_hbm.at[:, lanes(g)], raw.at[0, g, :, pl.ds(HD, HD)]))
    loads = [pltpu.make_async_copy(pair[0], pair[1], load_sem.at[i]) for i, pair in enumerate(pairs)]
    own = lax.axis_index("tm")
    core = lax.rem(own, 2)

    def device(step):
        return {"tm": lax.rem(own + step + frames, frames)}

    partner = device(1 - 2 * core)
    ahead, behind = device(2), device(frames - 2)
    third = device(jnp.where(core == 0, frames - 3, frames - 1))
    second_to = device(jnp.where(core == 0, 1, 3))
    second_back = device(jnp.where(core == 0, frames - 3, frames - 1))

    barrier = pltpu.get_barrier_semaphore()
    for peer in (partner, behind, third):
        pl.semaphore_signal(barrier, inc=1, device_id=peer, device_id_type=MESH)
    for load in loads:
        load.start()

    def remote(index, source, target, peer):
        return pltpu.make_async_remote_copy(
            src_ref=source, dst_ref=target, send_sem=send_sem.at[index], recv_sem=recv_sem.at[index],
            device_id=peer, device_id_type=MESH,
        )

    def outward(slot, role, g, peer):
        return (
            remote(slot, key_hbm.at[:, lanes(g)], raw.at[role, g, :, pl.ds(0, HD)], peer),
            remote(slot + 1, value_hbm.at[:, lanes(g)], raw.at[role, g, :, pl.ds(HD, HD)], peer),
        )

    send_two = [outward(2 * g, 2, g, ahead) for g in range(HK)]
    send_one = [outward(4 + 2 * g, 1, g, second_to) for g in range(HK)]
    relay = [remote(8 + g, raw.at[2, g], raw.at[3, g], partner) for g in range(HK)]
    inner = pl.ds(rim, tokens)
    back_relay = [remote(10 + g, grads.at[2, g, inner], arrived.at[2, g], partner) for g in range(HK)]
    back_two = [remote(12 + g, grads.at[1, g, inner], arrived.at[1, g], behind) for g in range(HK)]
    back_one = [remote(14 + g, grads.at[0, g, inner], arrived.at[0, g], second_back) for g in range(HK)]

    pl.semaphore_wait(barrier, 3)
    for copy in send_two[0] + send_one[0]:
        copy.start()

    new_id = lax.broadcasted_iota(jnp.int32, (tokens, tokens), 0)
    old_id = lax.broadcasted_iota(jnp.int32, (tokens, tokens), 1)
    turn = jnp.where((new_id % rows) * width + new_id // rows == old_id, 1.0, 0.0).astype(jnp.bfloat16)

    def permuted(block):
        return jnp.dot(turn, block, preferred_element_type=jnp.float32).astype(jnp.bfloat16)

    for load in loads[:3]:
        load.wait()
    key_id = lax.broadcasted_iota(jnp.int32, (span, lane_count), 0)
    query_id = lax.broadcasted_iota(jnp.int32, (span, lane_count), 1) % tile
    delta_row = key_id % rows - query_id % rows
    delta_col = key_id // rows - REACH - query_id // rows
    code = jnp.where((delta_col >= -3) & (delta_col <= 3), delta_row * 8 + delta_col, 1000)

    def mark(index, hit):
        wanted = offset_ref[0, index] * 8 + offset_ref[1, index]
        return jnp.where(code == wanted, 0.0, hit)

    spatial = lax.fori_loop(
        0, offset_ref.shape[1], mark, jnp.full((span, lane_count), negative_big, jnp.float32), unroll=True
    )
    lags = (jnp.int32(0), jnp.where(core == 0, 3, 1), jnp.int32(2), jnp.where(core == 0, 1, 3))
    for role in range(4):
        allow = lag_allowed(mask_ref, clip_ref, own, frames, lags[role])
        shut = jnp.where(allow == 1, 0.0, negative_big).astype(jnp.float32)
        bias[1, role] = spatial + shut
        bias[0, role] = jnp.where(key_id < rim, negative_big, spatial) + shut
        bias[2, role] = jnp.where(key_id >= span - rim, negative_big, spatial) + shut

    blank = jnp.zeros((rim, 2 * HD), jnp.bfloat16)
    for role in range(4):
        for g in range(HK):
            keyed[g, role, pl.ds(0, rim)] = blank
            keyed[g, role, pl.ds(rim + tokens, rim)] = blank

    for load in loads[3:5]:
        load.wait()
    hole = jnp.zeros((tiles, lane_count, HD), jnp.bfloat16)
    for g in range(HK):
        mixed[g, :, pl.ds(0, lane_count), pl.ds(HD, HD)] = hole
        mixed[g, :, pl.ds(lane_count, lane_count), pl.ds(0, HD)] = hole
        for a in range(GROUP):
            h = g * GROUP + a
            mixed[g, :, pl.ds(a * tile, tile), pl.ds(0, HD)] = permuted(query_ref[:, lanes(h)]).reshape(
                tiles, tile, HD
            )
            mixed[g, :, pl.ds(lane_count + a * tile, tile), pl.ds(HD, HD)] = permuted(
                cot_ref[:, lanes(h)]
            ).reshape(tiles, tile, HD)

    def follow(first, then):
        for copy in first:
            copy.wait_send()
        for copy in then:
            copy.start()

    def place(role, g):
        keyed[g, role, pl.ds(rim, tokens)] = permuted(raw[role, g])

    for load in loads[5:]:
        load.wait()
    for g in range(HK):
        place(0, g)

    def unit(g, j):
        first = pl.multiple_of(j * tile, tile)
        window = keyed[g, :, pl.ds(first, span), :].reshape(4 * span, 2 * HD)
        mix = mixed[g, j]
        both = lax.dot_general(window, mix, (((1,), (1,)), ((), ())), preferred_element_type=jnp.float32)
        variant = jnp.where(j == 0, 0, jnp.where(j == tiles - 1, 2, 1))
        logit = both[:, :lane_count] * (SCALE * LOG2E) + bias[variant].reshape(4 * span, lane_count)
        dot = both[:, lane_count:]
        top = jnp.max(logit, axis=0, keepdims=True)
        weight = jnp.exp2(logit - top)
        total = jnp.sum(weight, axis=0, keepdims=True)
        mean = jnp.sum(weight * dot, axis=0, keepdims=True) / total
        prob = weight * (1.0 / total)
        score = (prob * (dot - mean)).astype(jnp.bfloat16)
        scores_low[g, j] = score
        low = jnp.concatenate([score, prob.astype(jnp.bfloat16)], axis=1)
        part = jnp.dot(low, mix, preferred_element_type=jnp.float32).reshape(4, span, 2 * HD)
        begin = part[:, :tile] + held[...]
        held[...] = part[:, tile:]
        own_grads[g, pl.ds(first, tile)] = begin[0]
        grads[:, g, pl.ds(first, tile)] = begin[1:].astype(jnp.bfloat16)

    def queries_unit(g, j):
        first = pl.multiple_of(j * tile, tile)
        window = keyed[g, :, pl.ds(first, span), pl.ds(0, HD)].reshape(4 * span, HD)
        out = jnp.dot(scores_low[g, j].T, window, preferred_element_type=jnp.float32)
        for a in range(GROUP):
            dq_acc[g * GROUP + a, pl.ds(first, tile)] = out[a * tile : (a + 1) * tile]

    def receive(g):
        for copy in send_two[g]:
            copy.wait_recv()
        relay[g].start()
        place(2, g)
        for copy in send_one[g]:
            copy.wait_recv()
        place(1, g)
        relay[g].wait_recv()
        place(3, g)


    def work(g):
        held[...] = jnp.zeros_like(held)

        def step(j, _):
            unit(g, j)
            return 0

        lax.fori_loop(0, tiles, step, 0, unroll=UNROLL)
        end = pl.ds(tokens, span - tile)
        own_grads[g, end] = held[0]
        grads[:, g, end] = held[1:].astype(jnp.bfloat16)
        back_relay[g].start()
        back_one[g].start()

    def pass_two(g):
        back_relay[g].wait_recv()
        grads[1, g, inner] = (
            grads[1, g, inner].astype(jnp.float32) + arrived[2, g].astype(jnp.float32)
        ).astype(jnp.bfloat16)
        back_two[g].start()

    follow(send_two[0] + send_one[0], send_two[1] + send_one[1])
    receive(0)
    work(0)
    pass_two(0)
    receive(1)
    work(1)
    pass_two(1)

    for g in range(HK):

        def turn_step(j, _, g=g):
            queries_unit(g, j)
            return 0

        lax.fori_loop(0, tiles, turn_step, 0, unroll=UNROLL)

    for h in range(HQ):
        for r in range(rows):
            dq_out[pl.ds(r * width, width), lanes(h)] = dq_acc[h, pl.ds(r, width, stride=rows), :] * SCALE

    for g in range(HK):
        back_one[g].wait_recv()
        back_two[g].wait_recv()
        came = arrived[0, g].astype(jnp.float32) + arrived[1, g].astype(jnp.float32) + own_grads[g, inner]
        final[0, g] = came[:, :HD] * SCALE
        final[1, g] = came[:, HD:]
        for r in range(rows):
            dkv_out[0, pl.ds(r * width, width), lanes(g)] = final[0, g, pl.ds(r, width, stride=rows), :]
            dkv_out[1, pl.ds(r * width, width), lanes(g)] = final[1, g, pl.ds(r, width, stride=rows), :]
    for copy in send_two[1] + send_one[1]:
        copy.wait_send()
    for g in range(HK):
        for copy in (relay[g], back_relay[g], back_two[g], back_one[g]):
            copy.wait_send()


UNROLL = 8
VL = 40 * 1024 * 1024


def fused_body(queries, keys, values, grad_out, frame_mask, clip_frames, offsets):
    _, rows, width, wide = queries.shape
    tokens = rows * width
    narrow = keys.shape[3]
    frames = lax.axis_size("tm")
    tiles = width // TILE
    tile = TILE * rows
    padded = tokens + 2 * REACH * rows
    span = tile + 2 * REACH * rows

    def flat(array):
        return array.reshape(tokens, array.shape[3])

    hbm = pl.BlockSpec(memory_space=pltpu.HBM)
    vmem = pl.BlockSpec(memory_space=pltpu.VMEM)

    def kernel(*refs):
        fused(width, frames, *refs)

    dq, dkv = pl.pallas_call(
        kernel,
        out_shape=(
            pltpu.VMEM((tokens, wide), jnp.float32),
            pltpu.VMEM((2, tokens, narrow), jnp.float32),
        ),
        in_specs=[hbm] * 7,
        out_specs=(vmem, vmem),
        scratch_shapes=[
            pltpu.SMEM(frame_mask.shape, jnp.int32),
            pltpu.SMEM(clip_frames.shape, jnp.int32),
            pltpu.SMEM(offsets.shape[::-1], jnp.int32),
            pltpu.VMEM((tokens, wide), jnp.bfloat16),
            pltpu.VMEM((tokens, wide), jnp.bfloat16),
            pltpu.VMEM((4, HK, tokens, 2 * HD), jnp.bfloat16),
            pltpu.VMEM((HK, 4, padded, 2 * HD), jnp.bfloat16),
            pltpu.VMEM((HK, tiles, 2 * GROUP * tile, 2 * HD), jnp.bfloat16),
            pltpu.VMEM((3, 4, span, GROUP * tile), jnp.float32),
            pltpu.VMEM((4, span - tile, 2 * HD), jnp.float32),
            pltpu.VMEM((HK, padded, 2 * HD), jnp.float32),
            pltpu.VMEM((3, HK, padded, 2 * HD), jnp.bfloat16),
            pltpu.VMEM((3, HK, tokens, 2 * HD), jnp.bfloat16),
            pltpu.VMEM((HK, tiles, 4 * span, GROUP * tile), jnp.bfloat16),
            pltpu.VMEM((HQ, tokens, HD), jnp.float32),
            pltpu.VMEM((2, HK, tokens, HD), jnp.float32),
            pltpu.SemaphoreType.DMA((9,)),
            pltpu.SemaphoreType.DMA((16,)),
            pltpu.SemaphoreType.DMA((16,)),
        ],
        compiler_params=pltpu.CompilerParams(
            collective_id=0, has_side_effects=True, vmem_limit_bytes=VL
        ),
    )(*[
        pltpu.with_memory_space_constraint(operand, pltpu.HBM)
        for operand in (
            frame_mask, clip_frames, offsets.T, flat(queries), flat(keys), flat(values), flat(grad_out)
        )
    ])
    def ship(dq_ref, dkv_ref, dq_out, dk_out, dv_out, sem):
        pairs = ((dq_ref, dq_out), (dkv_ref.at[0], dk_out), (dkv_ref.at[1], dv_out))
        copies = [pltpu.make_async_copy(pair[0], pair[1], sem.at[i]) for i, pair in enumerate(pairs)]
        for copy in copies:
            copy.start()
        for copy in copies:
            copy.wait()

    dq, dk, dv = pl.pallas_call(
        ship,
        out_shape=(
            jax.ShapeDtypeStruct((tokens, wide), jnp.float32),
            jax.ShapeDtypeStruct((tokens, narrow), jnp.float32),
            jax.ShapeDtypeStruct((tokens, narrow), jnp.float32),
        ),
        in_specs=[vmem] * 2,
        out_specs=[hbm] * 3,
        scratch_shapes=[pltpu.SemaphoreType.DMA((3,))],
        compiler_params=pltpu.CompilerParams(vmem_limit_bytes=4 * 1024 * 1024),
        name="ship",
    )(*[pltpu.with_memory_space_constraint(part, pltpu.VMEM) for part in (dq, dkv)])
    shape = (1, rows, width)
    return dq.reshape(shape + (wide,)), dk.reshape(shape + (narrow,)), dv.reshape(shape + (narrow,))


def solution(mesh):
    whole_rows = mesh.shape["rows"] == 1 and mesh.shape["tm"] % 2 == 0 and mesh.shape["tm"] > 6
    return jax.shard_map(
        fused_body if whole_rows else body,
        mesh=mesh,
        in_specs=(
            P(("groups", "tm"), "rows", None, None),
            P(("groups", "tm"), "rows", None, None),
            P(("groups", "tm"), "rows", None, None),
            P(("groups", "tm"), "rows", None, None),
            P("groups", None),
            P("groups"),
            P(),
        ),
        out_specs=(
            P(("groups", "tm"), "rows", None, None),
            P(("groups", "tm"), "rows", None, None),
            P(("groups", "tm"), "rows", None, None),
        ),
        check_vma=False,
    )
```

```python
import jax
import jax.numpy as jnp
from jax import lax
from jax.experimental import pallas as pl
from jax.experimental.pallas import tpu as pltpu
from jax.sharding import PartitionSpec as P

HQ = 8
HK = 2
HD = 128


tile_cols = 8
key_span = 14
negative_big = -1e30


def padded_2(cells, sides, width):
    for axis, dim in sides:
        count = lax.axis_size(axis)
        ends = count - 1
        head = lax.slice_in_dim(cells, 0, width, axis=dim)
        tail = lax.slice_in_dim(cells, cells.shape[dim] - width, cells.shape[dim], axis=dim)
        cells = jnp.concatenate(
            [
                lax.ppermute(tail, axis, [(i, (i + 1) % count) for i in range(ends)]),
                cells,
                lax.ppermute(head, axis, [((i + 1) % count, i) for i in range(ends)]),
            ],
            axis=dim,
        )
    return cells


def passed_along(value, axis, steps):
    count = lax.axis_size(axis)
    pairs = [(source, (source + steps) % count) for source in range(count)]
    return lax.ppermute(value, axis, pairs)


def to_tiles(block, group_size):
    band_rows = block.shape[0]
    count_tiles = block.shape[1] // tile_cols
    shaped = block.reshape(band_rows, count_tiles, tile_cols, HK, group_size, HD)
    shaped = shaped.transpose(1, 3, 4, 0, 2, 5)
    return shaped.reshape(count_tiles, HK, group_size, band_rows * tile_cols, HD)


def from_tiles(tiles, band_rows):
    count_tiles = tiles.shape[0]
    group_size = tiles.shape[2]
    shaped = tiles.reshape(count_tiles, HK, group_size, band_rows, tile_cols, HD)
    shaped = shaped.transpose(3, 0, 4, 1, 2, 5)
    return shaped.reshape(1, band_rows, count_tiles * tile_cols, HK * group_size * HD)


def to_windows(extended):
    ext_rows = extended.shape[1]
    total_width = extended.shape[2]
    padded = jnp.pad(extended, ((0, 0), (0, 0), (3, 3), (0, 0)))
    pieces = [
        padded[:, :, column_tile * tile_cols : column_tile * tile_cols + key_span]
        for column_tile in range(total_width // tile_cols)
    ]
    stacked = jnp.stack(pieces, 0)
    stacked = stacked.reshape(len(pieces), 2, ext_rows, key_span, HK, HD)
    stacked = stacked.transpose(1, 0, 4, 2, 3, 5)
    return stacked.reshape(2, len(pieces), HK, ext_rows * key_span, HD)


def from_windows(window_grads, ext_rows, total_width):
    count_tiles = window_grads.shape[1]
    shaped = window_grads.reshape(2, count_tiles, HK, ext_rows, key_span, HD)
    shaped = shaped.transpose(0, 1, 3, 4, 2, 5).reshape(2, count_tiles, ext_rows, key_span, HK * HD)
    summed = jnp.zeros((2, ext_rows, total_width + 6, HK * HD), jnp.float32)
    for column_tile in range(count_tiles):
        first_col = column_tile * tile_cols
        summed = summed.at[:, :, first_col : first_col + key_span].add(shaped[:, column_tile])
    return summed[:, :, 3 : 3 + total_width]


def spatial_live(offsets, band_rows, total_width):
    ext_rows = band_rows + 6
    count_tiles = total_width // tile_cols
    query_row = jnp.repeat(jnp.arange(band_rows), tile_cols)
    query_col = jnp.tile(jnp.arange(tile_cols), band_rows)
    key_row = jnp.repeat(jnp.arange(ext_rows), key_span)
    key_col = jnp.tile(jnp.arange(key_span), ext_rows)
    delta_row = key_row[None, :] - 3 - query_row[:, None]
    delta_col = key_col[None, :] - 3 - query_col[:, None]
    offset_hit = jnp.any(
        (delta_row[None] == offsets[:, 0, None, None])
        & (delta_col[None] == offsets[:, 1, None, None]),
        axis=0,
    )
    band_index = lax.axis_index("rows")
    image_rows = band_rows * lax.axis_size("rows")
    image_row = band_index * band_rows + key_row - 3
    row_inside = (image_row >= 0) & (image_row < image_rows)
    tile_first = jnp.arange(count_tiles) * tile_cols
    image_col = tile_first[:, None] + key_col[None, :] - 3
    col_inside = (image_col >= 0) & (image_col < total_width)
    return offset_hit[None] & row_inside[None, None] & col_inside[:, None, :]


def running_sum(entries):
    places = jnp.arange(entries.shape[0])
    return jnp.sum(jnp.where(places[None, :] <= places[:, None], entries[None, :], 0), axis=1)


def frame_allowed(frame_mask, clip_frames, distance):
    frames = lax.axis_size("tm")
    lags = min(4, frames)
    own_frame = lax.axis_index("tm")
    seen_frame = (own_frame - distance) % frames
    clip_ends = running_sum(clip_frames)
    clip_starts = clip_ends - clip_frames
    is_longest = (clip_frames == lags).astype(jnp.int32)
    first_longest = (is_longest == 1) & (running_sum(is_longest) == 1)
    rotation = jnp.sum(jnp.where(first_longest, clip_starts, 0))
    own_place = (own_frame + 2 + rotation) % frames
    seen_place = (seen_frame + 2 + rotation) % frames
    own_clip = jnp.sum((own_place >= clip_ends).astype(jnp.int32))
    seen_clip = jnp.sum((seen_place >= clip_ends).astype(jnp.int32))
    grid_rows = jnp.arange(frames)[:, None]
    grid_cols = jnp.arange(frames)[None, :]
    picked = jnp.sum(jnp.where((grid_rows == own_frame) & (grid_cols == seen_frame), frame_mask, 0))
    kept = (picked == 1) | (distance <= 1)
    return (own_clip == seen_clip) & (seen_place <= own_place) & kept


def fold_rims(extended_grads, band_rows):
    interior = extended_grads[:, 3 : 3 + band_rows]
    rim_rows = jnp.concatenate([extended_grads[:, :3], extended_grads[:, band_rows + 3 :]], 1)
    haloed = padded_2(rim_rows.astype(jnp.bfloat16), (("rows", 1),), 3).astype(rim_rows.dtype)
    interior = interior.at[:, :3].add(haloed[:, :3])
    return interior.at[:, band_rows - 3 :].add(haloed[:, 9:])


def body(queries, keys, values, grad_out, frame_mask, clip_frames, offsets):
    band_rows = queries.shape[1]
    total_width = queries.shape[2]
    ext_rows = band_rows + 6
    group_size = HQ // HK
    scale = HD ** (-0.5)
    lags = min(4, lax.axis_size("tm"))
    query_tiles = to_tiles(queries[0], group_size)
    grad_tiles = to_tiles(grad_out[0], group_size)
    spatial = spatial_live(offsets, band_rows, total_width)[:, None, None]
    allowed = [frame_allowed(frame_mask, clip_frames, distance) for distance in range(lags)]
    stacked = jnp.stack([keys[0], values[0]], 0)
    resident = padded_2(stacked, (("rows", 1),), 3)

    def pair_terms(extended):
        windows = to_windows(extended)
        logits = (
            jnp.einsum(
                "cgaqd,cgkd->cgaqk", query_tiles, windows[0], preferred_element_type=jnp.float32
            )
            * scale
        )
        grad_dot = jnp.einsum(
            "cgaqd,cgkd->cgaqk", grad_tiles, windows[1], preferred_element_type=jnp.float32
        )
        return (windows, logits, grad_dot)

    stat_shape = (total_width // tile_cols, HK, group_size, band_rows * tile_cols)
    running = (
        jnp.full(stat_shape, negative_big, jnp.float32),
        jnp.zeros(stat_shape, jnp.float32),
        jnp.zeros(stat_shape, jnp.float32),
    )
    visiting = resident
    visited = []
    for distance in range(lags):
        visited.append(visiting)
        extended = visiting
        live_mask = spatial & allowed[distance]
        run_max, run_sum, run_dot = running
        stat_windows, stat_logits, stat_grad_dot = pair_terms(extended)
        masked = jnp.where(live_mask, stat_logits, negative_big)
        new_max = jnp.maximum(run_max, jnp.max(masked, axis=-1))
        factor = jnp.exp(run_max - new_max)
        weights = jnp.where(live_mask, jnp.exp(stat_logits - new_max[..., None]), 0.0)
        running = (
            new_max,
            run_sum * factor + jnp.sum(weights, axis=-1),
            run_dot * factor + jnp.sum(weights * stat_grad_dot, axis=-1),
        )
        if distance + 1 < lags:
            visiting = passed_along(visiting, "tm", 1)
    log_total = running[0] + jnp.log(running[1])
    mean_grad = running[2] / running[1]
    query_total = jnp.zeros(stat_shape + (HD,), jnp.float32)
    carried = jnp.zeros(resident.shape, jnp.float32)
    visiting = resident
    for distance in range(lags):
        extended = visiting
        live_mask = spatial & allowed[distance]
        grad_windows, grad_logits, grad_grad_dot = pair_terms(extended)
        probs = jnp.where(live_mask, jnp.exp(grad_logits - log_total[..., None]), 0.0)
        probs_low = probs.astype(jnp.bfloat16)
        dscore = (probs * (grad_grad_dot - mean_grad[..., None])).astype(jnp.bfloat16)
        query_part = jnp.einsum(
            "cgaqk,cgkd->cgaqd", dscore, grad_windows[0], preferred_element_type=jnp.float32
        )
        key_part = (
            jnp.einsum("cgaqk,cgaqd->cgkd", dscore, query_tiles, preferred_element_type=jnp.float32)
            * scale
        )
        value_part = jnp.einsum(
            "cgaqk,cgaqd->cgkd", probs_low, grad_tiles, preferred_element_type=jnp.float32
        )
        query_part, window_grads = (query_part, jnp.stack([key_part, value_part], 0))
        query_total = query_total + query_part
        ext_grads = from_windows(window_grads, ext_rows, total_width)
        carried = carried + ext_grads
        if distance + 1 < lags:
            visiting = passed_along(visiting, "tm", 1)
            carried = passed_along(carried, "tm", 1)
    carried = passed_along(carried, "tm", 1 - lags)
    finished = fold_rims(carried, band_rows)
    grad_queries = from_tiles(query_total * scale, band_rows)
    return (grad_queries, finished[0][None], finished[1][None])


MESH = pl.DeviceIdType.MESH
LOG2E = 1.4426950408889634
SCALE = HD**-0.5
GROUP = HQ // HK


def lag_allowed(mask_ref, clip_ref, own_frame, frames, lag):
    clips = clip_ref.shape[0]
    seen_frame = lax.rem(own_frame - lag + frames, frames)
    total = jnp.int32(0)
    rotation = jnp.int32(0)
    found = jnp.int32(0)
    for clip in range(clips):
        length = clip_ref[clip]
        first = jnp.where(length == 4, 1, 0) * (1 - found)
        rotation = rotation + first * total
        found = found + first
        total = total + length
    own_place = own_frame + 2 + rotation
    own_place = jnp.where(own_place >= frames, own_place - frames, own_place)
    own_place = jnp.where(own_place >= frames, own_place - frames, own_place)
    seen_place = seen_frame + 2 + rotation
    seen_place = jnp.where(seen_place >= frames, seen_place - frames, seen_place)
    seen_place = jnp.where(seen_place >= frames, seen_place - frames, seen_place)
    own_clip = jnp.int32(0)
    seen_clip = jnp.int32(0)
    end = jnp.int32(0)
    for clip in range(clips):
        end = end + clip_ref[clip]
        own_clip = own_clip + jnp.where(own_place >= end, 1, 0)
        seen_clip = seen_clip + jnp.where(seen_place >= end, 1, 0)
    kept = jnp.maximum(jnp.where(mask_ref[own_frame, seen_frame] == 1, 1, 0), jnp.where(lag <= 1, 1, 0))
    same = jnp.where(own_clip == seen_clip, 1, 0)
    causal = jnp.where(seen_place <= own_place, 1, 0)
    return kept * same * causal


TILE = 8
REACH = 4


def fused(
    width, frames,
    mask_hbm, clip_hbm, offset_hbm, query_hbm, key_hbm, value_hbm, cot_hbm,
    dq_out, dkv_out,
    mask_ref, clip_ref, offset_ref, query_ref, cot_ref, raw, keyed, mixed, bias, held, own_grads, grads, arrived,
    scores_low, dq_acc, final, load_sem, send_sem, recv_sem,
):
    tokens = query_ref.shape[0]
    rows = tokens // width
    tiles = width // TILE
    tile = TILE * rows
    rim = REACH * rows
    span = tile + 2 * rim
    lane_count = GROUP * tile

    def lanes(index):
        return pl.ds(pl.multiple_of(index * HD, HD), HD)

    pairs = [
        (offset_hbm, offset_ref),
        (clip_hbm, clip_ref),
        (mask_hbm, mask_ref),
        (query_hbm, query_ref),
        (cot_hbm, cot_ref),
    ]
    for g in range(HK):
        pairs.append((key_hbm.at[:, lanes(g)], raw.at[0, g, :, pl.ds(0, HD)]))
        pairs.append((value_hbm.at[:, lanes(g)], raw.at[0, g, :, pl.ds(HD, HD)]))
    loads = [pltpu.make_async_copy(pair[0], pair[1], load_sem.at[i]) for i, pair in enumerate(pairs)]
    own = lax.axis_index("tm")
    core = lax.rem(own, 2)

    def device(step):
        return {"tm": lax.rem(own + step + frames, frames)}

    partner = device(1 - 2 * core)
    ahead, behind = device(2), device(frames - 2)
    third = device(jnp.where(core == 0, frames - 3, frames - 1))
    second_to = device(jnp.where(core == 0, 1, 3))
    second_back = device(jnp.where(core == 0, frames - 3, frames - 1))

    barrier = pltpu.get_barrier_semaphore()
    for peer in (partner, behind, third):
        pl.semaphore_signal(barrier, inc=1, device_id=peer, device_id_type=MESH)
    for load in loads:
        load.start()

    def remote(index, source, target, peer):
        return pltpu.make_async_remote_copy(
            src_ref=source, dst_ref=target, send_sem=send_sem.at[index], recv_sem=recv_sem.at[index],
            device_id=peer, device_id_type=MESH,
        )

    def outward(slot, role, g, peer):
        if g in STAGED:
            return (remote(slot, raw.at[0, g], raw.at[role, g], peer),)
        return (
            remote(slot, key_hbm.at[:, lanes(g)], raw.at[role, g, :, pl.ds(0, HD)], peer),
            remote(slot + 1, value_hbm.at[:, lanes(g)], raw.at[role, g, :, pl.ds(HD, HD)], peer),
        )

    send_two = [outward(2 * g, 2, g, ahead) for g in range(HK)]
    send_one = [outward(4 + 2 * g, 1, g, second_to) for g in range(HK)]
    relay = [remote(8 + g, raw.at[2, g], raw.at[3, g], partner) for g in range(HK)]
    inner = pl.ds(rim, tokens)
    back_relay = [remote(10 + g, grads.at[2, g, inner], arrived.at[2, g], partner) for g in range(HK)]
    back_two = [remote(12 + g, grads.at[1, g, inner], arrived.at[1, g], behind) for g in range(HK)]
    back_one = [remote(14 + g, grads.at[0, g, inner], arrived.at[0, g], second_back) for g in range(HK)]

    pl.semaphore_wait(barrier, 3)
    odd_last = lax.rem(own, 4) == 3
    for copy in send_two[0] + send_one[0]:
        copy.start()

    for load in loads[7:]:
        load.wait()

    @pl.when(jnp.logical_not(odd_last))
    def _():
        for copy in send_one[1]:
            copy.start()


    new_id = lax.broadcasted_iota(jnp.int32, (tokens, tokens), 0)
    old_id = lax.broadcasted_iota(jnp.int32, (tokens, tokens), 1)
    turn = jnp.where((new_id % rows) * width + new_id // rows == old_id, 1.0, 0.0).astype(jnp.bfloat16)

    def permuted(block):
        return jnp.dot(turn, block, preferred_element_type=jnp.float32).astype(jnp.bfloat16)

    for load in loads[:3]:
        load.wait()
    key_id = lax.broadcasted_iota(jnp.int32, (span, lane_count), 0)
    query_id = lax.broadcasted_iota(jnp.int32, (span, lane_count), 1) % tile
    delta_row = key_id % rows - query_id % rows
    delta_col = key_id // rows - REACH - query_id // rows
    code = jnp.where((delta_col >= -3) & (delta_col <= 3), delta_row * 8 + delta_col, 1000)

    def mark(index, hit):
        wanted = offset_ref[0, index] * 8 + offset_ref[1, index]
        return jnp.where(code == wanted, 0.0, hit)

    spatial = lax.fori_loop(
        0, offset_ref.shape[1], mark, jnp.full((span, lane_count), negative_big, jnp.float32), unroll=True
    )
    lags = (jnp.int32(0), jnp.where(core == 0, 3, 1), jnp.int32(2), jnp.where(core == 0, 1, 3))
    for role in range(4):
        allow = lag_allowed(mask_ref, clip_ref, own, frames, lags[role])
        shut = jnp.where(allow == 1, 0.0, negative_big).astype(jnp.float32)
        bias[1, role] = spatial + shut
        bias[0, role] = jnp.where(key_id < rim, negative_big, spatial) + shut
        bias[2, role] = jnp.where(key_id >= span - rim, negative_big, spatial) + shut

    blank = jnp.zeros((rim, 2 * HD), jnp.bfloat16)
    for role in range(4):
        for g in range(HK):
            keyed[g, role, pl.ds(0, rim)] = blank
            keyed[g, role, pl.ds(rim + tokens, rim)] = blank

    for load in loads[3:5]:
        load.wait()
    hole = jnp.zeros((tiles, lane_count, HD), jnp.bfloat16)
    for g in range(HK):
        mixed[g, :, pl.ds(0, lane_count), pl.ds(HD, HD)] = hole
        mixed[g, :, pl.ds(lane_count, lane_count), pl.ds(0, HD)] = hole
        for a in range(GROUP):
            h = g * GROUP + a
            mixed[g, :, pl.ds(a * tile, tile), pl.ds(0, HD)] = permuted(query_ref[:, lanes(h)]).reshape(
                tiles, tile, HD
            )
            mixed[g, :, pl.ds(lane_count + a * tile, tile), pl.ds(HD, HD)] = permuted(
                cot_ref[:, lanes(h)]
            ).reshape(tiles, tile, HD)

    def follow(first, then):
        for copy in first:
            copy.wait_send()
        for copy in then:
            copy.start()

    def place(role, g):
        keyed[g, role, pl.ds(rim, tokens)] = permuted(raw[role, g])

    for load in loads[5:7]:
        load.wait()
    for g in range(HK):
        place(0, g)

    def unit(g, j):
        first = pl.multiple_of(j * tile, tile)
        window = keyed[g, :, pl.ds(first, span), :].reshape(4 * span, 2 * HD)
        mix = mixed[g, j]
        both = lax.dot_general(window, mix, (((1,), (1,)), ((), ())), preferred_element_type=jnp.float32)
        variant = jnp.where(j == 0, 0, jnp.where(j == tiles - 1, 2, 1))
        logit = both[:, :lane_count] * (SCALE * LOG2E) + bias[variant].reshape(4 * span, lane_count)
        dot = both[:, lane_count:]
        top = jnp.max(logit, axis=0, keepdims=True)
        weight = jnp.exp2(logit - top)
        total = jnp.sum(weight, axis=0, keepdims=True)
        mean = jnp.sum(weight * dot, axis=0, keepdims=True) / total
        prob = weight * (1.0 / total)
        score = (prob * (dot - mean)).astype(jnp.bfloat16)
        scores_low[g, j] = score
        low = jnp.concatenate([score, prob.astype(jnp.bfloat16)], axis=1)
        part = jnp.dot(low, mix, preferred_element_type=jnp.float32).reshape(4, span, 2 * HD)
        begin = part[:, :tile] + held[...]
        held[...] = part[:, tile:]
        own_grads[g, pl.ds(first, tile)] = begin[0]
        grads[:, g, pl.ds(first, tile)] = begin[1:].astype(jnp.bfloat16)

    def queries_unit(g, j):
        first = pl.multiple_of(j * tile, tile)
        window = keyed[g, :, pl.ds(first, span), pl.ds(0, HD)].reshape(4 * span, HD)
        out = jnp.dot(scores_low[g, j].T, window, preferred_element_type=jnp.float32)
        for a in range(GROUP):
            dq_acc[g * GROUP + a, pl.ds(first, tile)] = out[a * tile : (a + 1) * tile]

    def receive(g):
        for copy in send_two[g]:
            copy.wait_recv()
        relay[g].start()
        place(2, g)
        for copy in send_one[g]:
            copy.wait_recv()
        place(1, g)
        relay[g].wait_recv()
        place(3, g)


    def work(g):
        held[...] = jnp.zeros_like(held)

        def step(j, _):
            unit(g, j)
            return 0

        lax.fori_loop(0, tiles, step, 0, unroll=UNROLL)
        end = pl.ds(tokens, span - tile)
        own_grads[g, end] = held[0]
        grads[:, g, end] = held[1:].astype(jnp.bfloat16)
        back_relay[g].start()
        back_one[g].start()

    def pass_two(g):
        back_relay[g].wait_recv()
        grads[1, g, inner] = (
            grads[1, g, inner].astype(jnp.float32) + arrived[2, g].astype(jnp.float32)
        ).astype(jnp.bfloat16)
        back_two[g].start()

    follow(send_two[0], send_two[1])
    follow(send_one[0], ())

    @pl.when(odd_last)
    def _():
        follow((), send_one[1])

    receive(0)
    work(0)
    pass_two(0)
    receive(1)
    work(1)
    pass_two(1)

    for g in range(HK):

        def turn_step(j, _, g=g):
            queries_unit(g, j)
            return 0

        lax.fori_loop(0, tiles, turn_step, 0, unroll=UNROLL)

    for h in range(HQ):
        for r in range(rows):
            dq_out[pl.ds(r * width, width), lanes(h)] = dq_acc[h, pl.ds(r, width, stride=rows), :] * SCALE

    for g in range(HK):
        back_one[g].wait_recv()
        back_two[g].wait_recv()
        came = arrived[0, g].astype(jnp.float32) + arrived[1, g].astype(jnp.float32) + own_grads[g, inner]
        final[0, g] = came[:, :HD] * SCALE
        final[1, g] = came[:, HD:]
        for r in range(rows):
            dkv_out[0, pl.ds(r * width, width), lanes(g)] = final[0, g, pl.ds(r, width, stride=rows), :]
            dkv_out[1, pl.ds(r * width, width), lanes(g)] = final[1, g, pl.ds(r, width, stride=rows), :]
    for copy in send_two[1] + send_one[1]:
        copy.wait_send()
    for g in range(HK):
        for copy in (relay[g], back_relay[g], back_two[g], back_one[g]):
            copy.wait_send()


UNROLL = 8
STAGED = (1,)
VL = 40 * 1024 * 1024


def fused_body(queries, keys, values, grad_out, frame_mask, clip_frames, offsets):
    _, rows, width, wide = queries.shape
    tokens = rows * width
    narrow = keys.shape[3]
    frames = lax.axis_size("tm")
    tiles = width // TILE
    tile = TILE * rows
    padded = tokens + 2 * REACH * rows
    span = tile + 2 * REACH * rows

    def flat(array):
        return array.reshape(tokens, array.shape[3])

    hbm = pl.BlockSpec(memory_space=pltpu.HBM)
    vmem = pl.BlockSpec(memory_space=pltpu.VMEM)

    def kernel(*refs):
        fused(width, frames, *refs)

    dq, dkv = pl.pallas_call(
        kernel,
        out_shape=(
            pltpu.VMEM((tokens, wide), jnp.float32),
            pltpu.VMEM((2, tokens, narrow), jnp.float32),
        ),
        in_specs=[hbm] * 7,
        out_specs=(vmem, vmem),
        scratch_shapes=[
            pltpu.SMEM(frame_mask.shape, jnp.int32),
            pltpu.SMEM(clip_frames.shape, jnp.int32),
            pltpu.SMEM(offsets.shape[::-1], jnp.int32),
            pltpu.VMEM((tokens, wide), jnp.bfloat16),
            pltpu.VMEM((tokens, wide), jnp.bfloat16),
            pltpu.VMEM((4, HK, tokens, 2 * HD), jnp.bfloat16),
            pltpu.VMEM((HK, 4, padded, 2 * HD), jnp.bfloat16),
            pltpu.VMEM((HK, tiles, 2 * GROUP * tile, 2 * HD), jnp.bfloat16),
            pltpu.VMEM((3, 4, span, GROUP * tile), jnp.float32),
            pltpu.VMEM((4, span - tile, 2 * HD), jnp.float32),
            pltpu.VMEM((HK, padded, 2 * HD), jnp.float32),
            pltpu.VMEM((3, HK, padded, 2 * HD), jnp.bfloat16),
            pltpu.VMEM((3, HK, tokens, 2 * HD), jnp.bfloat16),
            pltpu.VMEM((HK, tiles, 4 * span, GROUP * tile), jnp.bfloat16),
            pltpu.VMEM((HQ, tokens, HD), jnp.float32),
            pltpu.VMEM((2, HK, tokens, HD), jnp.float32),
            pltpu.SemaphoreType.DMA((9,)),
            pltpu.SemaphoreType.DMA((16,)),
            pltpu.SemaphoreType.DMA((16,)),
        ],
        compiler_params=pltpu.CompilerParams(
            collective_id=0, has_side_effects=True, vmem_limit_bytes=VL
        ),
    )(*[
        pltpu.with_memory_space_constraint(operand, pltpu.HBM)
        for operand in (
            frame_mask, clip_frames, offsets.T, flat(queries), flat(keys), flat(values), flat(grad_out)
        )
    ])
    def ship(dq_ref, dkv_ref, dq_out, dk_out, dv_out, sem):
        pairs = ((dq_ref, dq_out), (dkv_ref.at[0], dk_out), (dkv_ref.at[1], dv_out))
        copies = [pltpu.make_async_copy(pair[0], pair[1], sem.at[i]) for i, pair in enumerate(pairs)]
        for copy in copies:
            copy.start()
        for copy in copies:
            copy.wait()

    dq, dk, dv = pl.pallas_call(
        ship,
        out_shape=(
            jax.ShapeDtypeStruct((tokens, wide), jnp.float32),
            jax.ShapeDtypeStruct((tokens, narrow), jnp.float32),
            jax.ShapeDtypeStruct((tokens, narrow), jnp.float32),
        ),
        in_specs=[vmem] * 2,
        out_specs=[hbm] * 3,
        scratch_shapes=[pltpu.SemaphoreType.DMA((3,))],
        compiler_params=pltpu.CompilerParams(vmem_limit_bytes=4 * 1024 * 1024),
        name="ship",
    )(*[pltpu.with_memory_space_constraint(part, pltpu.VMEM) for part in (dq, dkv)])
    shape = (1, rows, width)
    return dq.reshape(shape + (wide,)), dk.reshape(shape + (narrow,)), dv.reshape(shape + (narrow,))


def solution(mesh):
    whole_rows = mesh.shape["rows"] == 1 and mesh.shape["tm"] % 2 == 0 and mesh.shape["tm"] > 6
    return jax.shard_map(
        fused_body if whole_rows else body,
        mesh=mesh,
        in_specs=(
            P(("groups", "tm"), "rows", None, None),
            P(("groups", "tm"), "rows", None, None),
            P(("groups", "tm"), "rows", None, None),
            P(("groups", "tm"), "rows", None, None),
            P("groups", None),
            P("groups"),
            P(),
        ),
        out_specs=(
            P(("groups", "tm"), "rows", None, None),
            P(("groups", "tm"), "rows", None, None),
            P(("groups", "tm"), "rows", None, None),
        ),
        check_vma=False,
    )
```

```python
import jax
import jax.numpy as jnp
from jax import lax
from jax.experimental import pallas as pl
from jax.experimental.pallas import tpu as pltpu
from jax.sharding import PartitionSpec as P

HQ = 8
HK = 2
HD = 128


tile_cols = 8
key_span = 14
negative_big = -1e30


def padded_2(cells, sides, width):
    for axis, dim in sides:
        count = lax.axis_size(axis)
        ends = count - 1
        head = lax.slice_in_dim(cells, 0, width, axis=dim)
        tail = lax.slice_in_dim(cells, cells.shape[dim] - width, cells.shape[dim], axis=dim)
        cells = jnp.concatenate(
            [
                lax.ppermute(tail, axis, [(i, (i + 1) % count) for i in range(ends)]),
                cells,
                lax.ppermute(head, axis, [((i + 1) % count, i) for i in range(ends)]),
            ],
            axis=dim,
        )
    return cells


def passed_along(value, axis, steps):
    count = lax.axis_size(axis)
    pairs = [(source, (source + steps) % count) for source in range(count)]
    return lax.ppermute(value, axis, pairs)


def to_tiles(block, group_size):
    band_rows = block.shape[0]
    count_tiles = block.shape[1] // tile_cols
    shaped = block.reshape(band_rows, count_tiles, tile_cols, HK, group_size, HD)
    shaped = shaped.transpose(1, 3, 4, 0, 2, 5)
    return shaped.reshape(count_tiles, HK, group_size, band_rows * tile_cols, HD)


def from_tiles(tiles, band_rows):
    count_tiles = tiles.shape[0]
    group_size = tiles.shape[2]
    shaped = tiles.reshape(count_tiles, HK, group_size, band_rows, tile_cols, HD)
    shaped = shaped.transpose(3, 0, 4, 1, 2, 5)
    return shaped.reshape(1, band_rows, count_tiles * tile_cols, HK * group_size * HD)


def to_windows(extended):
    ext_rows = extended.shape[1]
    total_width = extended.shape[2]
    padded = jnp.pad(extended, ((0, 0), (0, 0), (3, 3), (0, 0)))
    pieces = [
        padded[:, :, column_tile * tile_cols : column_tile * tile_cols + key_span]
        for column_tile in range(total_width // tile_cols)
    ]
    stacked = jnp.stack(pieces, 0)
    stacked = stacked.reshape(len(pieces), 2, ext_rows, key_span, HK, HD)
    stacked = stacked.transpose(1, 0, 4, 2, 3, 5)
    return stacked.reshape(2, len(pieces), HK, ext_rows * key_span, HD)


def from_windows(window_grads, ext_rows, total_width):
    count_tiles = window_grads.shape[1]
    shaped = window_grads.reshape(2, count_tiles, HK, ext_rows, key_span, HD)
    shaped = shaped.transpose(0, 1, 3, 4, 2, 5).reshape(2, count_tiles, ext_rows, key_span, HK * HD)
    summed = jnp.zeros((2, ext_rows, total_width + 6, HK * HD), jnp.float32)
    for column_tile in range(count_tiles):
        first_col = column_tile * tile_cols
        summed = summed.at[:, :, first_col : first_col + key_span].add(shaped[:, column_tile])
    return summed[:, :, 3 : 3 + total_width]


def spatial_live(offsets, band_rows, total_width):
    ext_rows = band_rows + 6
    count_tiles = total_width // tile_cols
    query_row = jnp.repeat(jnp.arange(band_rows), tile_cols)
    query_col = jnp.tile(jnp.arange(tile_cols), band_rows)
    key_row = jnp.repeat(jnp.arange(ext_rows), key_span)
    key_col = jnp.tile(jnp.arange(key_span), ext_rows)
    delta_row = key_row[None, :] - 3 - query_row[:, None]
    delta_col = key_col[None, :] - 3 - query_col[:, None]
    offset_hit = jnp.any(
        (delta_row[None] == offsets[:, 0, None, None])
        & (delta_col[None] == offsets[:, 1, None, None]),
        axis=0,
    )
    band_index = lax.axis_index("rows")
    image_rows = band_rows * lax.axis_size("rows")
    image_row = band_index * band_rows + key_row - 3
    row_inside = (image_row >= 0) & (image_row < image_rows)
    tile_first = jnp.arange(count_tiles) * tile_cols
    image_col = tile_first[:, None] + key_col[None, :] - 3
    col_inside = (image_col >= 0) & (image_col < total_width)
    return offset_hit[None] & row_inside[None, None] & col_inside[:, None, :]


def running_sum(entries):
    places = jnp.arange(entries.shape[0])
    return jnp.sum(jnp.where(places[None, :] <= places[:, None], entries[None, :], 0), axis=1)


def frame_allowed(frame_mask, clip_frames, distance):
    frames = lax.axis_size("tm")
    lags = min(4, frames)
    own_frame = lax.axis_index("tm")
    seen_frame = (own_frame - distance) % frames
    clip_ends = running_sum(clip_frames)
    clip_starts = clip_ends - clip_frames
    is_longest = (clip_frames == lags).astype(jnp.int32)
    first_longest = (is_longest == 1) & (running_sum(is_longest) == 1)
    rotation = jnp.sum(jnp.where(first_longest, clip_starts, 0))
    own_place = (own_frame + 2 + rotation) % frames
    seen_place = (seen_frame + 2 + rotation) % frames
    own_clip = jnp.sum((own_place >= clip_ends).astype(jnp.int32))
    seen_clip = jnp.sum((seen_place >= clip_ends).astype(jnp.int32))
    grid_rows = jnp.arange(frames)[:, None]
    grid_cols = jnp.arange(frames)[None, :]
    picked = jnp.sum(jnp.where((grid_rows == own_frame) & (grid_cols == seen_frame), frame_mask, 0))
    kept = (picked == 1) | (distance <= 1)
    return (own_clip == seen_clip) & (seen_place <= own_place) & kept


def fold_rims(extended_grads, band_rows):
    interior = extended_grads[:, 3 : 3 + band_rows]
    rim_rows = jnp.concatenate([extended_grads[:, :3], extended_grads[:, band_rows + 3 :]], 1)
    haloed = padded_2(rim_rows.astype(jnp.bfloat16), (("rows", 1),), 3).astype(rim_rows.dtype)
    interior = interior.at[:, :3].add(haloed[:, :3])
    return interior.at[:, band_rows - 3 :].add(haloed[:, 9:])


def body(queries, keys, values, grad_out, frame_mask, clip_frames, offsets):
    band_rows = queries.shape[1]
    total_width = queries.shape[2]
    ext_rows = band_rows + 6
    group_size = HQ // HK
    scale = HD ** (-0.5)
    lags = min(4, lax.axis_size("tm"))
    query_tiles = to_tiles(queries[0], group_size)
    grad_tiles = to_tiles(grad_out[0], group_size)
    spatial = spatial_live(offsets, band_rows, total_width)[:, None, None]
    allowed = [frame_allowed(frame_mask, clip_frames, distance) for distance in range(lags)]
    stacked = jnp.stack([keys[0], values[0]], 0)
    resident = padded_2(stacked, (("rows", 1),), 3)

    def pair_terms(extended):
        windows = to_windows(extended)
        logits = (
            jnp.einsum(
                "cgaqd,cgkd->cgaqk", query_tiles, windows[0], preferred_element_type=jnp.float32
            )
            * scale
        )
        grad_dot = jnp.einsum(
            "cgaqd,cgkd->cgaqk", grad_tiles, windows[1], preferred_element_type=jnp.float32
        )
        return (windows, logits, grad_dot)

    stat_shape = (total_width // tile_cols, HK, group_size, band_rows * tile_cols)
    running = (
        jnp.full(stat_shape, negative_big, jnp.float32),
        jnp.zeros(stat_shape, jnp.float32),
        jnp.zeros(stat_shape, jnp.float32),
    )
    visiting = resident
    visited = []
    for distance in range(lags):
        visited.append(visiting)
        extended = visiting
        live_mask = spatial & allowed[distance]
        run_max, run_sum, run_dot = running
        stat_windows, stat_logits, stat_grad_dot = pair_terms(extended)
        masked = jnp.where(live_mask, stat_logits, negative_big)
        new_max = jnp.maximum(run_max, jnp.max(masked, axis=-1))
        factor = jnp.exp(run_max - new_max)
        weights = jnp.where(live_mask, jnp.exp(stat_logits - new_max[..., None]), 0.0)
        running = (
            new_max,
            run_sum * factor + jnp.sum(weights, axis=-1),
            run_dot * factor + jnp.sum(weights * stat_grad_dot, axis=-1),
        )
        if distance + 1 < lags:
            visiting = passed_along(visiting, "tm", 1)
    log_total = running[0] + jnp.log(running[1])
    mean_grad = running[2] / running[1]
    query_total = jnp.zeros(stat_shape + (HD,), jnp.float32)
    carried = jnp.zeros(resident.shape, jnp.float32)
    visiting = resident
    for distance in range(lags):
        extended = visiting
        live_mask = spatial & allowed[distance]
        grad_windows, grad_logits, grad_grad_dot = pair_terms(extended)
        probs = jnp.where(live_mask, jnp.exp(grad_logits - log_total[..., None]), 0.0)
        probs_low = probs.astype(jnp.bfloat16)
        dscore = (probs * (grad_grad_dot - mean_grad[..., None])).astype(jnp.bfloat16)
        query_part = jnp.einsum(
            "cgaqk,cgkd->cgaqd", dscore, grad_windows[0], preferred_element_type=jnp.float32
        )
        key_part = (
            jnp.einsum("cgaqk,cgaqd->cgkd", dscore, query_tiles, preferred_element_type=jnp.float32)
            * scale
        )
        value_part = jnp.einsum(
            "cgaqk,cgaqd->cgkd", probs_low, grad_tiles, preferred_element_type=jnp.float32
        )
        query_part, window_grads = (query_part, jnp.stack([key_part, value_part], 0))
        query_total = query_total + query_part
        ext_grads = from_windows(window_grads, ext_rows, total_width)
        carried = carried + ext_grads
        if distance + 1 < lags:
            visiting = passed_along(visiting, "tm", 1)
            carried = passed_along(carried, "tm", 1)
    carried = passed_along(carried, "tm", 1 - lags)
    finished = fold_rims(carried, band_rows)
    grad_queries = from_tiles(query_total * scale, band_rows)
    return (grad_queries, finished[0][None], finished[1][None])


MESH = pl.DeviceIdType.MESH
LOG2E = 1.4426950408889634
SCALE = HD**-0.5
GROUP = HQ // HK


def lag_allowed(mask_ref, clip_ref, own_frame, frames, lag):
    clips = clip_ref.shape[0]
    seen_frame = lax.rem(own_frame - lag + frames, frames)
    total = jnp.int32(0)
    rotation = jnp.int32(0)
    found = jnp.int32(0)
    for clip in range(clips):
        length = clip_ref[clip]
        first = jnp.where(length == 4, 1, 0) * (1 - found)
        rotation = rotation + first * total
        found = found + first
        total = total + length
    own_place = own_frame + 2 + rotation
    own_place = jnp.where(own_place >= frames, own_place - frames, own_place)
    own_place = jnp.where(own_place >= frames, own_place - frames, own_place)
    seen_place = seen_frame + 2 + rotation
    seen_place = jnp.where(seen_place >= frames, seen_place - frames, seen_place)
    seen_place = jnp.where(seen_place >= frames, seen_place - frames, seen_place)
    own_clip = jnp.int32(0)
    seen_clip = jnp.int32(0)
    end = jnp.int32(0)
    for clip in range(clips):
        end = end + clip_ref[clip]
        own_clip = own_clip + jnp.where(own_place >= end, 1, 0)
        seen_clip = seen_clip + jnp.where(seen_place >= end, 1, 0)
    kept = jnp.maximum(jnp.where(mask_ref[own_frame, seen_frame] == 1, 1, 0), jnp.where(lag <= 1, 1, 0))
    same = jnp.where(own_clip == seen_clip, 1, 0)
    causal = jnp.where(seen_place <= own_place, 1, 0)
    return kept * same * causal


TILE = 8
REACH = 4


def fused(
    width, frames,
    mask_hbm, clip_hbm, offset_hbm, query_hbm, key_hbm, value_hbm, cot_hbm,
    dq_out, dkv_out,
    mask_ref, clip_ref, offset_ref, query_ref, cot_ref, raw, keyed, mixed, bias, held, own_grads, grads, arrived,
    scores_low, dq_acc, final, load_sem, send_sem, recv_sem,
):
    tokens = query_ref.shape[0]
    rows = tokens // width
    tiles = width // TILE
    tile = TILE * rows
    rim = REACH * rows
    span = tile + 2 * rim
    lane_count = GROUP * tile

    def lanes(index):
        return pl.ds(pl.multiple_of(index * HD, HD), HD)

    pairs = [
        (offset_hbm, offset_ref),
        (clip_hbm, clip_ref),
        (mask_hbm, mask_ref),
        (query_hbm, query_ref),
        (cot_hbm, cot_ref),
    ]
    for g in range(HK):
        pairs.append((key_hbm.at[:, lanes(g)], raw.at[0, g, :, pl.ds(0, HD)]))
        pairs.append((value_hbm.at[:, lanes(g)], raw.at[0, g, :, pl.ds(HD, HD)]))
    loads = [pltpu.make_async_copy(pair[0], pair[1], load_sem.at[i]) for i, pair in enumerate(pairs)]
    own = lax.axis_index("tm")
    core = lax.rem(own, 2)

    def device(step):
        return {"tm": lax.rem(own + step + frames, frames)}

    partner = device(1 - 2 * core)
    ahead, behind = device(2), device(frames - 2)
    third = device(jnp.where(core == 0, frames - 3, frames - 1))
    second_to = device(jnp.where(core == 0, 1, 3))
    second_back = device(jnp.where(core == 0, frames - 3, frames - 1))

    barrier = pltpu.get_barrier_semaphore()
    for peer in (behind, third):
        pl.semaphore_signal(barrier, inc=1, device_id=peer, device_id_type=MESH)
    for load in loads:
        load.start()

    def remote(index, source, target, peer):
        return pltpu.make_async_remote_copy(
            src_ref=source, dst_ref=target, send_sem=send_sem.at[index], recv_sem=recv_sem.at[index],
            device_id=peer, device_id_type=MESH,
        )

    def outward(slot, role, g, peer):
        if g in STAGED:
            return (remote(slot, raw.at[0, g], raw.at[role, g], peer),)
        return (
            remote(slot, key_hbm.at[:, lanes(g)], raw.at[role, g, :, pl.ds(0, HD)], peer),
            remote(slot + 1, value_hbm.at[:, lanes(g)], raw.at[role, g, :, pl.ds(HD, HD)], peer),
        )

    send_two = [outward(2 * g, 2, g, ahead) for g in range(HK)]
    send_one = [outward(4 + 2 * g, 1, g, second_to) for g in range(HK)]
    relay = [remote(8 + g, raw.at[2, g], raw.at[3, g], partner) for g in range(HK)]
    inner = pl.ds(rim, tokens)
    back_relay = [remote(10 + g, grads.at[2, g, inner], arrived.at[2, g], partner) for g in range(HK)]
    back_two = [remote(12 + g, grads.at[1, g, inner], arrived.at[1, g], behind) for g in range(HK)]
    back_one = [remote(14 + g, grads.at[0, g, inner], arrived.at[0, g], second_back) for g in range(HK)]

    pl.semaphore_wait(barrier, 2)
    odd_last = lax.rem(own, 4) == 3
    for copy in send_two[0] + send_one[0]:
        copy.start()

    for load in loads[7:]:
        load.wait()

    @pl.when(jnp.logical_not(odd_last))
    def _():
        for copy in send_one[1]:
            copy.start()


    new_id = lax.broadcasted_iota(jnp.int32, (tokens, tokens), 0)
    old_id = lax.broadcasted_iota(jnp.int32, (tokens, tokens), 1)
    turn = jnp.where((new_id % rows) * width + new_id // rows == old_id, 1.0, 0.0).astype(jnp.bfloat16)

    def permuted(block):
        return jnp.dot(turn, block, preferred_element_type=jnp.float32).astype(jnp.bfloat16)

    for load in loads[:3]:
        load.wait()
    key_id = lax.broadcasted_iota(jnp.int32, (span, lane_count), 0)
    query_id = lax.broadcasted_iota(jnp.int32, (span, lane_count), 1) % tile
    delta_row = key_id % rows - query_id % rows
    delta_col = key_id // rows - REACH - query_id // rows
    code = jnp.where((delta_col >= -3) & (delta_col <= 3), delta_row * 8 + delta_col, 1000)

    def mark(index, hit):
        wanted = offset_ref[0, index] * 8 + offset_ref[1, index]
        return jnp.where(code == wanted, 0.0, hit)

    spatial = lax.fori_loop(
        0, offset_ref.shape[1], mark, jnp.full((span, lane_count), negative_big, jnp.float32), unroll=True
    )
    lags = (jnp.int32(0), jnp.where(core == 0, 3, 1), jnp.int32(2), jnp.where(core == 0, 1, 3))
    for role in range(4):
        allow = lag_allowed(mask_ref, clip_ref, own, frames, lags[role])
        shut = jnp.where(allow == 1, 0.0, negative_big).astype(jnp.float32)
        bias[1, role] = spatial + shut
        bias[0, role] = jnp.where(key_id < rim, negative_big, spatial) + shut
        bias[2, role] = jnp.where(key_id >= span - rim, negative_big, spatial) + shut

    blank = jnp.zeros((rim, 2 * HD), jnp.bfloat16)
    for role in range(4):
        for g in range(HK):
            keyed[g, role, pl.ds(0, rim)] = blank
            keyed[g, role, pl.ds(rim + tokens, rim)] = blank

    for load in loads[3:5]:
        load.wait()
    hole = jnp.zeros((tiles, lane_count, HD), jnp.bfloat16)
    for g in range(HK):
        mixed[g, :, pl.ds(0, lane_count), pl.ds(HD, HD)] = hole
        mixed[g, :, pl.ds(lane_count, lane_count), pl.ds(0, HD)] = hole
        for a in range(GROUP):
            h = g * GROUP + a
            mixed[g, :, pl.ds(a * tile, tile), pl.ds(0, HD)] = permuted(query_ref[:, lanes(h)]).reshape(
                tiles, tile, HD
            )
            mixed[g, :, pl.ds(lane_count + a * tile, tile), pl.ds(HD, HD)] = permuted(
                cot_ref[:, lanes(h)]
            ).reshape(tiles, tile, HD)

    def follow(first, then):
        for copy in first:
            copy.wait_send()
        for copy in then:
            copy.start()

    def place(role, g):
        keyed[g, role, pl.ds(rim, tokens)] = permuted(raw[role, g])

    for load in loads[5:7]:
        load.wait()
    for g in range(HK):
        place(0, g)

    def unit(g, j):
        first = pl.multiple_of(j * tile, tile)
        window = keyed[g, :, pl.ds(first, span), :].reshape(4 * span, 2 * HD)
        mix = mixed[g, j]
        both = lax.dot_general(window, mix, (((1,), (1,)), ((), ())), preferred_element_type=jnp.float32)
        variant = jnp.where(j == 0, 0, jnp.where(j == tiles - 1, 2, 1))
        logit = both[:, :lane_count] * (SCALE * LOG2E) + bias[variant].reshape(4 * span, lane_count)
        dot = both[:, lane_count:]
        top = jnp.max(logit, axis=0, keepdims=True)
        weight = jnp.exp2(logit - top)
        total = jnp.sum(weight, axis=0, keepdims=True)
        mean = jnp.sum(weight * dot, axis=0, keepdims=True) / total
        prob = weight * (1.0 / total)
        score = (prob * (dot - mean)).astype(jnp.bfloat16)
        scores_low[g, j] = score
        low = jnp.concatenate([score, prob.astype(jnp.bfloat16)], axis=1)
        part = jnp.dot(low, mix, preferred_element_type=jnp.float32).reshape(4, span, 2 * HD)
        begin = part[:, :tile] + held[...]
        held[...] = part[:, tile:]
        own_grads[g, pl.ds(first, tile)] = begin[0]
        grads[:, g, pl.ds(first, tile)] = begin[1:].astype(jnp.bfloat16)

    def queries_unit(g, j):
        first = pl.multiple_of(j * tile, tile)
        window = keyed[g, :, pl.ds(first, span), pl.ds(0, HD)].reshape(4 * span, HD)
        out = jnp.dot(scores_low[g, j].T, window, preferred_element_type=jnp.float32)
        for a in range(GROUP):
            dq_acc[g * GROUP + a, pl.ds(first, tile)] = out[a * tile : (a + 1) * tile]

    def receive(g):
        @pl.when(core == 1)
        def _():
            for copy in send_one[g]:
                copy.wait_recv()

        for copy in send_two[g]:
            copy.wait_recv()
        relay[g].start()
        place(2, g)

        @pl.when(core == 0)
        def _():
            for copy in send_one[g]:
                copy.wait_recv()

        place(1, g)
        relay[g].wait_recv()
        place(3, g)

    def work(g):
        held[...] = jnp.zeros_like(held)

        def step(j, _):
            unit(g, j)
            return 0

        lax.fori_loop(0, tiles, step, 0, unroll=UNROLL)
        end = pl.ds(tokens, span - tile)
        own_grads[g, end] = held[0]
        grads[:, g, end] = held[1:].astype(jnp.bfloat16)
        back_relay[g].start()
        back_one[g].start()

    def pass_two(g):
        back_relay[g].wait_recv()
        grads[1, g, inner] = (
            grads[1, g, inner].astype(jnp.float32) + arrived[2, g].astype(jnp.float32)
        ).astype(jnp.bfloat16)
        back_two[g].start()

    follow(send_two[0], send_two[1])

    @pl.when(odd_last)
    def _():
        follow((), send_one[1])

    follow(send_one[0], ())

    receive(0)
    work(0)
    pass_two(0)
    receive(1)
    work(1)
    pass_two(1)

    for g in range(HK):

        def turn_step(j, _, g=g):
            queries_unit(g, j)
            return 0

        lax.fori_loop(0, tiles, turn_step, 0, unroll=UNROLL)

    for h in range(HQ):
        for r in range(rows):
            dq_out[pl.ds(r * width, width), lanes(h)] = dq_acc[h, pl.ds(r, width, stride=rows), :] * SCALE

    for g in range(HK):
        back_one[g].wait_recv()
        back_two[g].wait_recv()
        came = arrived[0, g].astype(jnp.float32) + arrived[1, g].astype(jnp.float32) + own_grads[g, inner]
        final[0, g] = came[:, :HD] * SCALE
        final[1, g] = came[:, HD:]
        for r in range(rows):
            dkv_out[0, pl.ds(r * width, width), lanes(g)] = final[0, g, pl.ds(r, width, stride=rows), :]
            dkv_out[1, pl.ds(r * width, width), lanes(g)] = final[1, g, pl.ds(r, width, stride=rows), :]
    for copy in send_two[1] + send_one[1]:
        copy.wait_send()
    for g in range(HK):
        for copy in (relay[g], back_relay[g], back_two[g], back_one[g]):
            copy.wait_send()


UNROLL = 8
STAGED = (1,)
VL = 40 * 1024 * 1024


def fused_body(queries, keys, values, grad_out, frame_mask, clip_frames, offsets):
    _, rows, width, wide = queries.shape
    tokens = rows * width
    narrow = keys.shape[3]
    frames = lax.axis_size("tm")
    tiles = width // TILE
    tile = TILE * rows
    padded = tokens + 2 * REACH * rows
    span = tile + 2 * REACH * rows

    def flat(array):
        return array.reshape(tokens, array.shape[3])

    hbm = pl.BlockSpec(memory_space=pltpu.HBM)
    vmem = pl.BlockSpec(memory_space=pltpu.VMEM)

    def kernel(*refs):
        fused(width, frames, *refs)

    dq, dkv = pl.pallas_call(
        kernel,
        out_shape=(
            pltpu.VMEM((tokens, wide), jnp.float32),
            pltpu.VMEM((2, tokens, narrow), jnp.float32),
        ),
        in_specs=[hbm] * 7,
        out_specs=(vmem, vmem),
        scratch_shapes=[
            pltpu.SMEM(frame_mask.shape, jnp.int32),
            pltpu.SMEM(clip_frames.shape, jnp.int32),
            pltpu.SMEM(offsets.shape[::-1], jnp.int32),
            pltpu.VMEM((tokens, wide), jnp.bfloat16),
            pltpu.VMEM((tokens, wide), jnp.bfloat16),
            pltpu.VMEM((4, HK, tokens, 2 * HD), jnp.bfloat16),
            pltpu.VMEM((HK, 4, padded, 2 * HD), jnp.bfloat16),
            pltpu.VMEM((HK, tiles, 2 * GROUP * tile, 2 * HD), jnp.bfloat16),
            pltpu.VMEM((3, 4, span, GROUP * tile), jnp.float32),
            pltpu.VMEM((4, span - tile, 2 * HD), jnp.float32),
            pltpu.VMEM((HK, padded, 2 * HD), jnp.float32),
            pltpu.VMEM((3, HK, padded, 2 * HD), jnp.bfloat16),
            pltpu.VMEM((3, HK, tokens, 2 * HD), jnp.bfloat16),
            pltpu.VMEM((HK, tiles, 4 * span, GROUP * tile), jnp.bfloat16),
            pltpu.VMEM((HQ, tokens, HD), jnp.float32),
            pltpu.VMEM((2, HK, tokens, HD), jnp.float32),
            pltpu.SemaphoreType.DMA((9,)),
            pltpu.SemaphoreType.DMA((16,)),
            pltpu.SemaphoreType.DMA((16,)),
        ],
        compiler_params=pltpu.CompilerParams(
            collective_id=0, has_side_effects=True, vmem_limit_bytes=VL
        ),
    )(*[
        pltpu.with_memory_space_constraint(operand, pltpu.HBM)
        for operand in (
            frame_mask, clip_frames, offsets.T, flat(queries), flat(keys), flat(values), flat(grad_out)
        )
    ])
    def ship(dq_ref, dkv_ref, dq_out, dk_out, dv_out, sem):
        pairs = ((dq_ref, dq_out), (dkv_ref.at[0], dk_out), (dkv_ref.at[1], dv_out))
        copies = [pltpu.make_async_copy(pair[0], pair[1], sem.at[i]) for i, pair in enumerate(pairs)]
        for copy in copies:
            copy.start()
        for copy in copies:
            copy.wait()

    dq, dk, dv = pl.pallas_call(
        ship,
        out_shape=(
            jax.ShapeDtypeStruct((tokens, wide), jnp.float32),
            jax.ShapeDtypeStruct((tokens, narrow), jnp.float32),
            jax.ShapeDtypeStruct((tokens, narrow), jnp.float32),
        ),
        in_specs=[vmem] * 2,
        out_specs=[hbm] * 3,
        scratch_shapes=[pltpu.SemaphoreType.DMA((3,))],
        compiler_params=pltpu.CompilerParams(vmem_limit_bytes=4 * 1024 * 1024),
        name="ship",
    )(*[pltpu.with_memory_space_constraint(part, pltpu.VMEM) for part in (dq, dkv)])
    shape = (1, rows, width)
    return dq.reshape(shape + (wide,)), dk.reshape(shape + (narrow,)), dv.reshape(shape + (narrow,))


def solution(mesh):
    whole_rows = mesh.shape["rows"] == 1 and mesh.shape["tm"] % 2 == 0 and mesh.shape["tm"] > 6
    return jax.shard_map(
        fused_body if whole_rows else body,
        mesh=mesh,
        in_specs=(
            P(("groups", "tm"), "rows", None, None),
            P(("groups", "tm"), "rows", None, None),
            P(("groups", "tm"), "rows", None, None),
            P(("groups", "tm"), "rows", None, None),
            P("groups", None),
            P("groups"),
            P(),
        ),
        out_specs=(
            P(("groups", "tm"), "rows", None, None),
            P(("groups", "tm"), "rows", None, None),
            P(("groups", "tm"), "rows", None, None),
        ),
        check_vma=False,
    )
```

```python
import jax
import jax.numpy as jnp
from jax import lax
from jax.experimental import pallas as pl
from jax.experimental.pallas import tpu as pltpu
from jax.sharding import PartitionSpec as P

HQ = 8
HK = 2
HD = 128


tile_cols = 8
key_span = 14
negative_big = -1e30


def padded_2(cells, sides, width):
    for axis, dim in sides:
        count = lax.axis_size(axis)
        ends = count - 1
        head = lax.slice_in_dim(cells, 0, width, axis=dim)
        tail = lax.slice_in_dim(cells, cells.shape[dim] - width, cells.shape[dim], axis=dim)
        cells = jnp.concatenate(
            [
                lax.ppermute(tail, axis, [(i, (i + 1) % count) for i in range(ends)]),
                cells,
                lax.ppermute(head, axis, [((i + 1) % count, i) for i in range(ends)]),
            ],
            axis=dim,
        )
    return cells


def passed_along(value, axis, steps):
    count = lax.axis_size(axis)
    pairs = [(source, (source + steps) % count) for source in range(count)]
    return lax.ppermute(value, axis, pairs)


def to_tiles(block, group_size):
    band_rows = block.shape[0]
    count_tiles = block.shape[1] // tile_cols
    shaped = block.reshape(band_rows, count_tiles, tile_cols, HK, group_size, HD)
    shaped = shaped.transpose(1, 3, 4, 0, 2, 5)
    return shaped.reshape(count_tiles, HK, group_size, band_rows * tile_cols, HD)


def from_tiles(tiles, band_rows):
    count_tiles = tiles.shape[0]
    group_size = tiles.shape[2]
    shaped = tiles.reshape(count_tiles, HK, group_size, band_rows, tile_cols, HD)
    shaped = shaped.transpose(3, 0, 4, 1, 2, 5)
    return shaped.reshape(1, band_rows, count_tiles * tile_cols, HK * group_size * HD)


def to_windows(extended):
    ext_rows = extended.shape[1]
    total_width = extended.shape[2]
    padded = jnp.pad(extended, ((0, 0), (0, 0), (3, 3), (0, 0)))
    pieces = [
        padded[:, :, column_tile * tile_cols : column_tile * tile_cols + key_span]
        for column_tile in range(total_width // tile_cols)
    ]
    stacked = jnp.stack(pieces, 0)
    stacked = stacked.reshape(len(pieces), 2, ext_rows, key_span, HK, HD)
    stacked = stacked.transpose(1, 0, 4, 2, 3, 5)
    return stacked.reshape(2, len(pieces), HK, ext_rows * key_span, HD)


def from_windows(window_grads, ext_rows, total_width):
    count_tiles = window_grads.shape[1]
    shaped = window_grads.reshape(2, count_tiles, HK, ext_rows, key_span, HD)
    shaped = shaped.transpose(0, 1, 3, 4, 2, 5).reshape(2, count_tiles, ext_rows, key_span, HK * HD)
    summed = jnp.zeros((2, ext_rows, total_width + 6, HK * HD), jnp.float32)
    for column_tile in range(count_tiles):
        first_col = column_tile * tile_cols
        summed = summed.at[:, :, first_col : first_col + key_span].add(shaped[:, column_tile])
    return summed[:, :, 3 : 3 + total_width]


def spatial_live(offsets, band_rows, total_width):
    ext_rows = band_rows + 6
    count_tiles = total_width // tile_cols
    query_row = jnp.repeat(jnp.arange(band_rows), tile_cols)
    query_col = jnp.tile(jnp.arange(tile_cols), band_rows)
    key_row = jnp.repeat(jnp.arange(ext_rows), key_span)
    key_col = jnp.tile(jnp.arange(key_span), ext_rows)
    delta_row = key_row[None, :] - 3 - query_row[:, None]
    delta_col = key_col[None, :] - 3 - query_col[:, None]
    offset_hit = jnp.any(
        (delta_row[None] == offsets[:, 0, None, None])
        & (delta_col[None] == offsets[:, 1, None, None]),
        axis=0,
    )
    band_index = lax.axis_index("rows")
    image_rows = band_rows * lax.axis_size("rows")
    image_row = band_index * band_rows + key_row - 3
    row_inside = (image_row >= 0) & (image_row < image_rows)
    tile_first = jnp.arange(count_tiles) * tile_cols
    image_col = tile_first[:, None] + key_col[None, :] - 3
    col_inside = (image_col >= 0) & (image_col < total_width)
    return offset_hit[None] & row_inside[None, None] & col_inside[:, None, :]


def running_sum(entries):
    places = jnp.arange(entries.shape[0])
    return jnp.sum(jnp.where(places[None, :] <= places[:, None], entries[None, :], 0), axis=1)


def frame_allowed(frame_mask, clip_frames, distance):
    frames = lax.axis_size("tm")
    lags = min(4, frames)
    own_frame = lax.axis_index("tm")
    seen_frame = (own_frame - distance) % frames
    clip_ends = running_sum(clip_frames)
    clip_starts = clip_ends - clip_frames
    is_longest = (clip_frames == lags).astype(jnp.int32)
    first_longest = (is_longest == 1) & (running_sum(is_longest) == 1)
    rotation = jnp.sum(jnp.where(first_longest, clip_starts, 0))
    own_place = (own_frame + 2 + rotation) % frames
    seen_place = (seen_frame + 2 + rotation) % frames
    own_clip = jnp.sum((own_place >= clip_ends).astype(jnp.int32))
    seen_clip = jnp.sum((seen_place >= clip_ends).astype(jnp.int32))
    grid_rows = jnp.arange(frames)[:, None]
    grid_cols = jnp.arange(frames)[None, :]
    picked = jnp.sum(jnp.where((grid_rows == own_frame) & (grid_cols == seen_frame), frame_mask, 0))
    kept = (picked == 1) | (distance <= 1)
    return (own_clip == seen_clip) & (seen_place <= own_place) & kept


def fold_rims(extended_grads, band_rows):
    interior = extended_grads[:, 3 : 3 + band_rows]
    rim_rows = jnp.concatenate([extended_grads[:, :3], extended_grads[:, band_rows + 3 :]], 1)
    haloed = padded_2(rim_rows.astype(jnp.bfloat16), (("rows", 1),), 3).astype(rim_rows.dtype)
    interior = interior.at[:, :3].add(haloed[:, :3])
    return interior.at[:, band_rows - 3 :].add(haloed[:, 9:])


def body(queries, keys, values, grad_out, frame_mask, clip_frames, offsets):
    band_rows = queries.shape[1]
    total_width = queries.shape[2]
    ext_rows = band_rows + 6
    group_size = HQ // HK
    scale = HD ** (-0.5)
    lags = min(4, lax.axis_size("tm"))
    query_tiles = to_tiles(queries[0], group_size)
    grad_tiles = to_tiles(grad_out[0], group_size)
    spatial = spatial_live(offsets, band_rows, total_width)[:, None, None]
    allowed = [frame_allowed(frame_mask, clip_frames, distance) for distance in range(lags)]
    stacked = jnp.stack([keys[0], values[0]], 0)
    resident = padded_2(stacked, (("rows", 1),), 3)

    def pair_terms(extended):
        windows = to_windows(extended)
        logits = (
            jnp.einsum(
                "cgaqd,cgkd->cgaqk", query_tiles, windows[0], preferred_element_type=jnp.float32
            )
            * scale
        )
        grad_dot = jnp.einsum(
            "cgaqd,cgkd->cgaqk", grad_tiles, windows[1], preferred_element_type=jnp.float32
        )
        return (windows, logits, grad_dot)

    stat_shape = (total_width // tile_cols, HK, group_size, band_rows * tile_cols)
    running = (
        jnp.full(stat_shape, negative_big, jnp.float32),
        jnp.zeros(stat_shape, jnp.float32),
        jnp.zeros(stat_shape, jnp.float32),
    )
    visiting = resident
    visited = []
    for distance in range(lags):
        visited.append(visiting)
        extended = visiting
        live_mask = spatial & allowed[distance]
        run_max, run_sum, run_dot = running
        stat_windows, stat_logits, stat_grad_dot = pair_terms(extended)
        masked = jnp.where(live_mask, stat_logits, negative_big)
        new_max = jnp.maximum(run_max, jnp.max(masked, axis=-1))
        factor = jnp.exp(run_max - new_max)
        weights = jnp.where(live_mask, jnp.exp(stat_logits - new_max[..., None]), 0.0)
        running = (
            new_max,
            run_sum * factor + jnp.sum(weights, axis=-1),
            run_dot * factor + jnp.sum(weights * stat_grad_dot, axis=-1),
        )
        if distance + 1 < lags:
            visiting = passed_along(visiting, "tm", 1)
    log_total = running[0] + jnp.log(running[1])
    mean_grad = running[2] / running[1]
    query_total = jnp.zeros(stat_shape + (HD,), jnp.float32)
    carried = jnp.zeros(resident.shape, jnp.float32)
    visiting = resident
    for distance in range(lags):
        extended = visiting
        live_mask = spatial & allowed[distance]
        grad_windows, grad_logits, grad_grad_dot = pair_terms(extended)
        probs = jnp.where(live_mask, jnp.exp(grad_logits - log_total[..., None]), 0.0)
        probs_low = probs.astype(jnp.bfloat16)
        dscore = (probs * (grad_grad_dot - mean_grad[..., None])).astype(jnp.bfloat16)
        query_part = jnp.einsum(
            "cgaqk,cgkd->cgaqd", dscore, grad_windows[0], preferred_element_type=jnp.float32
        )
        key_part = (
            jnp.einsum("cgaqk,cgaqd->cgkd", dscore, query_tiles, preferred_element_type=jnp.float32)
            * scale
        )
        value_part = jnp.einsum(
            "cgaqk,cgaqd->cgkd", probs_low, grad_tiles, preferred_element_type=jnp.float32
        )
        query_part, window_grads = (query_part, jnp.stack([key_part, value_part], 0))
        query_total = query_total + query_part
        ext_grads = from_windows(window_grads, ext_rows, total_width)
        carried = carried + ext_grads
        if distance + 1 < lags:
            visiting = passed_along(visiting, "tm", 1)
            carried = passed_along(carried, "tm", 1)
    carried = passed_along(carried, "tm", 1 - lags)
    finished = fold_rims(carried, band_rows)
    grad_queries = from_tiles(query_total * scale, band_rows)
    return (grad_queries, finished[0][None], finished[1][None])


MESH = pl.DeviceIdType.MESH
LOG2E = 1.4426950408889634
SCALE = HD**-0.5
GROUP = HQ // HK


def lag_allowed(mask_ref, clip_ref, own_frame, frames, lag):
    clips = clip_ref.shape[0]
    seen_frame = lax.rem(own_frame - lag + frames, frames)
    total = jnp.int32(0)
    rotation = jnp.int32(0)
    found = jnp.int32(0)
    for clip in range(clips):
        length = clip_ref[clip]
        first = jnp.where(length == 4, 1, 0) * (1 - found)
        rotation = rotation + first * total
        found = found + first
        total = total + length
    own_place = own_frame + 2 + rotation
    own_place = jnp.where(own_place >= frames, own_place - frames, own_place)
    own_place = jnp.where(own_place >= frames, own_place - frames, own_place)
    seen_place = seen_frame + 2 + rotation
    seen_place = jnp.where(seen_place >= frames, seen_place - frames, seen_place)
    seen_place = jnp.where(seen_place >= frames, seen_place - frames, seen_place)
    own_clip = jnp.int32(0)
    seen_clip = jnp.int32(0)
    end = jnp.int32(0)
    for clip in range(clips):
        end = end + clip_ref[clip]
        own_clip = own_clip + jnp.where(own_place >= end, 1, 0)
        seen_clip = seen_clip + jnp.where(seen_place >= end, 1, 0)
    kept = jnp.maximum(jnp.where(mask_ref[own_frame, seen_frame] == 1, 1, 0), jnp.where(lag <= 1, 1, 0))
    same = jnp.where(own_clip == seen_clip, 1, 0)
    causal = jnp.where(seen_place <= own_place, 1, 0)
    return kept * same * causal


TILE = 8
REACH = 4


def fused(
    width, frames,
    mask_hbm, clip_hbm, offset_hbm, query_hbm, key_hbm, value_hbm, cot_hbm,
    dq_out, dkv_out,
    mask_ref, clip_ref, offset_ref, query_ref, cot_ref, raw, keyed, mixed, bias, held, own_grads, grads, arrived,
    scores_low, dq_acc, final, load_sem, send_sem, recv_sem,
):
    tokens = query_ref.shape[0]
    rows = tokens // width
    tiles = width // TILE
    tile = TILE * rows
    rim = REACH * rows
    span = tile + 2 * rim
    lane_count = GROUP * tile

    def lanes(index):
        return pl.ds(pl.multiple_of(index * HD, HD), HD)

    pairs = [
        (offset_hbm, offset_ref),
        (clip_hbm, clip_ref),
        (mask_hbm, mask_ref),
        (query_hbm, query_ref),
        (cot_hbm, cot_ref),
    ]
    for g in range(HK):
        pairs.append((key_hbm.at[:, lanes(g)], raw.at[0, g, :, pl.ds(0, HD)]))
        pairs.append((value_hbm.at[:, lanes(g)], raw.at[0, g, :, pl.ds(HD, HD)]))
    loads = [pltpu.make_async_copy(pair[0], pair[1], load_sem.at[i]) for i, pair in enumerate(pairs)]
    own = lax.axis_index("tm")
    core = lax.rem(own, 2)

    def device(step):
        return {"tm": lax.rem(own + step + frames, frames)}

    partner = device(1 - 2 * core)
    ahead, behind = device(2), device(frames - 2)
    third = device(jnp.where(core == 0, frames - 3, frames - 1))
    second_to = device(jnp.where(core == 0, 1, 3))
    second_back = device(jnp.where(core == 0, frames - 3, frames - 1))

    barrier = pltpu.get_barrier_semaphore()
    for peer in (behind, third):
        pl.semaphore_signal(barrier, inc=1, device_id=peer, device_id_type=MESH)

    def remote(index, source, target, peer):
        return pltpu.make_async_remote_copy(
            src_ref=source, dst_ref=target, send_sem=send_sem.at[index], recv_sem=recv_sem.at[index],
            device_id=peer, device_id_type=MESH,
        )

    def outward(slot, role, g, peer):
        if g in STAGED:
            return (remote(slot, raw.at[0, g], raw.at[role, g], peer),)
        return (
            remote(slot, key_hbm.at[:, lanes(g)], raw.at[role, g, :, pl.ds(0, HD)], peer),
            remote(slot + 1, value_hbm.at[:, lanes(g)], raw.at[role, g, :, pl.ds(HD, HD)], peer),
        )

    send_two = [outward(2 * g, 2, g, ahead) for g in range(HK)]
    send_one = [outward(4 + 2 * g, 1, g, second_to) for g in range(HK)]
    relay = [remote(8 + g, raw.at[2, g], raw.at[3, g], partner) for g in range(HK)]
    inner = pl.ds(rim, tokens)
    back_relay = [remote(10 + g, grads.at[2, g, inner], arrived.at[2, g], partner) for g in range(HK)]
    back_two = [remote(12 + g, grads.at[1, g, inner], arrived.at[1, g], behind) for g in range(HK)]
    back_one = [remote(14 + g, grads.at[0, g, inner], arrived.at[0, g], second_back) for g in range(HK)]

    pl.semaphore_wait(barrier, 2)
    odd_last = lax.rem(own, 4) == 3
    for copy in send_two[0] + send_one[0]:
        copy.start()
    for load in loads[7:] + loads[:7]:
        load.start()

    for load in loads[7:]:
        load.wait()

    @pl.when(jnp.logical_not(odd_last))
    def _():
        for copy in send_one[1]:
            copy.start()


    new_id = lax.broadcasted_iota(jnp.int32, (tokens, tokens), 0)
    old_id = lax.broadcasted_iota(jnp.int32, (tokens, tokens), 1)
    turn = jnp.where((new_id % rows) * width + new_id // rows == old_id, 1.0, 0.0).astype(jnp.bfloat16)

    def permuted(block):
        return jnp.dot(turn, block, preferred_element_type=jnp.float32).astype(jnp.bfloat16)

    for load in loads[:3]:
        load.wait()
    key_id = lax.broadcasted_iota(jnp.int32, (span, lane_count), 0)
    query_id = lax.broadcasted_iota(jnp.int32, (span, lane_count), 1) % tile
    delta_row = key_id % rows - query_id % rows
    delta_col = key_id // rows - REACH - query_id // rows
    code = jnp.where((delta_col >= -3) & (delta_col <= 3), delta_row * 8 + delta_col, 1000)

    def mark(index, hit):
        wanted = offset_ref[0, index] * 8 + offset_ref[1, index]
        return jnp.where(code == wanted, 0.0, hit)

    spatial = lax.fori_loop(
        0, offset_ref.shape[1], mark, jnp.full((span, lane_count), negative_big, jnp.float32), unroll=True
    )
    lags = (jnp.int32(0), jnp.where(core == 0, 3, 1), jnp.int32(2), jnp.where(core == 0, 1, 3))
    for role in range(4):
        allow = lag_allowed(mask_ref, clip_ref, own, frames, lags[role])
        shut = jnp.where(allow == 1, 0.0, negative_big).astype(jnp.float32)
        bias[1, role] = spatial + shut
        bias[0, role] = jnp.where(key_id < rim, negative_big, spatial) + shut
        bias[2, role] = jnp.where(key_id >= span - rim, negative_big, spatial) + shut

    blank = jnp.zeros((rim, 2 * HD), jnp.bfloat16)
    for role in range(4):
        for g in range(HK):
            keyed[g, role, pl.ds(0, rim)] = blank
            keyed[g, role, pl.ds(rim + tokens, rim)] = blank

    for load in loads[3:5]:
        load.wait()
    hole = jnp.zeros((tiles, lane_count, HD), jnp.bfloat16)
    for g in range(HK):
        mixed[g, :, pl.ds(0, lane_count), pl.ds(HD, HD)] = hole
        mixed[g, :, pl.ds(lane_count, lane_count), pl.ds(0, HD)] = hole
        for a in range(GROUP):
            h = g * GROUP + a
            mixed[g, :, pl.ds(a * tile, tile), pl.ds(0, HD)] = permuted(query_ref[:, lanes(h)]).reshape(
                tiles, tile, HD
            )
            mixed[g, :, pl.ds(lane_count + a * tile, tile), pl.ds(HD, HD)] = permuted(
                cot_ref[:, lanes(h)]
            ).reshape(tiles, tile, HD)

    def follow(first, then):
        for copy in first:
            copy.wait_send()
        for copy in then:
            copy.start()

    def place(role, g):
        keyed[g, role, pl.ds(rim, tokens)] = permuted(raw[role, g])

    for load in loads[5:7]:
        load.wait()
    for g in range(HK):
        place(0, g)

    def unit(g, j):
        first = pl.multiple_of(j * tile, tile)
        window = keyed[g, :, pl.ds(first, span), :].reshape(4 * span, 2 * HD)
        mix = mixed[g, j]
        both = lax.dot_general(window, mix, (((1,), (1,)), ((), ())), preferred_element_type=jnp.float32)
        variant = jnp.where(j == 0, 0, jnp.where(j == tiles - 1, 2, 1))
        logit = both[:, :lane_count] * (SCALE * LOG2E) + bias[variant].reshape(4 * span, lane_count)
        dot = both[:, lane_count:]
        top = jnp.max(logit, axis=0, keepdims=True)
        weight = jnp.exp2(logit - top)
        total = jnp.sum(weight, axis=0, keepdims=True)
        mean = jnp.sum(weight * dot, axis=0, keepdims=True) / total
        prob = weight * (1.0 / total)
        score = (prob * (dot - mean)).astype(jnp.bfloat16)
        scores_low[g, j] = score
        low = jnp.concatenate([score, prob.astype(jnp.bfloat16)], axis=1)
        part = jnp.dot(low, mix, preferred_element_type=jnp.float32).reshape(4, span, 2 * HD)
        begin = part[:, :tile] + held[...]
        held[...] = part[:, tile:]
        own_grads[g, pl.ds(first, tile)] = begin[0]
        grads[:, g, pl.ds(first, tile)] = begin[1:].astype(jnp.bfloat16)

    def queries_unit(g, j):
        first = pl.multiple_of(j * tile, tile)
        window = keyed[g, :, pl.ds(first, span), pl.ds(0, HD)].reshape(4 * span, HD)
        out = jnp.dot(scores_low[g, j].T, window, preferred_element_type=jnp.float32)
        for a in range(GROUP):
            dq_acc[g * GROUP + a, pl.ds(first, tile)] = out[a * tile : (a + 1) * tile]

    def receive(g):
        @pl.when(core == 1)
        def _():
            for copy in send_one[g]:
                copy.wait_recv()

        for copy in send_two[g]:
            copy.wait_recv()
        relay[g].start()
        place(2, g)

        @pl.when(core == 0)
        def _():
            for copy in send_one[g]:
                copy.wait_recv()

        place(1, g)
        relay[g].wait_recv()
        place(3, g)

    def work(g):
        held[...] = jnp.zeros_like(held)

        def step(j, _):
            unit(g, j)
            return 0

        lax.fori_loop(0, tiles, step, 0, unroll=UNROLL)
        end = pl.ds(tokens, span - tile)
        own_grads[g, end] = held[0]
        grads[:, g, end] = held[1:].astype(jnp.bfloat16)
        back_relay[g].start()
        back_one[g].start()

    def pass_two(g):
        back_relay[g].wait_recv()
        grads[1, g, inner] = (
            grads[1, g, inner].astype(jnp.float32) + arrived[2, g].astype(jnp.float32)
        ).astype(jnp.bfloat16)
        back_two[g].start()

    follow(send_two[0], send_two[1])

    @pl.when(odd_last)
    def _():
        follow((), send_one[1])

    follow(send_one[0], ())

    receive(0)
    work(0)
    pass_two(0)
    receive(1)
    work(1)
    pass_two(1)

    for g in range(HK):

        def turn_step(j, _, g=g):
            queries_unit(g, j)
            return 0

        lax.fori_loop(0, tiles, turn_step, 0, unroll=UNROLL)

    for h in range(HQ):
        for r in range(rows):
            dq_out[pl.ds(r * width, width), lanes(h)] = dq_acc[h, pl.ds(r, width, stride=rows), :] * SCALE

    for g in range(HK):
        back_one[g].wait_recv()
        back_two[g].wait_recv()
        came = arrived[0, g].astype(jnp.float32) + arrived[1, g].astype(jnp.float32) + own_grads[g, inner]
        final[0, g] = came[:, :HD] * SCALE
        final[1, g] = came[:, HD:]
        for r in range(rows):
            dkv_out[0, pl.ds(r * width, width), lanes(g)] = final[0, g, pl.ds(r, width, stride=rows), :]
            dkv_out[1, pl.ds(r * width, width), lanes(g)] = final[1, g, pl.ds(r, width, stride=rows), :]
    for copy in send_two[1] + send_one[1]:
        copy.wait_send()
    for g in range(HK):
        for copy in (relay[g], back_relay[g], back_two[g], back_one[g]):
            copy.wait_send()


UNROLL = 8
STAGED = (1,)
VL = 40 * 1024 * 1024


def fused_body(queries, keys, values, grad_out, frame_mask, clip_frames, offsets):
    _, rows, width, wide = queries.shape
    tokens = rows * width
    narrow = keys.shape[3]
    frames = lax.axis_size("tm")
    tiles = width // TILE
    tile = TILE * rows
    padded = tokens + 2 * REACH * rows
    span = tile + 2 * REACH * rows

    def flat(array):
        return array.reshape(tokens, array.shape[3])

    hbm = pl.BlockSpec(memory_space=pltpu.HBM)
    vmem = pl.BlockSpec(memory_space=pltpu.VMEM)

    def kernel(*refs):
        fused(width, frames, *refs)

    dq, dkv = pl.pallas_call(
        kernel,
        out_shape=(
            pltpu.VMEM((tokens, wide), jnp.float32),
            pltpu.VMEM((2, tokens, narrow), jnp.float32),
        ),
        in_specs=[hbm] * 7,
        out_specs=(vmem, vmem),
        scratch_shapes=[
            pltpu.SMEM(frame_mask.shape, jnp.int32),
            pltpu.SMEM(clip_frames.shape, jnp.int32),
            pltpu.SMEM(offsets.shape[::-1], jnp.int32),
            pltpu.VMEM((tokens, wide), jnp.bfloat16),
            pltpu.VMEM((tokens, wide), jnp.bfloat16),
            pltpu.VMEM((4, HK, tokens, 2 * HD), jnp.bfloat16),
            pltpu.VMEM((HK, 4, padded, 2 * HD), jnp.bfloat16),
            pltpu.VMEM((HK, tiles, 2 * GROUP * tile, 2 * HD), jnp.bfloat16),
            pltpu.VMEM((3, 4, span, GROUP * tile), jnp.float32),
            pltpu.VMEM((4, span - tile, 2 * HD), jnp.float32),
            pltpu.VMEM((HK, padded, 2 * HD), jnp.float32),
            pltpu.VMEM((3, HK, padded, 2 * HD), jnp.bfloat16),
            pltpu.VMEM((3, HK, tokens, 2 * HD), jnp.bfloat16),
            pltpu.VMEM((HK, tiles, 4 * span, GROUP * tile), jnp.bfloat16),
            pltpu.VMEM((HQ, tokens, HD), jnp.float32),
            pltpu.VMEM((2, HK, tokens, HD), jnp.float32),
            pltpu.SemaphoreType.DMA((9,)),
            pltpu.SemaphoreType.DMA((16,)),
            pltpu.SemaphoreType.DMA((16,)),
        ],
        compiler_params=pltpu.CompilerParams(
            collective_id=0, has_side_effects=True, vmem_limit_bytes=VL
        ),
    )(*[
        pltpu.with_memory_space_constraint(operand, pltpu.HBM)
        for operand in (
            frame_mask, clip_frames, offsets.T, flat(queries), flat(keys), flat(values), flat(grad_out)
        )
    ])
    def ship(dq_ref, dkv_ref, dq_out, dk_out, dv_out, sem):
        pairs = ((dq_ref, dq_out), (dkv_ref.at[0], dk_out), (dkv_ref.at[1], dv_out))
        copies = [pltpu.make_async_copy(pair[0], pair[1], sem.at[i]) for i, pair in enumerate(pairs)]
        for copy in copies:
            copy.start()
        for copy in copies:
            copy.wait()

    dq, dk, dv = pl.pallas_call(
        ship,
        out_shape=(
            jax.ShapeDtypeStruct((tokens, wide), jnp.float32),
            jax.ShapeDtypeStruct((tokens, narrow), jnp.float32),
            jax.ShapeDtypeStruct((tokens, narrow), jnp.float32),
        ),
        in_specs=[vmem] * 2,
        out_specs=[hbm] * 3,
        scratch_shapes=[pltpu.SemaphoreType.DMA((3,))],
        compiler_params=pltpu.CompilerParams(vmem_limit_bytes=4 * 1024 * 1024),
        name="ship",
    )(*[pltpu.with_memory_space_constraint(part, pltpu.VMEM) for part in (dq, dkv)])
    shape = (1, rows, width)
    return dq.reshape(shape + (wide,)), dk.reshape(shape + (narrow,)), dv.reshape(shape + (narrow,))


def solution(mesh):
    whole_rows = mesh.shape["rows"] == 1 and mesh.shape["tm"] % 2 == 0 and mesh.shape["tm"] > 6
    return jax.shard_map(
        fused_body if whole_rows else body,
        mesh=mesh,
        in_specs=(
            P(("groups", "tm"), "rows", None, None),
            P(("groups", "tm"), "rows", None, None),
            P(("groups", "tm"), "rows", None, None),
            P(("groups", "tm"), "rows", None, None),
            P("groups", None),
            P("groups"),
            P(),
        ),
        out_specs=(
            P(("groups", "tm"), "rows", None, None),
            P(("groups", "tm"), "rows", None, None),
            P(("groups", "tm"), "rows", None, None),
        ),
        check_vma=False,
    )
```

```python
import jax
import jax.numpy as jnp
from jax import lax
from jax.experimental import pallas as pl
from jax.experimental.pallas import tpu as pltpu
from jax.sharding import PartitionSpec as P

HQ = 8
HK = 2
HD = 128


tile_cols = 8
key_span = 14
negative_big = -1e30


def padded_2(cells, sides, width):
    for axis, dim in sides:
        count = lax.axis_size(axis)
        ends = count - 1
        head = lax.slice_in_dim(cells, 0, width, axis=dim)
        tail = lax.slice_in_dim(cells, cells.shape[dim] - width, cells.shape[dim], axis=dim)
        cells = jnp.concatenate(
            [
                lax.ppermute(tail, axis, [(i, (i + 1) % count) for i in range(ends)]),
                cells,
                lax.ppermute(head, axis, [((i + 1) % count, i) for i in range(ends)]),
            ],
            axis=dim,
        )
    return cells


def passed_along(value, axis, steps):
    count = lax.axis_size(axis)
    pairs = [(source, (source + steps) % count) for source in range(count)]
    return lax.ppermute(value, axis, pairs)


def to_tiles(block, group_size):
    band_rows = block.shape[0]
    count_tiles = block.shape[1] // tile_cols
    shaped = block.reshape(band_rows, count_tiles, tile_cols, HK, group_size, HD)
    shaped = shaped.transpose(1, 3, 4, 0, 2, 5)
    return shaped.reshape(count_tiles, HK, group_size, band_rows * tile_cols, HD)


def from_tiles(tiles, band_rows):
    count_tiles = tiles.shape[0]
    group_size = tiles.shape[2]
    shaped = tiles.reshape(count_tiles, HK, group_size, band_rows, tile_cols, HD)
    shaped = shaped.transpose(3, 0, 4, 1, 2, 5)
    return shaped.reshape(1, band_rows, count_tiles * tile_cols, HK * group_size * HD)


def to_windows(extended):
    ext_rows = extended.shape[1]
    total_width = extended.shape[2]
    padded = jnp.pad(extended, ((0, 0), (0, 0), (3, 3), (0, 0)))
    pieces = [
        padded[:, :, column_tile * tile_cols : column_tile * tile_cols + key_span]
        for column_tile in range(total_width // tile_cols)
    ]
    stacked = jnp.stack(pieces, 0)
    stacked = stacked.reshape(len(pieces), 2, ext_rows, key_span, HK, HD)
    stacked = stacked.transpose(1, 0, 4, 2, 3, 5)
    return stacked.reshape(2, len(pieces), HK, ext_rows * key_span, HD)


def from_windows(window_grads, ext_rows, total_width):
    count_tiles = window_grads.shape[1]
    shaped = window_grads.reshape(2, count_tiles, HK, ext_rows, key_span, HD)
    shaped = shaped.transpose(0, 1, 3, 4, 2, 5).reshape(2, count_tiles, ext_rows, key_span, HK * HD)
    summed = jnp.zeros((2, ext_rows, total_width + 6, HK * HD), jnp.float32)
    for column_tile in range(count_tiles):
        first_col = column_tile * tile_cols
        summed = summed.at[:, :, first_col : first_col + key_span].add(shaped[:, column_tile])
    return summed[:, :, 3 : 3 + total_width]


def spatial_live(offsets, band_rows, total_width):
    ext_rows = band_rows + 6
    count_tiles = total_width // tile_cols
    query_row = jnp.repeat(jnp.arange(band_rows), tile_cols)
    query_col = jnp.tile(jnp.arange(tile_cols), band_rows)
    key_row = jnp.repeat(jnp.arange(ext_rows), key_span)
    key_col = jnp.tile(jnp.arange(key_span), ext_rows)
    delta_row = key_row[None, :] - 3 - query_row[:, None]
    delta_col = key_col[None, :] - 3 - query_col[:, None]
    offset_hit = jnp.any(
        (delta_row[None] == offsets[:, 0, None, None])
        & (delta_col[None] == offsets[:, 1, None, None]),
        axis=0,
    )
    band_index = lax.axis_index("rows")
    image_rows = band_rows * lax.axis_size("rows")
    image_row = band_index * band_rows + key_row - 3
    row_inside = (image_row >= 0) & (image_row < image_rows)
    tile_first = jnp.arange(count_tiles) * tile_cols
    image_col = tile_first[:, None] + key_col[None, :] - 3
    col_inside = (image_col >= 0) & (image_col < total_width)
    return offset_hit[None] & row_inside[None, None] & col_inside[:, None, :]


def running_sum(entries):
    places = jnp.arange(entries.shape[0])
    return jnp.sum(jnp.where(places[None, :] <= places[:, None], entries[None, :], 0), axis=1)


def frame_allowed(frame_mask, clip_frames, distance):
    frames = lax.axis_size("tm")
    lags = min(4, frames)
    own_frame = lax.axis_index("tm")
    seen_frame = (own_frame - distance) % frames
    clip_ends = running_sum(clip_frames)
    clip_starts = clip_ends - clip_frames
    is_longest = (clip_frames == lags).astype(jnp.int32)
    first_longest = (is_longest == 1) & (running_sum(is_longest) == 1)
    rotation = jnp.sum(jnp.where(first_longest, clip_starts, 0))
    own_place = (own_frame + 2 + rotation) % frames
    seen_place = (seen_frame + 2 + rotation) % frames
    own_clip = jnp.sum((own_place >= clip_ends).astype(jnp.int32))
    seen_clip = jnp.sum((seen_place >= clip_ends).astype(jnp.int32))
    grid_rows = jnp.arange(frames)[:, None]
    grid_cols = jnp.arange(frames)[None, :]
    picked = jnp.sum(jnp.where((grid_rows == own_frame) & (grid_cols == seen_frame), frame_mask, 0))
    kept = (picked == 1) | (distance <= 1)
    return (own_clip == seen_clip) & (seen_place <= own_place) & kept


def fold_rims(extended_grads, band_rows):
    interior = extended_grads[:, 3 : 3 + band_rows]
    rim_rows = jnp.concatenate([extended_grads[:, :3], extended_grads[:, band_rows + 3 :]], 1)
    haloed = padded_2(rim_rows.astype(jnp.bfloat16), (("rows", 1),), 3).astype(rim_rows.dtype)
    interior = interior.at[:, :3].add(haloed[:, :3])
    return interior.at[:, band_rows - 3 :].add(haloed[:, 9:])


def body(queries, keys, values, grad_out, frame_mask, clip_frames, offsets):
    band_rows = queries.shape[1]
    total_width = queries.shape[2]
    ext_rows = band_rows + 6
    group_size = HQ // HK
    scale = HD ** (-0.5)
    lags = min(4, lax.axis_size("tm"))
    query_tiles = to_tiles(queries[0], group_size)
    grad_tiles = to_tiles(grad_out[0], group_size)
    spatial = spatial_live(offsets, band_rows, total_width)[:, None, None]
    allowed = [frame_allowed(frame_mask, clip_frames, distance) for distance in range(lags)]
    stacked = jnp.stack([keys[0], values[0]], 0)
    resident = padded_2(stacked, (("rows", 1),), 3)

    def pair_terms(extended):
        windows = to_windows(extended)
        logits = (
            jnp.einsum(
                "cgaqd,cgkd->cgaqk", query_tiles, windows[0], preferred_element_type=jnp.float32
            )
            * scale
        )
        grad_dot = jnp.einsum(
            "cgaqd,cgkd->cgaqk", grad_tiles, windows[1], preferred_element_type=jnp.float32
        )
        return (windows, logits, grad_dot)

    stat_shape = (total_width // tile_cols, HK, group_size, band_rows * tile_cols)
    running = (
        jnp.full(stat_shape, negative_big, jnp.float32),
        jnp.zeros(stat_shape, jnp.float32),
        jnp.zeros(stat_shape, jnp.float32),
    )
    visiting = resident
    visited = []
    for distance in range(lags):
        visited.append(visiting)
        extended = visiting
        live_mask = spatial & allowed[distance]
        run_max, run_sum, run_dot = running
        stat_windows, stat_logits, stat_grad_dot = pair_terms(extended)
        masked = jnp.where(live_mask, stat_logits, negative_big)
        new_max = jnp.maximum(run_max, jnp.max(masked, axis=-1))
        factor = jnp.exp(run_max - new_max)
        weights = jnp.where(live_mask, jnp.exp(stat_logits - new_max[..., None]), 0.0)
        running = (
            new_max,
            run_sum * factor + jnp.sum(weights, axis=-1),
            run_dot * factor + jnp.sum(weights * stat_grad_dot, axis=-1),
        )
        if distance + 1 < lags:
            visiting = passed_along(visiting, "tm", 1)
    log_total = running[0] + jnp.log(running[1])
    mean_grad = running[2] / running[1]
    query_total = jnp.zeros(stat_shape + (HD,), jnp.float32)
    carried = jnp.zeros(resident.shape, jnp.float32)
    visiting = resident
    for distance in range(lags):
        extended = visiting
        live_mask = spatial & allowed[distance]
        grad_windows, grad_logits, grad_grad_dot = pair_terms(extended)
        probs = jnp.where(live_mask, jnp.exp(grad_logits - log_total[..., None]), 0.0)
        probs_low = probs.astype(jnp.bfloat16)
        dscore = (probs * (grad_grad_dot - mean_grad[..., None])).astype(jnp.bfloat16)
        query_part = jnp.einsum(
            "cgaqk,cgkd->cgaqd", dscore, grad_windows[0], preferred_element_type=jnp.float32
        )
        key_part = (
            jnp.einsum("cgaqk,cgaqd->cgkd", dscore, query_tiles, preferred_element_type=jnp.float32)
            * scale
        )
        value_part = jnp.einsum(
            "cgaqk,cgaqd->cgkd", probs_low, grad_tiles, preferred_element_type=jnp.float32
        )
        query_part, window_grads = (query_part, jnp.stack([key_part, value_part], 0))
        query_total = query_total + query_part
        ext_grads = from_windows(window_grads, ext_rows, total_width)
        carried = carried + ext_grads
        if distance + 1 < lags:
            visiting = passed_along(visiting, "tm", 1)
            carried = passed_along(carried, "tm", 1)
    carried = passed_along(carried, "tm", 1 - lags)
    finished = fold_rims(carried, band_rows)
    grad_queries = from_tiles(query_total * scale, band_rows)
    return (grad_queries, finished[0][None], finished[1][None])


MESH = pl.DeviceIdType.MESH
LOG2E = 1.4426950408889634
SCALE = HD**-0.5
GROUP = HQ // HK


def lag_allowed(mask_ref, clip_ref, own_frame, frames, lag):
    clips = clip_ref.shape[0]
    seen_frame = lax.rem(own_frame - lag + frames, frames)
    total = jnp.int32(0)
    rotation = jnp.int32(0)
    found = jnp.int32(0)
    for clip in range(clips):
        length = clip_ref[clip]
        first = jnp.where(length == 4, 1, 0) * (1 - found)
        rotation = rotation + first * total
        found = found + first
        total = total + length
    own_place = own_frame + 2 + rotation
    own_place = jnp.where(own_place >= frames, own_place - frames, own_place)
    own_place = jnp.where(own_place >= frames, own_place - frames, own_place)
    seen_place = seen_frame + 2 + rotation
    seen_place = jnp.where(seen_place >= frames, seen_place - frames, seen_place)
    seen_place = jnp.where(seen_place >= frames, seen_place - frames, seen_place)
    own_clip = jnp.int32(0)
    seen_clip = jnp.int32(0)
    end = jnp.int32(0)
    for clip in range(clips):
        end = end + clip_ref[clip]
        own_clip = own_clip + jnp.where(own_place >= end, 1, 0)
        seen_clip = seen_clip + jnp.where(seen_place >= end, 1, 0)
    kept = jnp.maximum(jnp.where(mask_ref[own_frame, seen_frame] == 1, 1, 0), jnp.where(lag <= 1, 1, 0))
    same = jnp.where(own_clip == seen_clip, 1, 0)
    causal = jnp.where(seen_place <= own_place, 1, 0)
    return kept * same * causal


TILE = 8
REACH = 4


def fused(
    width, frames,
    mask_hbm, clip_hbm, offset_hbm, query_hbm, key_hbm, value_hbm, cot_hbm,
    dq_out, dkv_out,
    mask_ref, clip_ref, offset_ref, query_ref, cot_ref, raw, keyed, mixed, bias, own_grads, grads, arrived,
    scores_low, dq_acc, final, load_sem, send_sem, recv_sem,
):
    tokens = query_ref.shape[0]
    rows = tokens // width
    tiles = width // TILE
    tile = TILE * rows
    rim = REACH * rows
    span = tile + 2 * rim
    lane_count = GROUP * tile

    def lanes(index):
        return pl.ds(pl.multiple_of(index * HD, HD), HD)

    pairs = [
        (offset_hbm, offset_ref),
        (clip_hbm, clip_ref),
        (mask_hbm, mask_ref),
        (query_hbm, query_ref),
        (cot_hbm, cot_ref),
    ]
    for g in range(HK):
        pairs.append((key_hbm.at[:, lanes(g)], raw.at[0, g, :, pl.ds(0, HD)]))
        pairs.append((value_hbm.at[:, lanes(g)], raw.at[0, g, :, pl.ds(HD, HD)]))
    loads = [pltpu.make_async_copy(pair[0], pair[1], load_sem.at[i]) for i, pair in enumerate(pairs)]
    own = lax.axis_index("tm")
    core = lax.rem(own, 2)

    def device(step):
        return {"tm": lax.rem(own + step + frames, frames)}

    partner = device(1 - 2 * core)
    ahead, behind = device(2), device(frames - 2)
    third = device(jnp.where(core == 0, frames - 3, frames - 1))
    second_to = device(jnp.where(core == 0, 1, 3))
    second_back = device(jnp.where(core == 0, frames - 3, frames - 1))

    barrier = pltpu.get_barrier_semaphore()
    for peer in (behind, third):
        pl.semaphore_signal(barrier, inc=1, device_id=peer, device_id_type=MESH)

    def remote(index, source, target, peer):
        return pltpu.make_async_remote_copy(
            src_ref=source, dst_ref=target, send_sem=send_sem.at[index], recv_sem=recv_sem.at[index],
            device_id=peer, device_id_type=MESH,
        )

    def outward(slot, role, g, peer):
        if g in STAGED:
            return (remote(slot, raw.at[0, g], raw.at[role, g], peer),)
        return (
            remote(slot, key_hbm.at[:, lanes(g)], raw.at[role, g, :, pl.ds(0, HD)], peer),
            remote(slot + 1, value_hbm.at[:, lanes(g)], raw.at[role, g, :, pl.ds(HD, HD)], peer),
        )

    send_two = [outward(2 * g, 2, g, ahead) for g in range(HK)]
    send_one = [outward(4 + 2 * g, 1, g, second_to) for g in range(HK)]
    relay = [remote(8 + g, raw.at[2, g], raw.at[3, g], partner) for g in range(HK)]
    inner = pl.ds(rim, tokens)
    back_relay = [remote(10 + g, grads.at[2, g, inner], arrived.at[2, g], partner) for g in range(HK)]
    back_two = [remote(12 + g, grads.at[1, g, inner], arrived.at[1, g], behind) for g in range(HK)]
    back_one = [remote(14 + g, grads.at[0, g, inner], arrived.at[0, g], second_back) for g in range(HK)]

    pl.semaphore_wait(barrier, 2)
    odd_last = lax.rem(own, 4) == 3
    for copy in send_two[0] + send_one[0]:
        copy.start()
    for load in loads[7:] + loads[:7]:
        load.start()

    for load in loads[7:]:
        load.wait()

    @pl.when(jnp.logical_not(odd_last))
    def _():
        for copy in send_one[1]:
            copy.start()


    new_id = lax.broadcasted_iota(jnp.int32, (tokens, tokens), 0)
    old_id = lax.broadcasted_iota(jnp.int32, (tokens, tokens), 1)
    turn = jnp.where((new_id % rows) * width + new_id // rows == old_id, 1.0, 0.0).astype(jnp.bfloat16)

    def permuted(block):
        return jnp.dot(turn, block, preferred_element_type=jnp.float32).astype(jnp.bfloat16)

    for load in loads[:3]:
        load.wait()
    key_id = lax.broadcasted_iota(jnp.int32, (span, lane_count), 0)
    query_id = lax.broadcasted_iota(jnp.int32, (span, lane_count), 1) % tile
    delta_row = key_id % rows - query_id % rows
    delta_col = key_id // rows - REACH - query_id // rows
    code = jnp.where((delta_col >= -3) & (delta_col <= 3), delta_row * 8 + delta_col, 1000)

    def mark(index, hit):
        wanted = offset_ref[0, index] * 8 + offset_ref[1, index]
        return jnp.where(code == wanted, 0.0, hit)

    spatial = lax.fori_loop(
        0, offset_ref.shape[1], mark, jnp.full((span, lane_count), negative_big, jnp.float32), unroll=True
    )
    lags = (jnp.int32(0), jnp.where(core == 0, 3, 1), jnp.int32(2), jnp.where(core == 0, 1, 3))
    for role in range(4):
        allow = lag_allowed(mask_ref, clip_ref, own, frames, lags[role])
        shut = jnp.where(allow == 1, 0.0, negative_big).astype(jnp.float32)
        bias[1, role] = spatial + shut
        bias[0, role] = jnp.where(key_id < rim, negative_big, spatial) + shut
        bias[2, role] = jnp.where(key_id >= span - rim, negative_big, spatial) + shut

    blank = jnp.zeros((rim, 2 * HD), jnp.bfloat16)
    for role in range(4):
        for g in range(HK):
            keyed[g, role, pl.ds(0, rim)] = blank
            keyed[g, role, pl.ds(rim + tokens, rim)] = blank

    for load in loads[3:5]:
        load.wait()
    hole = jnp.zeros((tiles, lane_count, HD), jnp.bfloat16)
    for g in range(HK):
        mixed[g, :, pl.ds(0, lane_count), pl.ds(HD, HD)] = hole
        mixed[g, :, pl.ds(lane_count, lane_count), pl.ds(0, HD)] = hole
        for a in range(GROUP):
            h = g * GROUP + a
            mixed[g, :, pl.ds(a * tile, tile), pl.ds(0, HD)] = permuted(query_ref[:, lanes(h)]).reshape(
                tiles, tile, HD
            )
            mixed[g, :, pl.ds(lane_count + a * tile, tile), pl.ds(HD, HD)] = permuted(
                cot_ref[:, lanes(h)]
            ).reshape(tiles, tile, HD)

    def follow(first, then):
        for copy in first:
            copy.wait_send()
        for copy in then:
            copy.start()

    def place(role, g):
        keyed[g, role, pl.ds(rim, tokens)] = permuted(raw[role, g])

    for load in loads[5:7]:
        load.wait()
    for g in range(HK):
        place(0, g)

    def unit(g, j, held):
        first = j * tile
        window = keyed[g, :, pl.ds(first, span), :].reshape(4 * span, 2 * HD)
        mix = mixed[g, j]
        both = lax.dot_general(window, mix, (((1,), (1,)), ((), ())), preferred_element_type=jnp.float32)
        variant = 0 if j == 0 else 2 if j == tiles - 1 else 1
        logit = both[:, :lane_count] * (SCALE * LOG2E) + bias[variant].reshape(4 * span, lane_count)
        dot = both[:, lane_count:]
        top = jnp.max(logit, axis=0, keepdims=True)
        weight = jnp.exp2(logit - top)
        total = jnp.sum(weight, axis=0, keepdims=True)
        mean = jnp.sum(weight * dot, axis=0, keepdims=True) / total
        prob = weight * (1.0 / total)
        score = (prob * (dot - mean)).astype(jnp.bfloat16)
        scores_low[g, j] = score
        low = jnp.concatenate([score, prob.astype(jnp.bfloat16)], axis=1)
        part = jnp.dot(low, mix, preferred_element_type=jnp.float32).reshape(4, span, 2 * HD)
        begin = part[:, :tile] if held is None else part[:, :tile] + held
        own_grads[g, pl.ds(first, tile)] = begin[0]
        grads[:, g, pl.ds(first, tile)] = begin[1:].astype(jnp.bfloat16)
        return part[:, tile:]

    def queries_unit(g, j):
        first = pl.multiple_of(j * tile, tile)
        window = keyed[g, :, pl.ds(first, span), pl.ds(0, HD)].reshape(4 * span, HD)
        out = jnp.dot(scores_low[g, j].T, window, preferred_element_type=jnp.float32)
        for a in range(GROUP):
            dq_acc[g * GROUP + a, pl.ds(first, tile)] = out[a * tile : (a + 1) * tile]

    def receive(g):
        @pl.when(core == 1)
        def _():
            for copy in send_one[g]:
                copy.wait_recv()

        for copy in send_two[g]:
            copy.wait_recv()
        relay[g].start()
        place(2, g)

        @pl.when(core == 0)
        def _():
            for copy in send_one[g]:
                copy.wait_recv()

        place(1, g)
        relay[g].wait_recv()
        place(3, g)

    def work(g):
        held = None
        for j in range(tiles):
            held = unit(g, j, held)
        end = pl.ds(tokens, span - tile)
        own_grads[g, end] = held[0]
        grads[:, g, end] = held[1:].astype(jnp.bfloat16)
        back_relay[g].start()
        back_one[g].start()

    def pass_two(g):
        back_relay[g].wait_recv()
        grads[1, g, inner] = (
            grads[1, g, inner].astype(jnp.float32) + arrived[2, g].astype(jnp.float32)
        ).astype(jnp.bfloat16)
        back_two[g].start()

    follow(send_two[0], send_two[1])

    @pl.when(odd_last)
    def _():
        follow((), send_one[1])

    follow(send_one[0], ())

    receive(0)
    work(0)
    pass_two(0)
    receive(1)
    work(1)
    pass_two(1)

    for g in range(HK):

        def turn_step(j, _, g=g):
            queries_unit(g, j)
            return 0

        lax.fori_loop(0, tiles, turn_step, 0, unroll=UNROLL)

    for h in range(HQ):
        for r in range(rows):
            dq_out[pl.ds(r * width, width), lanes(h)] = dq_acc[h, pl.ds(r, width, stride=rows), :] * SCALE

    for g in range(HK):
        back_one[g].wait_recv()
        back_two[g].wait_recv()
        came = arrived[0, g].astype(jnp.float32) + arrived[1, g].astype(jnp.float32) + own_grads[g, inner]
        final[0, g] = came[:, :HD] * SCALE
        final[1, g] = came[:, HD:]
        for r in range(rows):
            dkv_out[0, pl.ds(r * width, width), lanes(g)] = final[0, g, pl.ds(r, width, stride=rows), :]
            dkv_out[1, pl.ds(r * width, width), lanes(g)] = final[1, g, pl.ds(r, width, stride=rows), :]
    for copy in send_two[1] + send_one[1]:
        copy.wait_send()
    for g in range(HK):
        for copy in (relay[g], back_relay[g], back_two[g], back_one[g]):
            copy.wait_send()


UNROLL = 8
STAGED = (1,)
VL = 40 * 1024 * 1024


def fused_body(queries, keys, values, grad_out, frame_mask, clip_frames, offsets):
    _, rows, width, wide = queries.shape
    tokens = rows * width
    narrow = keys.shape[3]
    frames = lax.axis_size("tm")
    tiles = width // TILE
    tile = TILE * rows
    padded = tokens + 2 * REACH * rows
    span = tile + 2 * REACH * rows

    def flat(array):
        return array.reshape(tokens, array.shape[3])

    hbm = pl.BlockSpec(memory_space=pltpu.HBM)
    vmem = pl.BlockSpec(memory_space=pltpu.VMEM)

    def kernel(*refs):
        fused(width, frames, *refs)

    dq, dkv = pl.pallas_call(
        kernel,
        out_shape=(
            pltpu.VMEM((tokens, wide), jnp.float32),
            pltpu.VMEM((2, tokens, narrow), jnp.float32),
        ),
        in_specs=[hbm] * 7,
        out_specs=(vmem, vmem),
        scratch_shapes=[
            pltpu.SMEM(frame_mask.shape, jnp.int32),
            pltpu.SMEM(clip_frames.shape, jnp.int32),
            pltpu.SMEM(offsets.shape[::-1], jnp.int32),
            pltpu.VMEM((tokens, wide), jnp.bfloat16),
            pltpu.VMEM((tokens, wide), jnp.bfloat16),
            pltpu.VMEM((4, HK, tokens, 2 * HD), jnp.bfloat16),
            pltpu.VMEM((HK, 4, padded, 2 * HD), jnp.bfloat16),
            pltpu.VMEM((HK, tiles, 2 * GROUP * tile, 2 * HD), jnp.bfloat16),
            pltpu.VMEM((3, 4, span, GROUP * tile), jnp.float32),
            pltpu.VMEM((HK, padded, 2 * HD), jnp.float32),
            pltpu.VMEM((3, HK, padded, 2 * HD), jnp.bfloat16),
            pltpu.VMEM((3, HK, tokens, 2 * HD), jnp.bfloat16),
            pltpu.VMEM((HK, tiles, 4 * span, GROUP * tile), jnp.bfloat16),
            pltpu.VMEM((HQ, tokens, HD), jnp.float32),
            pltpu.VMEM((2, HK, tokens, HD), jnp.float32),
            pltpu.SemaphoreType.DMA((9,)),
            pltpu.SemaphoreType.DMA((16,)),
            pltpu.SemaphoreType.DMA((16,)),
        ],
        compiler_params=pltpu.CompilerParams(
            collective_id=0, has_side_effects=True, vmem_limit_bytes=VL
        ),
    )(*[
        pltpu.with_memory_space_constraint(operand, pltpu.HBM)
        for operand in (
            frame_mask, clip_frames, offsets.T, flat(queries), flat(keys), flat(values), flat(grad_out)
        )
    ])
    def ship(dq_ref, dkv_ref, dq_out, dk_out, dv_out, sem):
        pairs = ((dq_ref, dq_out), (dkv_ref.at[0], dk_out), (dkv_ref.at[1], dv_out))
        copies = [pltpu.make_async_copy(pair[0], pair[1], sem.at[i]) for i, pair in enumerate(pairs)]
        for copy in copies:
            copy.start()
        for copy in copies:
            copy.wait()

    dq, dk, dv = pl.pallas_call(
        ship,
        out_shape=(
            jax.ShapeDtypeStruct((tokens, wide), jnp.float32),
            jax.ShapeDtypeStruct((tokens, narrow), jnp.float32),
            jax.ShapeDtypeStruct((tokens, narrow), jnp.float32),
        ),
        in_specs=[vmem] * 2,
        out_specs=[hbm] * 3,
        scratch_shapes=[pltpu.SemaphoreType.DMA((3,))],
        compiler_params=pltpu.CompilerParams(vmem_limit_bytes=4 * 1024 * 1024),
        name="ship",
    )(*[pltpu.with_memory_space_constraint(part, pltpu.VMEM) for part in (dq, dkv)])
    shape = (1, rows, width)
    return dq.reshape(shape + (wide,)), dk.reshape(shape + (narrow,)), dv.reshape(shape + (narrow,))


def solution(mesh):
    whole_rows = mesh.shape["rows"] == 1 and mesh.shape["tm"] % 2 == 0 and mesh.shape["tm"] > 6
    return jax.shard_map(
        fused_body if whole_rows else body,
        mesh=mesh,
        in_specs=(
            P(("groups", "tm"), "rows", None, None),
            P(("groups", "tm"), "rows", None, None),
            P(("groups", "tm"), "rows", None, None),
            P(("groups", "tm"), "rows", None, None),
            P("groups", None),
            P("groups"),
            P(),
        ),
        out_specs=(
            P(("groups", "tm"), "rows", None, None),
            P(("groups", "tm"), "rows", None, None),
            P(("groups", "tm"), "rows", None, None),
        ),
        check_vma=False,
    )
```
